32 devices in a mesh: dp: 4 (over z), expert: 2 (over x), tensor: 4 (over y, core).
Axes of the slice: x: 2, y: 2, z: 4, core: 2. Of those that a mesh axis runs over, the one named last changes fastest.
Arguments:
- skip_stream_entry: bfloat16 [512, 4096], P(('dp', 'expert', 'tensor')), may hold values from -6 to 6
- question_vectors: bfloat16 [512, 2048], P(('dp', 'expert'), 'tensor'), may hold values from -5 to 5
- fresh_lookup_vectors: bfloat16 [512, 512], P(('dp', 'expert'), 'tensor'), may hold values from -5 to 5
- fresh_content_vectors: bfloat16 [512, 512], P(('dp', 'expert'), 'tensor'), may hold values from -10 to 10
- stored_lookup_sheets: bfloat16 [320, 4, 128, 128], P(('dp', 'expert'), 'tensor'), may hold values from -5 to 5
- stored_content_sheets: bfloat16 [320, 4, 128, 128], P(('dp', 'expert'), 'tensor'), may hold values from -10 to 10
- sequence_sheet_map: int32 [136, 8], P(('dp', 'expert')), may hold values from 0 to 39
- stored_position_counts: int32 [136], P(('dp', 'expert')), may hold values from 2 to 1024
- attention_merge_matrix: bfloat16 [2048, 4096], P('tensor'), may hold values from -0.59765625 to 0.59765625
- premix_scale_factor: bfloat16 [4096], replicated, may hold values from 0.5 to 1.5
- chosen_specialists: int32 [512, 2], P(('dp', 'expert', 'tensor')), may hold values from 0 to 7, all different within a row; in each aligned block of 16 rows (0 to 15, 16 to 31, ...) at most 6 rows name the same one
- selection_shares: float32 [512, 2], P(('dp', 'expert', 'tensor')), may hold values from 0.2 to 1
- allowed_placements: int32 [8], replicated, may hold values from 2 to 3
- favored_specialist: int32 [1], replicated, may hold values from 0 to 7
- gating_matrices: bfloat16 [8, 7168, 4096], P('expert', ('dp', 'tensor')), may hold values from -0.09375 to 0.09375
- expand_matrices: bfloat16 [8, 7168, 4096], P('expert', ('dp', 'tensor')), may hold values from -0.09375 to 0.09375
- contract_matrices: bfloat16 [8, 7168, 4096], P('expert', ('dp', 'tensor')), may hold values from -0.0625 to 0.0625
Outputs:
- layer_out: bfloat16 [512, 4096], P(('dp', 'expert', 'tensor'))
The draws below stay inside these ranges and needn't reach their ends.
Inputs may be any that keep to these rules, and one draw needn't show every extreme that they name: `chosen_specialists`: in the 16 rows of one device no expert is named by more than 6 rows; a token names two different experts.
All inputs are finite; a program needn't handle non-finite values.
Results may differ from the reference program's by a relative error of at most 0.018.
Values may be sent and summed in bfloat16 or wider, within the bound.
No kernel may reach another device: no remote copies, remote signals or barrier semaphores. Data moves between devices by JAX's collectives and lax.ppermute only.
A program may use at most 128 MiB of HBM per device.

```python
import math
from functools import reduce
import jax
import jax.numpy as jnp
import numpy as np
from jax import lax

D = 4096
HD = 128
SPECIALIST_COUNT = 8
FF = 7168
QH = 16
KVH = 4
PAGE = 128
MAXP = 8
POOL = 40
TOK_DEV = 16
GROUPS = 8
ROWS_GROUP = 64
REQ = 17
TOKENS = 512
PLACEMENT_MOST = 6
CAP_MOST = 3
SHARDS = 16
FF_SHARD = 448


def draw_question_vectors(key, part):
    array_shape = (TOKENS, QH, HD)
    base = jnp.clip(jax.random.normal(jax.random.fold_in(key, 1), array_shape, jnp.float32), -5.0, 5.0)
    return base.reshape(TOKENS, QH * HD).astype(jnp.bfloat16)


def draw_stored_lookup_sheets(key, part):
    array_shape = (GROUPS * POOL, KVH, PAGE, HD)
    base = jnp.clip(jax.random.normal(jax.random.fold_in(key, 4), array_shape, jnp.float32), -5.0, 5.0)
    return base.astype(jnp.bfloat16)


def draw_stored_position_counts(key, part):
    longest = MAXP * PAGE
    drawn = jax.random.randint(jax.random.fold_in(key, 11), (GROUPS * REQ,), 2, longest + 1)
    target = jax.random.randint(jax.random.fold_in(key, 12), (), 0, GROUPS * REQ)
    return jnp.where(jnp.arange(GROUPS * REQ) == target, longest, drawn).astype(jnp.int32)


def draw_allowed_placements(key, part):
    drawn = jax.random.randint(jax.random.fold_in(key, 21), (SPECIALIST_COUNT,), 2, CAP_MOST + 1)
    target = jax.random.randint(jax.random.fold_in(key, 22), (), 0, SPECIALIST_COUNT)
    return jnp.where(jnp.arange(SPECIALIST_COUNT) == target, CAP_MOST, drawn).astype(jnp.int32)


def with_ends(result, stream_key, low, top_value):
    shape = result.shape
    spot = [jax.random.randint(jax.random.fold_in(stream_key, axis), (), 0, shape[axis]) for axis in range(len(shape))]
    result = result.at[tuple(spot)].set(low)
    longest = shape.index(max(shape))
    spot[longest] = (spot[longest] + 1) % shape[longest]
    return result.at[tuple(spot)].set(top_value)


def block_levels(own_key, extent, pieces, smallest, largest):
    factor_of = 1.0
    for axis_at, blocks in pieces:
        steps = jax.random.uniform(jax.random.fold_in(jax.random.fold_in(own_key, 6), axis_at), (blocks,), jnp.float32, smallest / len(pieces), largest / len(pieces))
        factor_of = factor_of * jnp.repeat(jnp.exp(steps), extent[axis_at] // blocks).reshape((-1,) + (1,) * (len(extent) - 1 - axis_at))
    return factor_of


def assign_block(own_key, own, number, rows, amount, top, bound, lean):
    order = jax.random.permutation(own_key, amount)
    crowded, ordinary = shares(amount, rows * top, bound, lean, True), shares(amount, rows * top, bound, lean, False)
    places = jnp.arange(amount)

    def named(tallies, offset_by):
        used = int((tallies > 0).sum())
        fixed = max(1, used // 4)
        passed = fixed + (places - fixed + offset_by * (used - fixed)) % max(1, amount - fixed)
        return jnp.zeros((amount,), jnp.int32).at[order[jnp.where(places < fixed, places, passed)]].set(jnp.asarray(tallies, jnp.int32))

    tallies = jnp.where(number % 4 == 0, named(crowded, number // 4), named(ordinary, number - number // 4 - 1))
    mixed = jax.random.permutation(jax.random.fold_in(own, 3), amount)
    giver, sink = mixed[0:amount // 2 * 2:2], mixed[1:amount // 2 * 2:2]
    slack = jnp.minimum(tallies[giver] - 1, bound - tallies[sink]) // 2
    slack = jnp.where((giver == order[0]) | (sink == order[0]) | (tallies[sink] == 0), 0, jnp.maximum(slack, 0))
    passed = jax.random.randint(jax.random.fold_in(own, 4), (amount // 2,), 0, 1 << 20) % (slack + 1)
    tallies = tallies.at[giver].add(-passed).at[sink].add(passed)
    labels = jnp.searchsorted(jnp.cumsum(tallies), jnp.arange(rows * top), side="right").astype(jnp.int32)
    grid = labels.reshape(top, rows).T
    grid = grid[jax.random.permutation(jax.random.fold_in(own, 1), rows)]
    offset_by = jax.random.randint(jax.random.fold_in(own, 2), (rows, 1), 0, top)
    return jnp.take_along_axis(grid, (jnp.arange(top)[None, :] + offset_by) % top, axis=1)


def shares(amount, total, reach, slope, full):
    weights = [(1 << 20) // math.isqrt(standing ** slope) + 1 for standing in range(1, amount + 1)]
    largest = reach if full else min(reach, max(-(-total // amount), total * weights[0] // sum(weights)))
    least = 1 if total - largest >= amount - 1 else 0
    counts, spare = [largest] + [least] * (amount - 1), total - largest - least * (amount - 1)
    while spare > 0:
        candidates = [i for i in range(1, amount) if counts[i] < largest] or [i for i in range(1, amount) if counts[i] < reach]
        pool, remaining = sum([weights[i] for i in candidates]), spare
        for i in candidates:
            extra = min(reach - counts[i], max(1, remaining * weights[i] // pool), spare)
            counts[i] = counts[i] + extra
            spare = spare - extra
    return np.array(counts)


def bell_draw(key, dims, spread, most, split=(), kind=jnp.bfloat16):
    entries = spread * jax.random.normal(key, dims, jnp.float32)
    if split:
        entries = entries * block_levels(key, dims, split, -0.22, 0.18)
    return jnp.clip(entries, -most, most).astype(kind)


def setup_inputs(seed: int = 0) -> dict:
    keys = jax.random.split(jax.random.key(seed), 18)
    skip_stream_entry = bell_draw(keys[0], (TOKENS, D), 1.0, 6.0, ((0, 32),))
    question_vectors = draw_question_vectors(jax.random.fold_in(keys[17], 71), 0)
    fresh_lookup_vectors = bell_draw(keys[2], (TOKENS, KVH * HD), 1.0, 5.0, ((0, 8), (1, 4)))
    fresh_content_vectors = bell_draw(keys[3], (TOKENS, KVH * HD), 2.0, 10.0, ((0, 8), (1, 4)))
    stored_lookup_sheets = draw_stored_lookup_sheets(jax.random.fold_in(keys[17], 71), 0)
    stored_content_sheets = bell_draw(keys[5], (GROUPS * POOL, KVH, PAGE, HD), 2.0, 10.0, ((0, 8), (1, 4)))
    sequence_sheet_map = with_ends(jax.random.randint(keys[6], (GROUPS * REQ, MAXP), 0, POOL), jax.random.fold_in(keys[6], 1), 0, POOL - 1).astype(jnp.int32)
    stored_position_counts = draw_stored_position_counts(jax.random.fold_in(keys[17], 71), 0)
    attention_merge_matrix = bell_draw(keys[8], (QH * HD, D), 0.1, 0.59765625, ((0, 4),))
    premix_scale_factor = jnp.clip(1.0 + 0.1 * jax.random.normal(keys[9], (D,), jnp.float32), 0.5, 1.5).astype(jnp.bfloat16)
    chosen_specialists_keys = jax.random.split(jax.random.fold_in(keys[10], 1), TOKENS // TOK_DEV)
    chosen_specialists_turns = jax.random.permutation(jax.random.fold_in(keys[10], 3), TOKENS // TOK_DEV)
    chosen_specialists = jax.vmap(lambda own, number: assign_block(jax.random.fold_in(keys[10], 2), own, number, TOK_DEV, SPECIALIST_COUNT, 2, PLACEMENT_MOST, 2))(chosen_specialists_keys, chosen_specialists_turns).reshape((TOKENS, 2))
    selection_shares = jnp.clip(0.2 + 0.8 * jax.random.uniform(keys[11], (TOKENS, 2), jnp.float32) ** block_levels(keys[11], (TOKENS, 2), ((0, 32),), -0.2, 0.2), 0.2, 1.0)
    allowed_placements = draw_allowed_placements(jax.random.fold_in(keys[17], 71), 0)
    favored_specialist = jax.random.randint(keys[13], (1,), 0, SPECIALIST_COUNT).astype(jnp.int32)
    gating_matrices = bell_draw(keys[14], (SPECIALIST_COUNT, FF, D), D ** -0.5, 0.09375, ((0, 2), (1, 16)))
    expand_matrices = bell_draw(keys[15], (SPECIALIST_COUNT, FF, D), D ** -0.5, 0.09375, ((0, 2), (1, 16)))
    contract_matrices = bell_draw(keys[16], (SPECIALIST_COUNT, FF, D), FF ** -0.5, 0.0625, ((0, 2), (1, 16)))
    return dict(skip_stream_entry=skip_stream_entry, question_vectors=question_vectors, fresh_lookup_vectors=fresh_lookup_vectors, fresh_content_vectors=fresh_content_vectors, stored_lookup_sheets=stored_lookup_sheets, stored_content_sheets=stored_content_sheets, sequence_sheet_map=sequence_sheet_map, stored_position_counts=stored_position_counts, attention_merge_matrix=attention_merge_matrix, premix_scale_factor=premix_scale_factor, chosen_specialists=chosen_specialists, selection_shares=selection_shares, allowed_placements=allowed_placements, favored_specialist=favored_specialist, gating_matrices=gating_matrices, expand_matrices=expand_matrices, contract_matrices=contract_matrices)


def normalize(parts):
    highest = reduce(jnp.maximum, [lax.optimization_barrier(jnp.max(jnp.where(visible, scores, -jnp.inf), axis=-1, keepdims=True)) for scores, visible in parts])
    portions = [jnp.where(visible, jnp.exp(scores - highest), 0.0) for scores, visible in parts]
    denominator = reduce(jnp.add, [lax.optimization_barrier(jnp.sum(portion, axis=-1, keepdims=True)) for portion in portions])
    return [(portion / denominator).astype(jnp.bfloat16) for portion in portions]

def attend(question_vectors, new_keys, new_values, key_pages, value_pages, table, spans):
    rows_all, head_count, head_width = question_vectors.shape
    kv_heads = new_keys.shape[1]
    group_size = head_count // kv_heads
    single_count = spans.shape[0] - 1
    page_count = table.shape[1]
    page_width = key_pages.shape[2]
    context = page_count * page_width
    inverse_root = 1.0 / math.sqrt(head_width)
    page_keys = key_pages[table].astype(jnp.float32)
    page_values = value_pages[table].astype(jnp.float32)
    grouped = question_vectors.astype(jnp.float32).reshape(rows_all, kv_heads, group_size, head_width)
    fresh_keys = new_keys.astype(jnp.float32)
    fresh_values = new_values.astype(jnp.float32)
    positions = jnp.arange(context, dtype=jnp.int32)
    single_q = grouped[:single_count]
    cache_dec = jnp.einsum('rkgh,rmkph->rkgmp', single_q, page_keys[:single_count]).reshape(single_count, kv_heads, group_size, context) * inverse_root
    seen_dec = (positions[None, :] < spans[:single_count, None])[:, None, None, :]
    own_dec = jnp.einsum('rkgh,rkh->rkg', single_q, fresh_keys[:single_count])[..., None] * inverse_root
    weight_cache, weight_own = normalize([(cache_dec, seen_dec), (own_dec, jnp.full(own_dec.shape, True))])
    out_dec = jnp.einsum('rkgmp,rmkph->rkgh', weight_cache.astype(jnp.float32).reshape(single_count, kv_heads, group_size, page_count, page_width), page_values[:single_count])
    out_dec = out_dec + weight_own.astype(jnp.float32) * fresh_values[:single_count][:, :, None, :]
    prompt_q = grouped[single_count:]
    prompt_rows = rows_all - single_count
    cache_pro = jnp.einsum('rkgh,mkph->rkgmp', prompt_q, page_keys[single_count]).reshape(prompt_rows, kv_heads, group_size, context) * inverse_root
    seen_pro = (positions < spans[single_count])[None, None, None, :]
    new_pro = jnp.einsum('rkgh,mkh->rkgm', prompt_q, fresh_keys[single_count:]) * inverse_root
    prompt_index = jnp.arange(prompt_rows, dtype=jnp.int32)
    causal = (prompt_index[:, None] >= prompt_index[None, :])[:, None, None, :]
    weight_cpro, weight_npro = normalize([(cache_pro, seen_pro), (new_pro, causal)])
    out_pro = jnp.einsum('rkgmp,mkph->rkgh', weight_cpro.astype(jnp.float32).reshape(prompt_rows, kv_heads, group_size, page_count, page_width), page_values[single_count])
    out_pro = out_pro + jnp.einsum('rkgm,mkh->rkgh', weight_npro.astype(jnp.float32), fresh_values[single_count:])
    joined = jnp.concatenate([out_dec, out_pro], axis=0).astype(jnp.bfloat16)
    return joined.reshape(rows_all, head_count * head_width)

def expert_rows(buffer, gate_w, up_w, down_w):
    gate_part = jnp.dot(buffer, gate_w.T, preferred_element_type=jnp.float32)
    up_part = jnp.dot(buffer, up_w.T, preferred_element_type=jnp.float32)
    hidden = (jax.nn.silu(gate_part) * up_part).astype(jnp.bfloat16)
    blocks = hidden.reshape(hidden.shape[0], SHARDS, FF_SHARD).transpose(1, 0, 2)
    downs = down_w.reshape(SHARDS, FF_SHARD, D)

    def add_block(running, pair):
        partial_out = jnp.dot(pair[0], pair[1], preferred_element_type=jnp.float32).astype(jnp.bfloat16)
        partial_out = lax.optimization_barrier(partial_out)
        return (running + partial_out.astype(jnp.float32), None)
    summed, unused = lax.scan(add_block, jnp.zeros((hidden.shape[0], D), jnp.float32), (blocks, downs))
    return summed.astype(jnp.bfloat16)

def reference(skip_stream_entry, question_vectors, fresh_lookup_vectors, fresh_content_vectors, stored_lookup_sheets, stored_content_sheets, sequence_sheet_map, stored_position_counts, attention_merge_matrix, premix_scale_factor, chosen_specialists, selection_shares, allowed_placements, favored_specialist, gating_matrices, expand_matrices, contract_matrices):
    group_q = question_vectors.reshape(GROUPS, ROWS_GROUP, QH, HD)
    group_k = fresh_lookup_vectors.reshape(GROUPS, ROWS_GROUP, KVH, HD)
    group_v = fresh_content_vectors.reshape(GROUPS, ROWS_GROUP, KVH, HD)
    cache_k = stored_lookup_sheets.reshape(GROUPS, POOL, KVH, PAGE, HD)
    cache_v = stored_content_sheets.reshape(GROUPS, POOL, KVH, PAGE, HD)
    tables = sequence_sheet_map.reshape(GROUPS, REQ, MAXP)
    spans = stored_position_counts.reshape(GROUPS, REQ)
    heads_out = lax.map(lambda items: attend(*items), (group_q, group_k, group_v, cache_k, cache_v, tables, spans))
    heads_out = heads_out.reshape(TOKENS, QH * HD)
    attn_sum = jnp.dot(heads_out, attention_merge_matrix, preferred_element_type=jnp.float32)
    stream = (skip_stream_entry.astype(jnp.float32) + attn_sum).astype(jnp.bfloat16)
    wide = stream.astype(jnp.float32)
    squares = lax.optimization_barrier(jnp.mean(wide * wide, axis=1, keepdims=True))
    normed = (wide * lax.rsqrt(squares + 1e-05) * premix_scale_factor.astype(jnp.float32)).astype(jnp.bfloat16)
    picked = (chosen_specialists[:, :, None] == jnp.arange(SPECIALIST_COUNT, dtype=jnp.int32)[None, None, :]).astype(jnp.int32)
    busiest_specialist = favored_specialist[0]
    nblock = TOKENS // TOK_DEV
    flat_blocks = picked.reshape(nblock, TOK_DEV * 2, SPECIALIST_COUNT)
    before = (jnp.cumsum(flat_blocks, axis=1) - flat_blocks).reshape(TOKENS, 2, SPECIALIST_COUNT)
    ranking = lax.optimization_barrier(jnp.sum(before * picked, axis=2))
    placement_ceiling = jnp.where(jnp.arange(SPECIALIST_COUNT, dtype=jnp.int32) == busiest_specialist, PLACEMENT_MOST, allowed_placements)
    keeping = ranking < lax.optimization_barrier(jnp.sum(picked * placement_ceiling[None, None, :], axis=2))
    slot_hit = ranking[:, :, None] == jnp.arange(PLACEMENT_MOST, dtype=jnp.int32)[None, None, :]
    table_all = (picked[..., None] > 0) & keeping[:, :, None, None] & slot_hit[:, :, None, :]
    table_f = table_all.reshape(nblock, TOK_DEV, 2, SPECIALIST_COUNT, PLACEMENT_MOST).astype(jnp.float32)
    send = jnp.einsum('bnkes,bnd->ebsd', table_f, normed.reshape(nblock, TOK_DEV, D).astype(jnp.float32)).astype(jnp.bfloat16)
    outputs = lax.map(lambda items: expert_rows(items[0].reshape(nblock * PLACEMENT_MOST, D), items[1], items[2], items[3]), (send, gating_matrices, expand_matrices, contract_matrices))
    outputs = outputs.reshape(SPECIALIST_COUNT, nblock, PLACEMENT_MOST, D).astype(jnp.float32)
    chosen = jnp.einsum('bnkes,ebsd->bnkd', table_f, outputs).reshape(TOKENS, 2, D)
    mixed = lax.optimization_barrier(jnp.sum(selection_shares[:, :, None] * chosen, axis=1))
    return (wide + mixed).astype(jnp.bfloat16)
```

```python
from functools import reduce
import math

import jax
import jax.numpy as jnp
from jax import lax
from jax.experimental import pallas as pl
from jax.experimental.pallas import tpu as pltpu
from jax.sharding import PartitionSpec as P

HD = 128
PLACEMENT_MOST = 6


def normalize(parts):
    highest = reduce(
        jnp.maximum,
        [
            jnp.max(jnp.where(visible, scores, -jnp.inf), axis=-1, keepdims=True)
            for scores, visible in parts
        ],
    )
    portions = [jnp.where(visible, jnp.exp(scores - highest), 0.0) for scores, visible in parts]
    denominator = reduce(
        jnp.add, [jnp.sum(portion, axis=-1, keepdims=True) for portion in portions]
    )
    return [(portion / denominator).astype(jnp.bfloat16) for portion in portions]


def attend(question_vectors, new_keys, new_values, key_pages, value_pages, table, spans):
    rows_all, head_count, head_width = question_vectors.shape
    kv_heads = new_keys.shape[1]
    group_size = head_count // kv_heads
    single_count = spans.shape[0] - 1
    page_count = table.shape[1]
    page_width = key_pages.shape[2]
    context = page_count * page_width
    inverse_root = 1.0 / math.sqrt(head_width)
    page_keys = key_pages[table]
    page_values = value_pages[table]
    grouped = question_vectors.reshape(rows_all, kv_heads, group_size, head_width)
    positions = jnp.arange(context, dtype=jnp.int32)
    single_q = grouped[:single_count]
    cache_dec = (
        jnp.einsum(
            "rkgh,rmkph->rkgmp",
            single_q,
            page_keys[:single_count],
            preferred_element_type=jnp.float32,
        ).reshape(single_count, kv_heads, group_size, context)
        * inverse_root
    )
    seen_dec = (positions[None, :] < spans[:single_count, None])[:, None, None, :]
    own_dec = (
        jnp.einsum(
            "rkgh,rkh->rkg", single_q, new_keys[:single_count], preferred_element_type=jnp.float32
        )[..., None]
        * inverse_root
    )
    weight_cache, weight_own = normalize(
        [(cache_dec, seen_dec), (own_dec, jnp.full(own_dec.shape, True))]
    )
    out_dec = jnp.einsum(
        "rkgmp,rmkph->rkgh",
        weight_cache.reshape(single_count, kv_heads, group_size, page_count, page_width),
        page_values[:single_count],
        preferred_element_type=jnp.float32,
    )
    out_dec = (
        out_dec
        + weight_own.astype(jnp.float32)
        * new_values[:single_count].astype(jnp.float32)[:, :, None, :]
    )
    prompt_q = grouped[single_count:]
    prompt_rows = rows_all - single_count
    cache_pro = (
        jnp.einsum(
            "rkgh,mkph->rkgmp",
            prompt_q,
            page_keys[single_count],
            preferred_element_type=jnp.float32,
        ).reshape(prompt_rows, kv_heads, group_size, context)
        * inverse_root
    )
    seen_pro = (positions < spans[single_count])[None, None, None, :]
    new_pro = (
        jnp.einsum(
            "rkgh,mkh->rkgm", prompt_q, new_keys[single_count:], preferred_element_type=jnp.float32
        )
        * inverse_root
    )
    prompt_index = jnp.arange(prompt_rows, dtype=jnp.int32)
    causal = (prompt_index[:, None] >= prompt_index[None, :])[:, None, None, :]
    weight_cpro, weight_npro = normalize([(cache_pro, seen_pro), (new_pro, causal)])
    out_pro = jnp.einsum(
        "rkgmp,mkph->rkgh",
        weight_cpro.reshape(prompt_rows, kv_heads, group_size, page_count, page_width),
        page_values[single_count],
        preferred_element_type=jnp.float32,
    )
    out_pro = out_pro + jnp.einsum(
        "rkgm,mkh->rkgh", weight_npro, new_values[single_count:], preferred_element_type=jnp.float32
    )
    joined = jnp.concatenate([out_dec, out_pro], axis=0).astype(jnp.bfloat16)
    return joined.reshape(rows_all, head_count * head_width)


def slot_table(member, ranking, keeping, slot_count):
    slot_hit = (
        ranking[:, :, None, None] == jnp.arange(slot_count, dtype=jnp.int32)[None, None, None, :]
    )
    return ((member[..., None] > 0) & keeping[:, :, None, None] & slot_hit).astype(jnp.bfloat16)


def expert_pass(send, gating_matrices, expand_matrices, contract_matrices):
    specialist_index, slot_count, model_width = send.shape
    holders = lax.axis_size("expert")
    local_count = gating_matrices.shape[0]
    arrived = lax.all_to_all(
        send.reshape(holders, local_count, slot_count, model_width),
        "expert",
        split_axis=0,
        concat_axis=0,
        tiled=True,
    )
    row_piece = lax.all_gather(arrived, ("dp", "tensor"), axis=0, tiled=True)
    gate_part = jnp.einsum(
        "qesd,efd->qesf", row_piece, gating_matrices, preferred_element_type=jnp.float32
    )
    up_part = jnp.einsum(
        "qesd,efd->qesf", row_piece, expand_matrices, preferred_element_type=jnp.float32
    )
    hidden = (jax.nn.silu(gate_part) * up_part).astype(jnp.bfloat16)
    summed = lax.psum_scatter(
        jnp.einsum(
            "qesf,efd->qesd", hidden, contract_matrices, preferred_element_type=jnp.float32
        ).astype(jnp.bfloat16),
        ("dp", "tensor"),
        scatter_dimension=0,
        tiled=True,
    )
    arrived_back = lax.all_to_all(summed, "expert", split_axis=0, concat_axis=0, tiled=True)
    return arrived_back.reshape(specialist_index, slot_count, model_width)


def local(
    skip_stream_entry,
    question_vectors,
    fresh_lookup_vectors,
    fresh_content_vectors,
    stored_lookup_sheets,
    stored_content_sheets,
    sequence_sheet_map,
    stored_position_counts,
    attention_merge_matrix,
    premix_scale_factor,
    chosen_specialists,
    selection_shares,
    allowed_placements,
    favored_specialist,
    gating_matrices,
    expand_matrices,
    contract_matrices,
):
    token_count = chosen_specialists.shape[0]
    specialist_index = allowed_placements.shape[0]
    picked = (
        chosen_specialists[:, :, None]
        == jnp.arange(specialist_index, dtype=jnp.int32)[None, None, :]
    ).astype(jnp.int32)
    flat_routes = picked.reshape(token_count * 2, specialist_index)
    busiest_specialist = favored_specialist[0]
    before = (jnp.cumsum(flat_routes, axis=0) - flat_routes).reshape(
        token_count, 2, specialist_index
    )
    ranking = jnp.sum(before * picked, axis=2)
    placement_ceiling = jnp.where(
        jnp.arange(specialist_index, dtype=jnp.int32) == busiest_specialist,
        PLACEMENT_MOST,
        allowed_placements,
    )
    keeping = ranking < jnp.sum(picked * placement_ceiling[None, None, :], axis=2)
    row_total = question_vectors.shape[0]
    heads_out = attend(
        question_vectors.reshape(row_total, -1, HD),
        fresh_lookup_vectors.reshape(row_total, -1, HD),
        fresh_content_vectors.reshape(row_total, -1, HD),
        stored_lookup_sheets,
        stored_content_sheets,
        sequence_sheet_map,
        stored_position_counts,
    )
    total_attn = lax.psum(
        jnp.dot(heads_out, attention_merge_matrix, preferred_element_type=jnp.float32).astype(
            jnp.bfloat16
        ),
        "tensor",
    ).astype(jnp.float32)
    own_attn = lax.dynamic_slice_in_dim(
        total_attn, lax.axis_index("tensor") * token_count, token_count, 0
    )
    stream = (skip_stream_entry.astype(jnp.float32) + own_attn).astype(jnp.bfloat16)
    wide = stream.astype(jnp.float32)
    squares = jnp.mean(wide * wide, axis=1, keepdims=True)
    normed = (wide * lax.rsqrt(squares + 1e-05) * premix_scale_factor.astype(jnp.float32)).astype(
        jnp.bfloat16
    )
    main_slots = PLACEMENT_MOST
    table_main = slot_table(picked, ranking, keeping, main_slots)
    send = jnp.einsum(
        "nkes,nd->esd", table_main, normed, preferred_element_type=jnp.float32
    ).astype(jnp.bfloat16)
    expert_out = expert_pass(send, gating_matrices, expand_matrices, contract_matrices)
    chosen = jnp.einsum("nkes,esd->nkd", table_main, expert_out, preferred_element_type=jnp.float32)
    mixed = jnp.sum(selection_shares[:, :, None] * chosen, axis=1)
    return (wide + mixed).astype(jnp.bfloat16)


PAIRS_CORE = [(0, 1), (1, 0), (2, 3), (3, 2)]
PAIRS_Y = [(0, 2), (2, 0), (1, 3), (3, 1)]
PAIRS_X = [(0, 1), (1, 0)]
SINGLES = 16
PROMPT = 48
CAP_MOST = 3
NEG = -1e30
MIB = 1 << 20


def over_core(a):
    return lax.ppermute(a, "tensor", PAIRS_CORE)


def over_y(a):
    return lax.ppermute(a, "tensor", PAIRS_Y)


def over_x(a):
    return lax.ppermute(a, "expert", PAIRS_X)


def over_z(a, k):
    return lax.ppermute(a, "dp", [(i, i ^ k) for i in range(4)])


def dot_nt(a, b):
    return lax.dot_general(a, b, (((1,), (1,)), ((), ())), preferred_element_type=jnp.float32)


def dot_nn(a, b):
    return lax.dot_general(a, b, (((1,), (0,)), ((), ())), preferred_element_type=jnp.float32)


def attend_kernel(
    place, table_s, table_v, counts_v, counts_s, q, k_new, v_new, k_hbm, v_hbm, w_hbm,
    send, keep,
    k_pool, v_pool, w_out, scores, times, weights, k_prompt, v_prompt, heads, ordered, sems,
):
    pool_rows = k_pool.shape[0]
    pages = pool_rows // 128
    slots = table_v.shape[1]
    group = q.shape[1] // HD
    copies = [
        pltpu.make_async_copy(src, dst, sems.at[i])
        for i, (src, dst) in enumerate(((k_hbm, k_pool), (v_hbm, v_pool), (w_hbm, w_out)))
    ]
    for copy in copies:
        copy.start()
    root = 1.0 / math.sqrt(HD)

    lane = lax.broadcasted_iota(jnp.int32, (SINGLES, 128), 1)
    spans = jnp.broadcast_to(counts_v[0:SINGLES, :], (SINGLES, 128))
    named = [jnp.broadcast_to(table_v[0:SINGLES, m : m + 1], (SINGLES, 128)) for m in range(slots)]
    seen = [jnp.where(lane + m * 128 < spans, 1.0, 0.0) for m in range(slots)]
    for page in range(pages):
        total = jnp.zeros((SINGLES, 128), jnp.float32)
        for m in range(slots):
            total = total + jnp.where(named[m] == page, seen[m], 0.0)
        times[:, page * 128 : (page + 1) * 128] = total

    copies[0].wait()
    q_single = jnp.concatenate([q[0:SINGLES, h * HD : (h + 1) * HD] for h in range(group)], axis=0)
    q_prompt = jnp.concatenate([q[SINGLES:, h * HD : (h + 1) * HD] for h in range(group)], axis=0)
    step = 1024
    for start in range(0, pool_rows, step):
        scores[:, start : start + step] = dot_nt(q_single, k_pool[start : start + step, :])
    for m in range(slots):
        page = table_s[SINGLES, m]
        k_prompt[m * 128 : (m + 1) * 128, :] = k_pool[pl.ds(pl.multiple_of(page * 128, 128), 128), :]
    s_cache = dot_nt(q_prompt, k_prompt[...]) * root
    s_new = dot_nt(q_prompt, k_new[SINGLES:, :]) * root
    own = k_new[0:SINGLES, :].astype(jnp.float32)

    denominators, own_parts = [], []
    for h in range(group):
        rows = slice(h * SINGLES, (h + 1) * SINGLES)
        often = times[...]
        s = jnp.where(often > 0.0, scores[rows, :] * root, NEG)
        s_own = (
            jnp.sum(q_single[rows, :].astype(jnp.float32) * own, axis=1, keepdims=True) * root
        )
        highest = jnp.maximum(jnp.max(s, axis=1, keepdims=True), s_own)
        p = jnp.exp(s - highest) * often
        p_own = jnp.exp(s_own - highest)
        denominators.append(jnp.sum(p, axis=1, keepdims=True) + p_own)
        own_parts.append(p_own)
        weights[rows, :] = p.astype(jnp.bfloat16)

    position = lax.broadcasted_iota(jnp.int32, s_cache.shape, 1)
    s_cache = jnp.where(position < counts_s[SINGLES], s_cache, NEG)
    row = lax.broadcasted_iota(jnp.int32, (PROMPT, PROMPT), 0)
    col = lax.broadcasted_iota(jnp.int32, (PROMPT, PROMPT), 1)
    causal = jnp.concatenate([jnp.where(row >= col, 0.0, NEG)] * group, axis=0)
    s_new = s_new + causal
    highest = jnp.maximum(
        jnp.max(s_cache, axis=1, keepdims=True), jnp.max(s_new, axis=1, keepdims=True)
    )
    p_cache = jnp.exp(s_cache - highest)
    p_new = jnp.exp(s_new - highest)
    denominator = jnp.sum(p_cache, axis=1, keepdims=True) + jnp.sum(p_new, axis=1, keepdims=True)

    copies[1].wait()
    for m in range(slots):
        page = table_s[SINGLES, m]
        v_prompt[m * 128 : (m + 1) * 128, :] = v_pool[pl.ds(pl.multiple_of(page * 128, 128), 128), :]
    out_prompt = dot_nn(p_cache.astype(jnp.bfloat16), v_prompt[...])
    out_prompt = out_prompt + dot_nn(p_new.astype(jnp.bfloat16), v_new[SINGLES:, :])
    out_prompt = (out_prompt / denominator).astype(jnp.bfloat16)
    out_single = dot_nn(weights[...], v_pool[...])
    fresh = v_new[0:SINGLES, :].astype(jnp.float32)
    for h in range(group):
        lanes = slice(h * HD, (h + 1) * HD)
        one = out_single[h * SINGLES : (h + 1) * SINGLES, :] + own_parts[h] * fresh
        heads[0:SINGLES, lanes] = (one / denominators[h]).astype(jnp.bfloat16)
        heads[SINGLES:, lanes] = out_prompt[h * PROMPT : (h + 1) * PROMPT, :]

    t = place[0]
    core, y = lax.rem(t, 2), lax.div(t, 2)
    order = [(1 - y) * 2 + 1 - core, y * 2 + 1 - core, (1 - y) * 2 + core, y * 2 + core]
    for i, block in enumerate(order):
        ordered[i * 16 : (i + 1) * 16, :] = heads[pl.ds(pl.multiple_of(block * 16, 16), 16), :]
    copies[2].wait()
    for start in range(0, w_out.shape[1], 512):
        part = dot_nn(ordered[...], w_out[:, start : start + 512]).astype(jnp.bfloat16)
        send[:, start : start + 512] = part[0:32, :]
        keep[:, start : start + 512] = part[32:64, :]


def attention_call(place, table, counts, q, k_new, v_new, k_pool, v_pool, w_out):
    pool_rows, rows, width = k_pool.shape[0], q.shape[0], w_out.shape[1]
    vmem, smem, hbm = (pl.BlockSpec(memory_space=s) for s in (pltpu.VMEM, pltpu.SMEM, pl.ANY))
    half = jax.ShapeDtypeStruct((rows // 2, width), jnp.bfloat16)
    singles = SINGLES * (q.shape[1] // HD)
    return pl.pallas_call(
        attend_kernel,
        out_shape=(half, half),
        in_specs=[smem, smem, vmem, vmem, smem, vmem, vmem, vmem, hbm, hbm, hbm],
        out_specs=(vmem, vmem),
        scratch_shapes=[
            pltpu.VMEM((pool_rows, HD), jnp.bfloat16),
            pltpu.VMEM((pool_rows, HD), jnp.bfloat16),
            pltpu.VMEM(w_out.shape, jnp.bfloat16),
            pltpu.VMEM((singles, pool_rows), jnp.float32),
            pltpu.VMEM((SINGLES, pool_rows), jnp.float32),
            pltpu.VMEM((singles, pool_rows), jnp.bfloat16),
            pltpu.VMEM((table.shape[1] * 128, HD), jnp.bfloat16),
            pltpu.VMEM((table.shape[1] * 128, HD), jnp.bfloat16),
            pltpu.VMEM((rows, q.shape[1]), jnp.bfloat16),
            pltpu.VMEM((rows, q.shape[1]), jnp.bfloat16),
            pltpu.SemaphoreType.DMA((3,)),
        ],
        compiler_params=pltpu.CompilerParams(vmem_limit_bytes=32 * MIB),
        cost_estimate=pl.CostEstimate(flops=10**9, bytes_accessed=8 * 10**6, transcendentals=6 * 10**5),
        name="attention",
    )(place, table, table, counts[:, None], counts, q, k_new, v_new, k_pool, v_pool, w_out)


def routes_kernel(hot, shares, pick, spread, scale):
    rows, tokens = pick.shape
    tile = scale.shape[0] // 5
    share = shares[...]
    kept = jnp.where(share > 0.0, 1.0, 0.0)
    below = lax.broadcasted_iota(jnp.int32, (tokens, tokens), 1) < lax.broadcasted_iota(
        jnp.int32, (tokens, tokens), 0
    )
    rank = dot_nn(jnp.where(below, 1.0, 0.0).astype(jnp.bfloat16), kept.astype(jnp.bfloat16))
    lane = lax.broadcasted_iota(jnp.int32, share.shape, 1)
    favored = hot[0]
    base = lane * tile + jnp.where((favored >= 0) & (lane > favored), tile, 0)
    place = jnp.where(kept > 0.0, rank + base.astype(jnp.float32), -1.0)
    place_t = place.T
    row_id = lax.broadcasted_iota(jnp.int32, (rows, tokens), 0).astype(jnp.float32)
    col_id = lax.broadcasted_iota(jnp.int32, (tokens, rows), 1).astype(jnp.float32)
    picked = jnp.zeros((rows, tokens), jnp.float32)
    spreading = jnp.zeros((tokens, rows), jnp.float32)
    for e in range(4):
        picked = picked + jnp.where(row_id == place_t[e : e + 1, :], 1.0, 0.0)
        spreading = spreading + jnp.where(col_id == place[:, e : e + 1], 1.0, 0.0)
    picked = picked.astype(jnp.bfloat16)
    pick[...] = picked
    spread[...] = spreading.astype(jnp.bfloat16)
    found = jnp.zeros((rows, share.shape[1]), jnp.float32)
    rest = share
    for _ in range(3):
        part = rest.astype(jnp.bfloat16)
        found = found + dot_nn(picked, part)
        rest = rest - part.astype(jnp.float32)
    row = lax.broadcasted_iota(jnp.int32, found.shape, 0)
    column = lax.broadcasted_iota(jnp.int32, found.shape, 1)
    first = column * tile + jnp.where((favored >= 0) & (column > favored), tile, 0)
    size = jnp.where(column == favored, 2 * tile, tile)
    mine = (row >= first) & (row < first + size) & (column < 4)
    total = jnp.sum(jnp.where(mine, found, 0.0), axis=1, keepdims=True)
    scale[...] = jnp.broadcast_to(total, scale.shape)


def routes_call(hot, shares, tile):
    tokens = shares.shape[0]
    vmem, smem = (pl.BlockSpec(memory_space=s) for s in (pltpu.VMEM, pltpu.SMEM))
    return pl.pallas_call(
        routes_kernel,
        out_shape=(
            jax.ShapeDtypeStruct((5 * tile, tokens), jnp.bfloat16),
            jax.ShapeDtypeStruct((tokens, 5 * tile), jnp.bfloat16),
            jax.ShapeDtypeStruct((5 * tile, 128), jnp.float32),
        ),
        in_specs=[smem, vmem],
        out_specs=(vmem, vmem, vmem),
        compiler_params=pltpu.CompilerParams(vmem_limit_bytes=32 * MIB),
        cost_estimate=pl.CostEstimate(flops=10**8, bytes_accessed=10**6, transcendentals=0),
        name="routes",
    )(hot, shares)


def experts_kernel(
    hot, a0, a1, a2, a3, b0, b1, b2, b3, pick, spread, scale, gate, up, down,
    a_send, a_keep, b_send, b_keep,
    tokens, taken, total, made, sems,
):
    expert, chunk = pl.program_id(0), pl.program_id(1)
    last = pl.num_programs(1) - 1
    tile = made.shape[0] // 5
    half = tokens.shape[1] // 2
    favored = hot[0]

    @pl.when((expert == 0) & (chunk == 0))
    def _():
        copies = []
        for i, ref in enumerate((a0, a1, a2, a3)):
            copies.append((ref, tokens.at[i * 128 : (i + 1) * 128, 0:half]))
        for i, ref in enumerate((b0, b1, b2, b3)):
            for j in range(2):
                first = (i // 2) * 256 + j * 128 + (i % 2) * 64
                copies.append(
                    (ref.at[j * 64 : (j + 1) * 64, :], tokens.at[first : first + 64, half:])
                )
        started = []
        for i, (src, dst) in enumerate(copies):
            copy = pltpu.make_async_copy(src, dst, sems.at[i])
            copy.start()
            started.append(copy)
        made[4 * tile :, :] = jnp.zeros_like(made[4 * tile :, :])
        for copy in started:
            copy.wait()

        @pl.loop(0, tokens.shape[1], step=512)
        def _(start):
            cols = pl.ds(pl.multiple_of(start, 512), 512)
            taken[:, cols] = dot_nn(pick[...], tokens[:, cols]).astype(jnp.bfloat16)

    first = expert * tile + jnp.where((favored >= 0) & (expert > favored), tile, 0)

    def run(rows):
        span = pl.ds(pl.multiple_of(first, 32), rows)
        x = taken[span, :]
        g = dot_nt(x, gate[0])
        u = dot_nt(x, up[0])
        act = (g / (1.0 + jnp.exp(-g)) * u).astype(jnp.bfloat16)
        part = scale[span, 0:1]

        @pl.when(chunk == 0)
        def _():
            total[0:rows, :] = dot_nn(act, down[0])

        @pl.when(chunk > 0)
        def _():
            total[0:rows, :] += dot_nn(act, down[0])

        @pl.when(chunk == last)
        def _():
            made[span, :] = (total[0:rows, :] * part).astype(jnp.bfloat16)

    @pl.when(expert == favored)
    def _():
        run(2 * tile)

    @pl.when(expert != favored)
    def _():
        run(tile)

    @pl.when((expert == pl.num_programs(0) - 1) & (chunk == last))
    def _():
        rows = tokens.shape[0] // 2
        for i, (out_keep, out_send) in enumerate(((a_keep, a_send), (b_keep, b_send))):

            @pl.loop(0, half, step=512)
            def _(start, i=i, out_keep=out_keep, out_send=out_send):
                cols = pl.ds(pl.multiple_of(start, 512), 512)
                source = pl.ds(pl.multiple_of(i * half + start, 512), 512)
                y = dot_nn(spread[...], made[:, source]).astype(jnp.bfloat16)
                for side, out in enumerate((out_keep, out_send)):
                    for j in range(4):
                        to = j if i == 0 else (j % 2) * 2 + j // 2
                        out[to * 64 : (to + 1) * 64, cols] = y[side * rows + j * 64 : side * rows + (j + 1) * 64, :]


def experts_call(hot, pieces, pick, spread, scale, gate, up, down):
    experts, hidden, width = gate.shape
    tokens = spread.shape[0]
    rows = pick.shape[0]
    tile = rows // 5
    chunk = hidden // 2
    vmem, smem, hbm = (pl.BlockSpec(memory_space=s) for s in (pltpu.VMEM, pltpu.SMEM, pl.ANY))
    weight = pl.BlockSpec((1, chunk, width), lambda e, c: (e, c, 0))
    out = jax.ShapeDtypeStruct((tokens // 2, width // 2), jnp.bfloat16)
    return pl.pallas_call(
        experts_kernel,
        grid=(experts, 2),
        out_shape=(out, out, out, out),
        in_specs=[smem] + [hbm] * 8 + [vmem] * 3 + [weight] * 3,
        out_specs=(vmem,) * 4,
        scratch_shapes=[
            pltpu.VMEM((tokens, width), jnp.bfloat16),
            pltpu.VMEM((rows, width), jnp.bfloat16),
            pltpu.VMEM((2 * tile, width), jnp.float32),
            pltpu.VMEM((rows, width), jnp.bfloat16),
            pltpu.SemaphoreType.DMA((12,)),
        ],
        compiler_params=pltpu.CompilerParams(vmem_limit_bytes=50 * MIB),
        cost_estimate=pl.CostEstimate(
            flops=6 * rows * hidden * width, bytes_accessed=experts * 6 * hidden * width, transcendentals=rows * hidden
        ),
        name="experts",
    )(hot, *pieces, pick, spread, scale, gate, up, down)


def kept_shares(chosen_specialists, selection_shares, allowed_placements, favored_specialist):
    count, experts = chosen_specialists.shape[0], allowed_placements.shape[0]
    index = jnp.arange(experts, dtype=jnp.int32)
    picked = chosen_specialists[:, :, None] == index[None, None, :]
    named = jnp.any(picked, axis=1)
    earlier = jnp.arange(count)[:, None] > jnp.arange(count)[None, :]
    before = jnp.dot(
        earlier.astype(jnp.bfloat16), named.astype(jnp.bfloat16), preferred_element_type=jnp.float32
    )
    limit = jnp.where(index == favored_specialist[0], PLACEMENT_MOST, allowed_placements)
    share = jnp.sum(jnp.where(picked, selection_shares[:, :, None], 0.0), axis=1)
    return jnp.where(before < limit[None, :].astype(jnp.float32), share, 0.0)


def joined(*parts):
    return jnp.concatenate(parts, axis=0)


def plus(a, b):
    return (a.astype(jnp.float32) + b.astype(jnp.float32)).astype(jnp.bfloat16)


def local_fast(
    skip_stream_entry,
    question_vectors,
    fresh_lookup_vectors,
    fresh_content_vectors,
    stored_lookup_sheets,
    stored_content_sheets,
    sequence_sheet_map,
    stored_position_counts,
    attention_merge_matrix,
    premix_scale_factor,
    chosen_specialists,
    selection_shares,
    allowed_placements,
    favored_specialist,
    gating_matrices,
    expand_matrices,
    contract_matrices,
):
    width = skip_stream_entry.shape[1]
    half = width // 2
    own_experts = gating_matrices.shape[0]
    count = chosen_specialists.shape[0]
    z, x, t = (lax.axis_index(name) for name in ("dp", "expert", "tensor"))

    shares = kept_shares(chosen_specialists, selection_shares, allowed_placements, favored_specialist)
    shares = lax.all_gather(shares, ("dp", "expert", "tensor"), axis=0, tiled=True)
    away = jnp.arange(32, dtype=jnp.int32)
    block = ((z ^ (away % 4)) * 2 + (x ^ (away // 4 % 2))) * 4 + (t ^ (away // 8 % 2 * 2 + away // 16))
    shares = lax.dynamic_slice_in_dim(shares, x * own_experts, own_experts, 1)
    shares = shares.reshape(32, count, own_experts)[block].reshape(32 * count, own_experts)
    shares = jnp.pad(shares, ((0, 0), (0, 128 - own_experts)))
    hot = favored_specialist - x * own_experts
    hot = jnp.where((hot >= 0) & (hot < own_experts), hot, -1).astype(jnp.int32)
    pick, spread, scale = routes_call(hot, shares, CAP_MOST * 32)

    send, keep = attention_call(
        t.astype(jnp.int32)[None],
        sequence_sheet_map,
        stored_position_counts,
        question_vectors,
        fresh_lookup_vectors,
        fresh_content_vectors,
        stored_lookup_sheets.reshape(-1, HD),
        stored_content_sheets.reshape(-1, HD),
        attention_merge_matrix,
    )
    got = over_core(send)
    far = plus(got[0:count], keep[0:count])
    near = plus(got[count:], keep[count:])
    own_attn = over_y(far).astype(jnp.float32) + near.astype(jnp.float32)
    stream = (skip_stream_entry.astype(jnp.float32) + own_attn).astype(jnp.bfloat16)
    wide = stream.astype(jnp.float32)
    squares = jnp.mean(wide * wide, axis=1, keepdims=True)
    normed = (wide * lax.rsqrt(squares + 1e-05) * premix_scale_factor.astype(jnp.float32)).astype(
        jnp.bfloat16
    )

    pieces = []
    for i, (first, second) in enumerate(((over_x, over_y), (over_y, over_x))):
        part = normed[:, i * half : (i + 1) * half]
        part = joined(part, over_z(part, 1), over_z(part, 2), over_z(part, 3))
        part = joined(part, first(part))
        other = second(part)
        pieces += [part, other, over_core(part), over_core(other)]
    a_send, a_keep, b_send, b_keep = experts_call(
        hot, pieces, pick, spread, scale, gating_matrices, expand_matrices, contract_matrices
    )
    results = []
    for sent, kept, first, second in (
        (a_send, a_keep, over_y, over_x),
        (b_send, b_keep, over_x, over_y),
    ):
        got = over_core(sent)
        rows = kept.shape[0] // 2
        far = plus(got[rows:], kept[rows:])
        near = plus(got[:rows], kept[:rows])
        got = first(far)
        rows = rows // 2
        far = plus(got[rows:], near[rows:])
        near = plus(got[:rows], near[:rows])
        got = second(far)
        total = near.astype(jnp.float32) + got.astype(jnp.float32)
        out = total[0:count]
        for k in (1, 2, 3):
            mine = total[k * count : (k + 1) * count].astype(jnp.bfloat16)
            out = out + over_z(mine, k).astype(jnp.float32)
        results.append(out)
    return (wide + jnp.concatenate(results, axis=1)).astype(jnp.bfloat16)


def solution(mesh):
    placed = (
        P(("dp", "expert", "tensor"), None),
        P(("dp", "expert"), "tensor"),
        P(("dp", "expert"), "tensor"),
        P(("dp", "expert"), "tensor"),
        P(("dp", "expert"), "tensor", None, None),
        P(("dp", "expert"), "tensor", None, None),
        P(("dp", "expert"), None),
        P(("dp", "expert")),
        P("tensor", None),
        P(),
        P(("dp", "expert", "tensor"), None),
        P(("dp", "expert", "tensor"), None),
        P(),
        P(),
        P("expert", ("dp", "tensor"), None),
        P("expert", ("dp", "tensor"), None),
        P("expert", ("dp", "tensor"), None),
    )
    sizes = tuple(mesh.shape[name] for name in ("dp", "expert", "tensor"))
    return jax.shard_map(
        local_fast if sizes == (4, 2, 4) else local,
        mesh=mesh,
        in_specs=placed,
        out_specs=P(("dp", "expert", "tensor"), None),
        check_vma=False,
    )
```

```python
import functools
from functools import reduce
import math

import jax
import jax.numpy as jnp
from jax import lax
from jax.experimental import pallas as pl
from jax.experimental.pallas import tpu as pltpu
from jax.sharding import PartitionSpec as P

HD = 128
PLACEMENT_MOST = 6


def normalize(parts):
    highest = reduce(
        jnp.maximum,
        [
            jnp.max(jnp.where(visible, scores, -jnp.inf), axis=-1, keepdims=True)
            for scores, visible in parts
        ],
    )
    portions = [jnp.where(visible, jnp.exp(scores - highest), 0.0) for scores, visible in parts]
    denominator = reduce(
        jnp.add, [jnp.sum(portion, axis=-1, keepdims=True) for portion in portions]
    )
    return [(portion / denominator).astype(jnp.bfloat16) for portion in portions]


def attend(question_vectors, new_keys, new_values, key_pages, value_pages, table, spans):
    rows_all, head_count, head_width = question_vectors.shape
    kv_heads = new_keys.shape[1]
    group_size = head_count // kv_heads
    single_count = spans.shape[0] - 1
    page_count = table.shape[1]
    page_width = key_pages.shape[2]
    context = page_count * page_width
    inverse_root = 1.0 / math.sqrt(head_width)
    page_keys = key_pages[table]
    page_values = value_pages[table]
    grouped = question_vectors.reshape(rows_all, kv_heads, group_size, head_width)
    positions = jnp.arange(context, dtype=jnp.int32)
    single_q = grouped[:single_count]
    cache_dec = (
        jnp.einsum(
            "rkgh,rmkph->rkgmp",
            single_q,
            page_keys[:single_count],
            preferred_element_type=jnp.float32,
        ).reshape(single_count, kv_heads, group_size, context)
        * inverse_root
    )
    seen_dec = (positions[None, :] < spans[:single_count, None])[:, None, None, :]
    own_dec = (
        jnp.einsum(
            "rkgh,rkh->rkg", single_q, new_keys[:single_count], preferred_element_type=jnp.float32
        )[..., None]
        * inverse_root
    )
    weight_cache, weight_own = normalize(
        [(cache_dec, seen_dec), (own_dec, jnp.full(own_dec.shape, True))]
    )
    out_dec = jnp.einsum(
        "rkgmp,rmkph->rkgh",
        weight_cache.reshape(single_count, kv_heads, group_size, page_count, page_width),
        page_values[:single_count],
        preferred_element_type=jnp.float32,
    )
    out_dec = (
        out_dec
        + weight_own.astype(jnp.float32)
        * new_values[:single_count].astype(jnp.float32)[:, :, None, :]
    )
    prompt_q = grouped[single_count:]
    prompt_rows = rows_all - single_count
    cache_pro = (
        jnp.einsum(
            "rkgh,mkph->rkgmp",
            prompt_q,
            page_keys[single_count],
            preferred_element_type=jnp.float32,
        ).reshape(prompt_rows, kv_heads, group_size, context)
        * inverse_root
    )
    seen_pro = (positions < spans[single_count])[None, None, None, :]
    new_pro = (
        jnp.einsum(
            "rkgh,mkh->rkgm", prompt_q, new_keys[single_count:], preferred_element_type=jnp.float32
        )
        * inverse_root
    )
    prompt_index = jnp.arange(prompt_rows, dtype=jnp.int32)
    causal = (prompt_index[:, None] >= prompt_index[None, :])[:, None, None, :]
    weight_cpro, weight_npro = normalize([(cache_pro, seen_pro), (new_pro, causal)])
    out_pro = jnp.einsum(
        "rkgmp,mkph->rkgh",
        weight_cpro.reshape(prompt_rows, kv_heads, group_size, page_count, page_width),
        page_values[single_count],
        preferred_element_type=jnp.float32,
    )
    out_pro = out_pro + jnp.einsum(
        "rkgm,mkh->rkgh", weight_npro, new_values[single_count:], preferred_element_type=jnp.float32
    )
    joined = jnp.concatenate([out_dec, out_pro], axis=0).astype(jnp.bfloat16)
    return joined.reshape(rows_all, head_count * head_width)


def slot_table(member, ranking, keeping, slot_count):
    slot_hit = (
        ranking[:, :, None, None] == jnp.arange(slot_count, dtype=jnp.int32)[None, None, None, :]
    )
    return ((member[..., None] > 0) & keeping[:, :, None, None] & slot_hit).astype(jnp.bfloat16)


def expert_pass(send, gating_matrices, expand_matrices, contract_matrices):
    specialist_index, slot_count, model_width = send.shape
    holders = lax.axis_size("expert")
    local_count = gating_matrices.shape[0]
    arrived = lax.all_to_all(
        send.reshape(holders, local_count, slot_count, model_width),
        "expert",
        split_axis=0,
        concat_axis=0,
        tiled=True,
    )
    row_piece = lax.all_gather(arrived, ("dp", "tensor"), axis=0, tiled=True)
    gate_part = jnp.einsum(
        "qesd,efd->qesf", row_piece, gating_matrices, preferred_element_type=jnp.float32
    )
    up_part = jnp.einsum(
        "qesd,efd->qesf", row_piece, expand_matrices, preferred_element_type=jnp.float32
    )
    hidden = (jax.nn.silu(gate_part) * up_part).astype(jnp.bfloat16)
    summed = lax.psum_scatter(
        jnp.einsum(
            "qesf,efd->qesd", hidden, contract_matrices, preferred_element_type=jnp.float32
        ).astype(jnp.bfloat16),
        ("dp", "tensor"),
        scatter_dimension=0,
        tiled=True,
    )
    arrived_back = lax.all_to_all(summed, "expert", split_axis=0, concat_axis=0, tiled=True)
    return arrived_back.reshape(specialist_index, slot_count, model_width)


def local(
    skip_stream_entry,
    question_vectors,
    fresh_lookup_vectors,
    fresh_content_vectors,
    stored_lookup_sheets,
    stored_content_sheets,
    sequence_sheet_map,
    stored_position_counts,
    attention_merge_matrix,
    premix_scale_factor,
    chosen_specialists,
    selection_shares,
    allowed_placements,
    favored_specialist,
    gating_matrices,
    expand_matrices,
    contract_matrices,
):
    token_count = chosen_specialists.shape[0]
    specialist_index = allowed_placements.shape[0]
    picked = (
        chosen_specialists[:, :, None]
        == jnp.arange(specialist_index, dtype=jnp.int32)[None, None, :]
    ).astype(jnp.int32)
    flat_routes = picked.reshape(token_count * 2, specialist_index)
    busiest_specialist = favored_specialist[0]
    before = (jnp.cumsum(flat_routes, axis=0) - flat_routes).reshape(
        token_count, 2, specialist_index
    )
    ranking = jnp.sum(before * picked, axis=2)
    placement_ceiling = jnp.where(
        jnp.arange(specialist_index, dtype=jnp.int32) == busiest_specialist,
        PLACEMENT_MOST,
        allowed_placements,
    )
    keeping = ranking < jnp.sum(picked * placement_ceiling[None, None, :], axis=2)
    row_total = question_vectors.shape[0]
    heads_out = attend(
        question_vectors.reshape(row_total, -1, HD),
        fresh_lookup_vectors.reshape(row_total, -1, HD),
        fresh_content_vectors.reshape(row_total, -1, HD),
        stored_lookup_sheets,
        stored_content_sheets,
        sequence_sheet_map,
        stored_position_counts,
    )
    total_attn = lax.psum(
        jnp.dot(heads_out, attention_merge_matrix, preferred_element_type=jnp.float32).astype(
            jnp.bfloat16
        ),
        "tensor",
    ).astype(jnp.float32)
    own_attn = lax.dynamic_slice_in_dim(
        total_attn, lax.axis_index("tensor") * token_count, token_count, 0
    )
    stream = (skip_stream_entry.astype(jnp.float32) + own_attn).astype(jnp.bfloat16)
    wide = stream.astype(jnp.float32)
    squares = jnp.mean(wide * wide, axis=1, keepdims=True)
    normed = (wide * lax.rsqrt(squares + 1e-05) * premix_scale_factor.astype(jnp.float32)).astype(
        jnp.bfloat16
    )
    main_slots = PLACEMENT_MOST
    table_main = slot_table(picked, ranking, keeping, main_slots)
    send = jnp.einsum(
        "nkes,nd->esd", table_main, normed, preferred_element_type=jnp.float32
    ).astype(jnp.bfloat16)
    expert_out = expert_pass(send, gating_matrices, expand_matrices, contract_matrices)
    chosen = jnp.einsum("nkes,esd->nkd", table_main, expert_out, preferred_element_type=jnp.float32)
    mixed = jnp.sum(selection_shares[:, :, None] * chosen, axis=1)
    return (wide + mixed).astype(jnp.bfloat16)


PAIRS_CORE = [(0, 1), (1, 0), (2, 3), (3, 2)]
PAIRS_Y = [(0, 2), (2, 0), (1, 3), (3, 1)]
PAIRS_X = [(0, 1), (1, 0)]
SINGLES = 16
PROMPT = 48
CAP_MOST = 3
NEG = -1e30
MIB = 1 << 20


def over_core(a):
    return lax.ppermute(a, "tensor", PAIRS_CORE)


def over_y(a):
    return lax.ppermute(a, "tensor", PAIRS_Y)


def over_x(a):
    return lax.ppermute(a, "expert", PAIRS_X)


def over_z(a, k):
    return lax.ppermute(a, "dp", [(i, i ^ k) for i in range(4)])


def dot_nt(a, b):
    return lax.dot_general(a, b, (((1,), (1,)), ((), ())), preferred_element_type=jnp.float32)


def dot_nn(a, b):
    return lax.dot_general(a, b, (((1,), (0,)), ((), ())), preferred_element_type=jnp.float32)


def attend_kernel(
    place, table, counts, q, k_new, v_new, k_hbm, v_hbm, w_hbm,
    send, keep,
    k_pool, v_pool, w_out, scores, times, weights, k_prompt, v_prompt, heads, ordered, sems,
):
    pool_rows = k_pool.shape[0]
    pages = pool_rows // 128
    slots = table.shape[0]
    group = q.shape[1] // HD
    copies = [
        pltpu.make_async_copy(src, dst, sems.at[i])
        for i, (src, dst) in enumerate(((k_hbm, k_pool), (v_hbm, v_pool), (w_hbm, w_out)))
    ]
    for copy in copies:
        copy.start()
    root = 1.0 / math.sqrt(HD)

    lane = lax.broadcasted_iota(jnp.int32, (SINGLES, 128), 1)
    request = lax.broadcasted_iota(jnp.int32, (SINGLES, 128), 0)
    spans = jnp.zeros((SINGLES, 128), jnp.int32)
    named = [spans] * slots
    for r in range(SINGLES):
        here = request == r
        spans = jnp.where(here, counts[r], spans)
        named = [jnp.where(here, table[m, r], named[m]) for m in range(slots)]
    seen = [jnp.where(lane + m * 128 < spans, 1.0, 0.0) for m in range(slots)]
    for page in range(pages):
        total = jnp.zeros((SINGLES, 128), jnp.float32)
        for m in range(slots):
            total = total + jnp.where(named[m] == page, seen[m], 0.0)
        times[:, page * 128 : (page + 1) * 128] = total

    copies[0].wait()
    q_single = jnp.concatenate([q[0:SINGLES, h * HD : (h + 1) * HD] for h in range(group)], axis=0)
    q_prompt = jnp.concatenate([q[SINGLES:, h * HD : (h + 1) * HD] for h in range(group)], axis=0)
    step = 1024
    for start in range(0, pool_rows, step):
        scores[:, start : start + step] = dot_nt(q_single, k_pool[start : start + step, :])
    for m in range(slots):
        page = table[m, SINGLES]
        k_prompt[m * 128 : (m + 1) * 128, :] = k_pool[pl.ds(pl.multiple_of(page * 128, 128), 128), :]
    s_cache = dot_nt(q_prompt, k_prompt[...]) * root
    s_new = dot_nt(q_prompt, k_new[SINGLES:, :]) * root
    own = k_new[0:SINGLES, :].astype(jnp.float32)

    denominators, own_parts = [], []
    for h in range(group):
        rows = slice(h * SINGLES, (h + 1) * SINGLES)
        often = times[...]
        s = jnp.where(often > 0.0, scores[rows, :] * root, NEG)
        s_own = (
            jnp.sum(q_single[rows, :].astype(jnp.float32) * own, axis=1, keepdims=True) * root
        )
        highest = jnp.maximum(jnp.max(s, axis=1, keepdims=True), s_own)
        p = jnp.exp(s - highest) * often
        p_own = jnp.exp(s_own - highest)
        denominators.append(jnp.sum(p, axis=1, keepdims=True) + p_own)
        own_parts.append(p_own)
        weights[rows, :] = p.astype(jnp.bfloat16)

    position = lax.broadcasted_iota(jnp.int32, s_cache.shape, 1)
    s_cache = jnp.where(position < counts[SINGLES], s_cache, NEG)
    row = lax.broadcasted_iota(jnp.int32, (PROMPT, PROMPT), 0)
    col = lax.broadcasted_iota(jnp.int32, (PROMPT, PROMPT), 1)
    causal = jnp.concatenate([jnp.where(row >= col, 0.0, NEG)] * group, axis=0)
    s_new = s_new + causal
    highest = jnp.maximum(
        jnp.max(s_cache, axis=1, keepdims=True), jnp.max(s_new, axis=1, keepdims=True)
    )
    p_cache = jnp.exp(s_cache - highest)
    p_new = jnp.exp(s_new - highest)
    denominator = jnp.sum(p_cache, axis=1, keepdims=True) + jnp.sum(p_new, axis=1, keepdims=True)

    copies[1].wait()
    for m in range(slots):
        page = table[m, SINGLES]
        v_prompt[m * 128 : (m + 1) * 128, :] = v_pool[pl.ds(pl.multiple_of(page * 128, 128), 128), :]
    out_prompt = dot_nn(p_cache.astype(jnp.bfloat16), v_prompt[...])
    out_prompt = out_prompt + dot_nn(p_new.astype(jnp.bfloat16), v_new[SINGLES:, :])
    out_prompt = (out_prompt / denominator).astype(jnp.bfloat16)
    out_single = dot_nn(weights[...], v_pool[...])
    fresh = v_new[0:SINGLES, :].astype(jnp.float32)
    for h in range(group):
        lanes = slice(h * HD, (h + 1) * HD)
        one = out_single[h * SINGLES : (h + 1) * SINGLES, :] + own_parts[h] * fresh
        heads[0:SINGLES, lanes] = (one / denominators[h]).astype(jnp.bfloat16)
        heads[SINGLES:, lanes] = out_prompt[h * PROMPT : (h + 1) * PROMPT, :]

    t = place[0]
    core, y = lax.rem(t, 2), lax.div(t, 2)
    order = [(1 - y) * 2 + 1 - core, y * 2 + 1 - core, (1 - y) * 2 + core, y * 2 + core]
    for i, block in enumerate(order):
        ordered[i * 16 : (i + 1) * 16, :] = heads[pl.ds(pl.multiple_of(block * 16, 16), 16), :]
    copies[2].wait()
    for start in range(0, w_out.shape[1], 512):
        part = dot_nn(ordered[...], w_out[:, start : start + 512]).astype(jnp.bfloat16)
        send[:, start : start + 512] = part[0:32, :]
        keep[:, start : start + 512] = part[32:64, :]


def attention_call(place, table, counts, q, k_new, v_new, k_pool, v_pool, w_out):
    pool_rows, rows, width = k_pool.shape[0], q.shape[0], w_out.shape[1]
    vmem, smem, hbm = (pl.BlockSpec(memory_space=s) for s in (pltpu.VMEM, pltpu.SMEM, pl.ANY))
    half = jax.ShapeDtypeStruct((rows // 2, width), jnp.bfloat16)
    singles = SINGLES * (q.shape[1] // HD)
    return pl.pallas_call(
        attend_kernel,
        out_shape=(half, half),
        in_specs=[smem, smem, smem, vmem, vmem, vmem, hbm, hbm, hbm],
        out_specs=(vmem, vmem),
        scratch_shapes=[
            pltpu.VMEM((pool_rows, HD), jnp.bfloat16),
            pltpu.VMEM((pool_rows, HD), jnp.bfloat16),
            pltpu.VMEM(w_out.shape, jnp.bfloat16),
            pltpu.VMEM((singles, pool_rows), jnp.float32),
            pltpu.VMEM((SINGLES, pool_rows), jnp.float32),
            pltpu.VMEM((singles, pool_rows), jnp.bfloat16),
            pltpu.VMEM((table.shape[0] * 128, HD), jnp.bfloat16),
            pltpu.VMEM((table.shape[0] * 128, HD), jnp.bfloat16),
            pltpu.VMEM((rows, q.shape[1]), jnp.bfloat16),
            pltpu.VMEM((rows, q.shape[1]), jnp.bfloat16),
            pltpu.SemaphoreType.DMA((3,)),
        ],
        compiler_params=pltpu.CompilerParams(vmem_limit_bytes=60 * MIB),
        cost_estimate=pl.CostEstimate(flops=10**9, bytes_accessed=8 * 10**6, transcendentals=6 * 10**5),
        name="attention",
    )(place, table, counts, q, k_new, v_new, k_pool, v_pool, w_out)


def routes_kernel(place, hot, n0, n1, n2, n3, pick_a, pick_b, spread_a, spread_b, scale):
    rows, tokens = pick_a.shape
    tile = rows // 5
    notes = jnp.concatenate([n0[...], n1[...], n2[...], n3[...]], axis=0)
    width = notes.shape[1]
    source = lax.broadcasted_iota(jnp.int32, (width, width), 0)
    target = lax.broadcasted_iota(jnp.int32, (width, width), 1)
    wanted = (source < 24) & (target < 4) & (lax.rem(source, 8) == place[0] * 4 + target)
    share = dot_nn(notes, jnp.where(wanted, 1.0, 0.0).astype(jnp.bfloat16))
    kept = jnp.where(share > 0.0, 1.0, 0.0)
    below = lax.broadcasted_iota(jnp.int32, (tokens, tokens), 1) < lax.broadcasted_iota(
        jnp.int32, (tokens, tokens), 0
    )
    rank = dot_nn(jnp.where(below, 1.0, 0.0).astype(jnp.bfloat16), kept.astype(jnp.bfloat16))
    lane = lax.broadcasted_iota(jnp.int32, share.shape, 1)
    favored = hot[0]
    base = lane * tile + jnp.where((favored >= 0) & (lane > favored), tile, 0)
    spot = jnp.where(kept > 0.0, rank + base.astype(jnp.float32), -1.0)
    spot_t = spot.T
    row_id = lax.broadcasted_iota(jnp.int32, (rows, tokens), 0).astype(jnp.float32)
    col_id = lax.broadcasted_iota(jnp.int32, (tokens, rows), 1).astype(jnp.float32)
    picked = jnp.zeros((rows, tokens), jnp.float32)
    spreading = jnp.zeros((tokens, rows), jnp.float32)
    for e in range(4):
        picked = picked + jnp.where(row_id == spot_t[e : e + 1, :], 1.0, 0.0)
        spreading = spreading + jnp.where(col_id == spot[:, e : e + 1], 1.0, 0.0)
    picked = picked.astype(jnp.bfloat16)
    spreading = spreading.astype(jnp.bfloat16)
    pick_a[...] = picked
    spread_a[...] = spreading
    for i in range(0, tokens // 64, 4):
        for j, k in enumerate((0, 2, 1, 3)):
            old, new = slice((i + k) * 64, (i + k + 1) * 64), slice((i + j) * 64, (i + j + 1) * 64)
            pick_b[:, new] = picked[:, old]
            spread_b[new, :] = spreading[old, :]
    found = dot_nn(picked, notes)
    row = lax.broadcasted_iota(jnp.int32, found.shape, 0)
    column = lax.broadcasted_iota(jnp.int32, found.shape, 1)
    mine = lax.rem(column, 8) - place[0] * 4
    first = mine * tile + jnp.where((favored >= 0) & (mine > favored), tile, 0)
    size = jnp.where(mine == favored, 2 * tile, tile)
    inside = (row >= first) & (row < first + size) & (mine >= 0) & (mine < 4) & (column < 24)
    total = jnp.sum(jnp.where(inside, found, 0.0), axis=1, keepdims=True)
    scale[...] = jnp.broadcast_to(total, scale.shape)


def routes_call(place, hot, pieces, tile):
    tokens = sum(piece.shape[0] for piece in pieces)
    rows = 5 * tile
    vmem, smem = (pl.BlockSpec(memory_space=s) for s in (pltpu.VMEM, pltpu.SMEM))
    column = pieces[0].shape[1] // 128 - 1
    note = pl.BlockSpec((pieces[0].shape[0], 128), lambda i: (0, column))
    pick = jax.ShapeDtypeStruct((rows, tokens), jnp.bfloat16)
    spread = jax.ShapeDtypeStruct((tokens, rows), jnp.bfloat16)
    return pl.pallas_call(
        routes_kernel,
        grid=(1,),
        out_shape=(pick, pick, spread, spread, jax.ShapeDtypeStruct((rows, 128), jnp.float32)),
        in_specs=[smem, smem] + [note] * 4,
        out_specs=(vmem,) * 5,
        compiler_params=pltpu.CompilerParams(vmem_limit_bytes=20 * MIB),
        cost_estimate=pl.CostEstimate(flops=10**8, bytes_accessed=2 * 10**6, transcendentals=0),
        name="routes",
    )(place, hot, *pieces)


def span_of(expert, favored, tile, rows):
    first = expert * tile + jnp.where((favored >= 0) & (expert > favored), tile, 0)
    return pl.ds(pl.multiple_of(first, 32), rows)


def by_size(expert, favored, tile, run):
    @pl.when(expert == favored)
    def _():
        run(span_of(expert, favored, tile, 2 * tile))

    @pl.when(expert != favored)
    def _():
        run(span_of(expert, favored, tile, tile))


def inner_kernel(done, hot, x0, x1, x2, x3, pick, gate, up, *refs):
    expert = pl.program_id(0)
    tile = pick.shape[0] // 5
    favored = hot[0]
    if done:
        g_in, u_in, act, taken = refs
    else:
        g_out, u_out, taken = refs

    @pl.when(expert == 0)
    def _():
        for start in range(0, taken.shape[1], 512):
            total = jnp.zeros((pick.shape[0], 512), jnp.float32)
            for i, piece in enumerate((x0, x1, x2, x3)):
                rows = piece.shape[0]
                total = total + dot_nn(pick[:, i * rows : (i + 1) * rows], piece[:, start : start + 512])
            taken[:, start : start + 512] = total.astype(jnp.bfloat16)
        if done:
            act[4 * tile :, :] = jnp.zeros_like(act[4 * tile :, :])

    def run(span):
        x = taken[span, :]
        g = dot_nt(x, gate[0])
        u = dot_nt(x, up[0])
        if done:
            g = g + g_in[span, :]
            u = u + u_in[span, :]
            act[span, :] = (g / (1.0 + jnp.exp(-g)) * u).astype(jnp.bfloat16)
        else:
            g_out[span, :] = g
            u_out[span, :] = u

    by_size(expert, favored, tile, run)


def inner_call(half, hot, pieces, pick, gate, up, before):
    experts, hidden, width = gate.shape
    rows = pick.shape[0]
    wide = width // 2
    vmem, smem = (pl.BlockSpec(memory_space=s) for s in (pltpu.VMEM, pltpu.SMEM))
    weight = pl.BlockSpec((1, hidden, wide), lambda e: (e, 0, half))
    part = jax.ShapeDtypeStruct((rows, hidden), jnp.float32)
    out = jax.ShapeDtypeStruct((rows, hidden), jnp.bfloat16)
    return pl.pallas_call(
        functools.partial(inner_kernel, bool(before)),
        grid=(experts,),
        out_shape=out if before else (part, part),
        in_specs=[smem] + [vmem] * 5 + [weight] * 2 + [vmem] * len(before),
        out_specs=vmem if before else (vmem, vmem),
        scratch_shapes=[pltpu.VMEM((rows, wide), jnp.bfloat16)],
        compiler_params=pltpu.CompilerParams(vmem_limit_bytes=24 * MIB),
        cost_estimate=pl.CostEstimate(
            flops=4 * rows * hidden * wide, bytes_accessed=experts * 4 * hidden * wide, transcendentals=rows * hidden
        ),
        name="inner_second" if before else "inner_first",
    )(hot, *pieces, pick, gate, up, *before)


def outer_kernel(hot, act, spread, scale, down, keep, send, made):
    expert = pl.program_id(0)
    tile = made.shape[0] // 5
    favored = hot[0]

    @pl.when(expert == 0)
    def _():
        made[4 * tile :, :] = jnp.zeros_like(made[4 * tile :, :])

    def run(span):
        made[span, :] = (dot_nn(act[span, :], down[0]) * scale[span, 0:1]).astype(jnp.bfloat16)

    by_size(expert, favored, tile, run)

    @pl.when(expert == pl.num_programs(0) - 1)
    def _():
        rows = keep.shape[0]
        for start in range(0, made.shape[1], 512):
            y = dot_nn(spread[...], made[:, start : start + 512]).astype(jnp.bfloat16)
            keep[:, start : start + 512] = y[0:rows, :]
            send[:, start : start + 512] = y[rows:, :]


def outer_call(half, hot, act, spread, scale, down):
    experts, hidden, width = down.shape
    rows, wide = act.shape[0], width // 2
    vmem, smem = (pl.BlockSpec(memory_space=s) for s in (pltpu.VMEM, pltpu.SMEM))
    weight = pl.BlockSpec((1, hidden, wide), lambda e: (e, 0, half))
    out = jax.ShapeDtypeStruct((spread.shape[0] // 2, wide), jnp.bfloat16)
    return pl.pallas_call(
        outer_kernel,
        grid=(experts,),
        out_shape=(out, out),
        in_specs=[smem] + [vmem] * 3 + [weight],
        out_specs=(vmem, vmem),
        scratch_shapes=[pltpu.VMEM((rows, wide), jnp.bfloat16)],
        compiler_params=pltpu.CompilerParams(vmem_limit_bytes=20 * MIB),
        cost_estimate=pl.CostEstimate(
            flops=4 * rows * hidden * wide, bytes_accessed=experts * 2 * hidden * wide, transcendentals=0
        ),
        name="outer",
    )(hot, act, spread, scale, down)


def kept_shares(chosen_specialists, selection_shares, allowed_placements, favored_specialist):
    count, experts = chosen_specialists.shape[0], allowed_placements.shape[0]
    index = jnp.arange(experts, dtype=jnp.int32)
    picked = chosen_specialists[:, :, None] == index[None, None, :]
    named = jnp.any(picked, axis=1)
    earlier = jnp.arange(count)[:, None] > jnp.arange(count)[None, :]
    before = jnp.dot(
        earlier.astype(jnp.bfloat16), named.astype(jnp.bfloat16), preferred_element_type=jnp.float32
    )
    limit = jnp.where(index == favored_specialist[0], PLACEMENT_MOST, allowed_placements)
    share = jnp.sum(jnp.where(picked, selection_shares[:, :, None], 0.0), axis=1)
    return jnp.where(before < limit[None, :].astype(jnp.float32), share, 0.0)


def notes_of(shares):
    parts = []
    for _ in range(3):
        part = lax.reduce_precision(shares, 8, 7)
        parts.append(part.astype(jnp.bfloat16))
        shares = shares - part
    notes = jnp.concatenate(parts, axis=1)
    return jnp.pad(notes, ((0, 0), (0, 128 - notes.shape[1])))


def joined(*parts):
    return jnp.concatenate(parts, axis=0)


def plus(a, b):
    return (a.astype(jnp.float32) + b.astype(jnp.float32)).astype(jnp.bfloat16)


def local_fast(
    skip_stream_entry,
    question_vectors,
    fresh_lookup_vectors,
    fresh_content_vectors,
    stored_lookup_sheets,
    stored_content_sheets,
    sequence_sheet_map,
    stored_position_counts,
    attention_merge_matrix,
    premix_scale_factor,
    chosen_specialists,
    selection_shares,
    allowed_placements,
    favored_specialist,
    gating_matrices,
    expand_matrices,
    contract_matrices,
):
    width = skip_stream_entry.shape[1]
    half = width // 2
    own_experts = gating_matrices.shape[0]
    count = chosen_specialists.shape[0]
    x, t = lax.axis_index("expert"), lax.axis_index("tensor")

    notes = notes_of(
        kept_shares(chosen_specialists, selection_shares, allowed_placements, favored_specialist)
    )
    hot = favored_specialist - x * own_experts
    hot = jnp.where((hot >= 0) & (hot < own_experts), hot, -1).astype(jnp.int32)

    send, keep = attention_call(
        t.astype(jnp.int32)[None],
        sequence_sheet_map.T,
        stored_position_counts,
        question_vectors,
        fresh_lookup_vectors,
        fresh_content_vectors,
        stored_lookup_sheets.reshape(-1, HD),
        stored_content_sheets.reshape(-1, HD),
        attention_merge_matrix,
    )
    got = over_core(send)
    far = plus(got[0:count], keep[0:count])
    near = plus(got[count:], keep[count:])
    own_attn = over_y(far).astype(jnp.float32) + near.astype(jnp.float32)
    stream = (skip_stream_entry.astype(jnp.float32) + own_attn).astype(jnp.bfloat16)
    wide = stream.astype(jnp.float32)
    squares = jnp.mean(wide * wide, axis=1, keepdims=True)
    normed = (wide * lax.rsqrt(squares + 1e-05) * premix_scale_factor.astype(jnp.float32)).astype(
        jnp.bfloat16
    )

    gathered = []
    for part, first, second in (
        (jnp.concatenate([normed[:, :half], notes], axis=1), over_x, over_y),
        (normed[:, half:], over_y, over_x),
    ):
        part = joined(part, over_z(part, 1), over_z(part, 2), over_z(part, 3))
        part = joined(part, first(part))
        other = second(part)
        gathered.append((part, other, over_core(part), over_core(other)))
    pick_a, pick_b, spread_a, spread_b, scale = routes_call(
        x.astype(jnp.int32)[None], hot, gathered[0], CAP_MOST * 32
    )
    before = inner_call(0, hot, gathered[0], pick_a, gating_matrices, expand_matrices, ())
    act = inner_call(1, hot, gathered[1], pick_b, gating_matrices, expand_matrices, before)
    a_keep, a_send = outer_call(0, hot, act, spread_a, scale, contract_matrices)
    b_keep, b_send = outer_call(1, hot, act, spread_b, scale, contract_matrices)
    results = []
    for sent, kept, first, second in (
        (a_send, a_keep, over_y, over_x),
        (b_send, b_keep, over_x, over_y),
    ):
        got = over_core(sent)
        rows = kept.shape[0] // 2
        far = plus(got[rows:], kept[rows:])
        near = plus(got[:rows], kept[:rows])
        got = first(far)
        rows = rows // 2
        far = plus(got[rows:], near[rows:])
        near = plus(got[:rows], near[:rows])
        got = second(far)
        total = near.astype(jnp.float32) + got.astype(jnp.float32)
        out = total[0:count]
        for k in (1, 2, 3):
            mine = total[k * count : (k + 1) * count].astype(jnp.bfloat16)
            out = out + over_z(mine, k).astype(jnp.float32)
        results.append(out)
    return (wide + jnp.concatenate(results, axis=1)).astype(jnp.bfloat16)


def solution(mesh):
    placed = (
        P(("dp", "expert", "tensor"), None),
        P(("dp", "expert"), "tensor"),
        P(("dp", "expert"), "tensor"),
        P(("dp", "expert"), "tensor"),
        P(("dp", "expert"), "tensor", None, None),
        P(("dp", "expert"), "tensor", None, None),
        P(("dp", "expert"), None),
        P(("dp", "expert")),
        P("tensor", None),
        P(),
        P(("dp", "expert", "tensor"), None),
        P(("dp", "expert", "tensor"), None),
        P(),
        P(),
        P("expert", ("dp", "tensor"), None),
        P("expert", ("dp", "tensor"), None),
        P("expert", ("dp", "tensor"), None),
    )
    sizes = tuple(mesh.shape[name] for name in ("dp", "expert", "tensor"))
    return jax.shard_map(
        local_fast if sizes == (4, 2, 4) else local,
        mesh=mesh,
        in_specs=placed,
        out_specs=P(("dp", "expert", "tensor"), None),
        check_vma=False,
    )
```

```python
from functools import reduce
import math

import jax
import jax.numpy as jnp
from jax import lax
from jax.experimental import pallas as pl
from jax.experimental.pallas import tpu as pltpu
from jax.sharding import PartitionSpec as P

HD = 128
PLACEMENT_MOST = 6


def normalize(parts):
    highest = reduce(
        jnp.maximum,
        [
            jnp.max(jnp.where(visible, scores, -jnp.inf), axis=-1, keepdims=True)
            for scores, visible in parts
        ],
    )
    portions = [jnp.where(visible, jnp.exp(scores - highest), 0.0) for scores, visible in parts]
    denominator = reduce(
        jnp.add, [jnp.sum(portion, axis=-1, keepdims=True) for portion in portions]
    )
    return [(portion / denominator).astype(jnp.bfloat16) for portion in portions]


def attend(question_vectors, new_keys, new_values, key_pages, value_pages, table, spans):
    rows_all, head_count, head_width = question_vectors.shape
    kv_heads = new_keys.shape[1]
    group_size = head_count // kv_heads
    single_count = spans.shape[0] - 1
    page_count = table.shape[1]
    page_width = key_pages.shape[2]
    context = page_count * page_width
    inverse_root = 1.0 / math.sqrt(head_width)
    page_keys = key_pages[table]
    page_values = value_pages[table]
    grouped = question_vectors.reshape(rows_all, kv_heads, group_size, head_width)
    positions = jnp.arange(context, dtype=jnp.int32)
    single_q = grouped[:single_count]
    cache_dec = (
        jnp.einsum(
            "rkgh,rmkph->rkgmp",
            single_q,
            page_keys[:single_count],
            preferred_element_type=jnp.float32,
        ).reshape(single_count, kv_heads, group_size, context)
        * inverse_root
    )
    seen_dec = (positions[None, :] < spans[:single_count, None])[:, None, None, :]
    own_dec = (
        jnp.einsum(
            "rkgh,rkh->rkg", single_q, new_keys[:single_count], preferred_element_type=jnp.float32
        )[..., None]
        * inverse_root
    )
    weight_cache, weight_own = normalize(
        [(cache_dec, seen_dec), (own_dec, jnp.full(own_dec.shape, True))]
    )
    out_dec = jnp.einsum(
        "rkgmp,rmkph->rkgh",
        weight_cache.reshape(single_count, kv_heads, group_size, page_count, page_width),
        page_values[:single_count],
        preferred_element_type=jnp.float32,
    )
    out_dec = (
        out_dec
        + weight_own.astype(jnp.float32)
        * new_values[:single_count].astype(jnp.float32)[:, :, None, :]
    )
    prompt_q = grouped[single_count:]
    prompt_rows = rows_all - single_count
    cache_pro = (
        jnp.einsum(
            "rkgh,mkph->rkgmp",
            prompt_q,
            page_keys[single_count],
            preferred_element_type=jnp.float32,
        ).reshape(prompt_rows, kv_heads, group_size, context)
        * inverse_root
    )
    seen_pro = (positions < spans[single_count])[None, None, None, :]
    new_pro = (
        jnp.einsum(
            "rkgh,mkh->rkgm", prompt_q, new_keys[single_count:], preferred_element_type=jnp.float32
        )
        * inverse_root
    )
    prompt_index = jnp.arange(prompt_rows, dtype=jnp.int32)
    causal = (prompt_index[:, None] >= prompt_index[None, :])[:, None, None, :]
    weight_cpro, weight_npro = normalize([(cache_pro, seen_pro), (new_pro, causal)])
    out_pro = jnp.einsum(
        "rkgmp,mkph->rkgh",
        weight_cpro.reshape(prompt_rows, kv_heads, group_size, page_count, page_width),
        page_values[single_count],
        preferred_element_type=jnp.float32,
    )
    out_pro = out_pro + jnp.einsum(
        "rkgm,mkh->rkgh", weight_npro, new_values[single_count:], preferred_element_type=jnp.float32
    )
    joined = jnp.concatenate([out_dec, out_pro], axis=0).astype(jnp.bfloat16)
    return joined.reshape(rows_all, head_count * head_width)


def slot_table(member, ranking, keeping, slot_count):
    slot_hit = (
        ranking[:, :, None, None] == jnp.arange(slot_count, dtype=jnp.int32)[None, None, None, :]
    )
    return ((member[..., None] > 0) & keeping[:, :, None, None] & slot_hit).astype(jnp.bfloat16)


def expert_pass(send, gating_matrices, expand_matrices, contract_matrices):
    specialist_index, slot_count, model_width = send.shape
    holders = lax.axis_size("expert")
    local_count = gating_matrices.shape[0]
    arrived = lax.all_to_all(
        send.reshape(holders, local_count, slot_count, model_width),
        "expert",
        split_axis=0,
        concat_axis=0,
        tiled=True,
    )
    row_piece = lax.all_gather(arrived, ("dp", "tensor"), axis=0, tiled=True)
    gate_part = jnp.einsum(
        "qesd,efd->qesf", row_piece, gating_matrices, preferred_element_type=jnp.float32
    )
    up_part = jnp.einsum(
        "qesd,efd->qesf", row_piece, expand_matrices, preferred_element_type=jnp.float32
    )
    hidden = (jax.nn.silu(gate_part) * up_part).astype(jnp.bfloat16)
    summed = lax.psum_scatter(
        jnp.einsum(
            "qesf,efd->qesd", hidden, contract_matrices, preferred_element_type=jnp.float32
        ).astype(jnp.bfloat16),
        ("dp", "tensor"),
        scatter_dimension=0,
        tiled=True,
    )
    arrived_back = lax.all_to_all(summed, "expert", split_axis=0, concat_axis=0, tiled=True)
    return arrived_back.reshape(specialist_index, slot_count, model_width)


def local(
    skip_stream_entry,
    question_vectors,
    fresh_lookup_vectors,
    fresh_content_vectors,
    stored_lookup_sheets,
    stored_content_sheets,
    sequence_sheet_map,
    stored_position_counts,
    attention_merge_matrix,
    premix_scale_factor,
    chosen_specialists,
    selection_shares,
    allowed_placements,
    favored_specialist,
    gating_matrices,
    expand_matrices,
    contract_matrices,
):
    token_count = chosen_specialists.shape[0]
    specialist_index = allowed_placements.shape[0]
    picked = (
        chosen_specialists[:, :, None]
        == jnp.arange(specialist_index, dtype=jnp.int32)[None, None, :]
    ).astype(jnp.int32)
    flat_routes = picked.reshape(token_count * 2, specialist_index)
    busiest_specialist = favored_specialist[0]
    before = (jnp.cumsum(flat_routes, axis=0) - flat_routes).reshape(
        token_count, 2, specialist_index
    )
    ranking = jnp.sum(before * picked, axis=2)
    placement_ceiling = jnp.where(
        jnp.arange(specialist_index, dtype=jnp.int32) == busiest_specialist,
        PLACEMENT_MOST,
        allowed_placements,
    )
    keeping = ranking < jnp.sum(picked * placement_ceiling[None, None, :], axis=2)
    row_total = question_vectors.shape[0]
    heads_out = attend(
        question_vectors.reshape(row_total, -1, HD),
        fresh_lookup_vectors.reshape(row_total, -1, HD),
        fresh_content_vectors.reshape(row_total, -1, HD),
        stored_lookup_sheets,
        stored_content_sheets,
        sequence_sheet_map,
        stored_position_counts,
    )
    total_attn = lax.psum(
        jnp.dot(heads_out, attention_merge_matrix, preferred_element_type=jnp.float32).astype(
            jnp.bfloat16
        ),
        "tensor",
    ).astype(jnp.float32)
    own_attn = lax.dynamic_slice_in_dim(
        total_attn, lax.axis_index("tensor") * token_count, token_count, 0
    )
    stream = (skip_stream_entry.astype(jnp.float32) + own_attn).astype(jnp.bfloat16)
    wide = stream.astype(jnp.float32)
    squares = jnp.mean(wide * wide, axis=1, keepdims=True)
    normed = (wide * lax.rsqrt(squares + 1e-05) * premix_scale_factor.astype(jnp.float32)).astype(
        jnp.bfloat16
    )
    main_slots = PLACEMENT_MOST
    table_main = slot_table(picked, ranking, keeping, main_slots)
    send = jnp.einsum(
        "nkes,nd->esd", table_main, normed, preferred_element_type=jnp.float32
    ).astype(jnp.bfloat16)
    expert_out = expert_pass(send, gating_matrices, expand_matrices, contract_matrices)
    chosen = jnp.einsum("nkes,esd->nkd", table_main, expert_out, preferred_element_type=jnp.float32)
    mixed = jnp.sum(selection_shares[:, :, None] * chosen, axis=1)
    return (wide + mixed).astype(jnp.bfloat16)


PAIRS_CORE = [(0, 1), (1, 0), (2, 3), (3, 2)]
PAIRS_Y = [(0, 2), (2, 0), (1, 3), (3, 1)]
PAIRS_X = [(0, 1), (1, 0)]
SINGLES = 16
PROMPT = 48
CAP_MOST = 3
NEG = -1e30
MIB = 1 << 20


def over_core(a):
    return lax.ppermute(a, "tensor", PAIRS_CORE)


def over_y(a):
    return lax.ppermute(a, "tensor", PAIRS_Y)


def over_x(a):
    return lax.ppermute(a, "expert", PAIRS_X)


def over_z(a, k):
    return lax.ppermute(a, "dp", [(i, i ^ k) for i in range(4)])


def dot_nt(a, b):
    return lax.dot_general(a, b, (((1,), (1,)), ((), ())), preferred_element_type=jnp.float32)


def dot_nn(a, b):
    return lax.dot_general(a, b, (((1,), (0,)), ((), ())), preferred_element_type=jnp.float32)


def attend_kernel(
    place, table, counts, q, k_new, v_new, k_hbm, v_hbm, w_hbm,
    send, keep,
    k_pool, v_pool, w_out, scores, times, weights, k_prompt, v_prompt, heads, ordered, sems,
):
    pool_rows = k_pool.shape[0]
    pages = pool_rows // 128
    slots = table.shape[0]
    group = q.shape[1] // HD
    copies = [
        pltpu.make_async_copy(src, dst, sems.at[i])
        for i, (src, dst) in enumerate(((k_hbm, k_pool), (v_hbm, v_pool), (w_hbm, w_out)))
    ]
    for copy in copies:
        copy.start()
    root = 1.0 / math.sqrt(HD)

    lane = lax.broadcasted_iota(jnp.int32, (SINGLES, 128), 1)
    request = lax.broadcasted_iota(jnp.int32, (SINGLES, 128), 0)
    spans = jnp.zeros((SINGLES, 128), jnp.int32)
    named = [spans] * slots
    for r in range(SINGLES):
        here = request == r
        spans = jnp.where(here, counts[r], spans)
        named = [jnp.where(here, table[m, r], named[m]) for m in range(slots)]
    seen = [jnp.where(lane + m * 128 < spans, 1.0, 0.0) for m in range(slots)]
    for page in range(pages):
        total = jnp.zeros((SINGLES, 128), jnp.float32)
        for m in range(slots):
            total = total + jnp.where(named[m] == page, seen[m], 0.0)
        times[:, page * 128 : (page + 1) * 128] = total

    copies[0].wait()
    q_single = jnp.concatenate([q[0:SINGLES, h * HD : (h + 1) * HD] for h in range(group)], axis=0)
    q_prompt = jnp.concatenate([q[SINGLES:, h * HD : (h + 1) * HD] for h in range(group)], axis=0)
    step = 1024
    for start in range(0, pool_rows, step):
        scores[:, start : start + step] = dot_nt(q_single, k_pool[start : start + step, :])
    for m in range(slots):
        page = table[m, SINGLES]
        k_prompt[m * 128 : (m + 1) * 128, :] = k_pool[pl.ds(pl.multiple_of(page * 128, 128), 128), :]
    s_cache = dot_nt(q_prompt, k_prompt[...]) * root
    s_new = dot_nt(q_prompt, k_new[SINGLES:, :]) * root
    own = k_new[0:SINGLES, :].astype(jnp.float32)

    denominators, own_parts = [], []
    for h in range(group):
        rows = slice(h * SINGLES, (h + 1) * SINGLES)
        often = times[...]
        s = jnp.where(often > 0.0, scores[rows, :] * root, NEG)
        s_own = (
            jnp.sum(q_single[rows, :].astype(jnp.float32) * own, axis=1, keepdims=True) * root
        )
        highest = jnp.maximum(jnp.max(s, axis=1, keepdims=True), s_own)
        p = jnp.exp(s - highest) * often
        p_own = jnp.exp(s_own - highest)
        denominators.append(jnp.sum(p, axis=1, keepdims=True) + p_own)
        own_parts.append(p_own)
        weights[rows, :] = p.astype(jnp.bfloat16)

    position = lax.broadcasted_iota(jnp.int32, s_cache.shape, 1)
    s_cache = jnp.where(position < counts[SINGLES], s_cache, NEG)
    row = lax.broadcasted_iota(jnp.int32, (PROMPT, PROMPT), 0)
    col = lax.broadcasted_iota(jnp.int32, (PROMPT, PROMPT), 1)
    causal = jnp.concatenate([jnp.where(row >= col, 0.0, NEG)] * group, axis=0)
    s_new = s_new + causal
    highest = jnp.maximum(
        jnp.max(s_cache, axis=1, keepdims=True), jnp.max(s_new, axis=1, keepdims=True)
    )
    p_cache = jnp.exp(s_cache - highest)
    p_new = jnp.exp(s_new - highest)
    denominator = jnp.sum(p_cache, axis=1, keepdims=True) + jnp.sum(p_new, axis=1, keepdims=True)

    copies[1].wait()
    for m in range(slots):
        page = table[m, SINGLES]
        v_prompt[m * 128 : (m + 1) * 128, :] = v_pool[pl.ds(pl.multiple_of(page * 128, 128), 128), :]
    out_prompt = dot_nn(p_cache.astype(jnp.bfloat16), v_prompt[...])
    out_prompt = out_prompt + dot_nn(p_new.astype(jnp.bfloat16), v_new[SINGLES:, :])
    out_prompt = (out_prompt / denominator).astype(jnp.bfloat16)
    out_single = dot_nn(weights[...], v_pool[...])
    fresh = v_new[0:SINGLES, :].astype(jnp.float32)
    for h in range(group):
        lanes = slice(h * HD, (h + 1) * HD)
        one = out_single[h * SINGLES : (h + 1) * SINGLES, :] + own_parts[h] * fresh
        heads[0:SINGLES, lanes] = (one / denominators[h]).astype(jnp.bfloat16)
        heads[SINGLES:, lanes] = out_prompt[h * PROMPT : (h + 1) * PROMPT, :]

    t = place[0]
    core, y = lax.rem(t, 2), lax.div(t, 2)
    order = [(1 - y) * 2 + 1 - core, y * 2 + 1 - core, (1 - y) * 2 + core, y * 2 + core]
    for i, block in enumerate(order):
        ordered[i * 16 : (i + 1) * 16, :] = heads[pl.ds(pl.multiple_of(block * 16, 16), 16), :]
    copies[2].wait()
    for start in range(0, w_out.shape[1], 512):
        part = dot_nn(ordered[...], w_out[:, start : start + 512]).astype(jnp.bfloat16)
        send[:, start : start + 512] = part[0:32, :]
        keep[:, start : start + 512] = part[32:64, :]


def attention_call(place, table, counts, q, k_new, v_new, k_pool, v_pool, w_out):
    pool_rows, rows, width = k_pool.shape[0], q.shape[0], w_out.shape[1]
    vmem, smem, hbm = (pl.BlockSpec(memory_space=s) for s in (pltpu.VMEM, pltpu.SMEM, pl.ANY))
    half = jax.ShapeDtypeStruct((rows // 2, width), jnp.bfloat16)
    singles = SINGLES * (q.shape[1] // HD)
    return pl.pallas_call(
        attend_kernel,
        out_shape=(half, half),
        in_specs=[smem, smem, smem, vmem, vmem, vmem, hbm, hbm, hbm],
        out_specs=(vmem, vmem),
        scratch_shapes=[
            pltpu.VMEM((pool_rows, HD), jnp.bfloat16),
            pltpu.VMEM((pool_rows, HD), jnp.bfloat16),
            pltpu.VMEM(w_out.shape, jnp.bfloat16),
            pltpu.VMEM((singles, pool_rows), jnp.float32),
            pltpu.VMEM((SINGLES, pool_rows), jnp.float32),
            pltpu.VMEM((singles, pool_rows), jnp.bfloat16),
            pltpu.VMEM((table.shape[0] * 128, HD), jnp.bfloat16),
            pltpu.VMEM((table.shape[0] * 128, HD), jnp.bfloat16),
            pltpu.VMEM((rows, q.shape[1]), jnp.bfloat16),
            pltpu.VMEM((rows, q.shape[1]), jnp.bfloat16),
            pltpu.SemaphoreType.DMA((3,)),
        ],
        compiler_params=pltpu.CompilerParams(vmem_limit_bytes=60 * MIB),
        cost_estimate=pl.CostEstimate(flops=10**9, bytes_accessed=8 * 10**6, transcendentals=6 * 10**5),
        name="attention",
    )(place, table, counts, q, k_new, v_new, k_pool, v_pool, w_out)


def slot_spans(tile):
    return [(0, 2 * tile), (2 * tile, tile), (3 * tile, tile), (4 * tile, tile)]


def experts_kernel(
    place, favored, a0, a1, a2, a3, b0, b1, b2, b3, gate, up, down,
    a_keep, a_send, b_keep, b_send,
    tokens, ring, pick, spread, scale, taken, act, made, out_a, out_b, in_sems, w_sems, out_sems,
):
    count = tokens.shape[0]
    half = out_a.shape[1]
    notes_at = half
    tile = taken.shape[0] // 5
    spans = slot_spans(tile)
    first = jnp.maximum(favored[0], 0)
    expert_of = [first] + [jnp.where(s - 1 < first, s - 1, s) for s in (1, 2, 3)]

    loads = []
    for i, ref in enumerate((a0, a1, a2, a3)):
        loads.append((ref, tokens.at[i * 128 : (i + 1) * 128, 0 : half + 128]))
    for i, ref in enumerate((b0, b1, b2, b3)):
        for j in range(2):
            row = (i // 2) * 256 + j * 128 + (i % 2) * 64
            loads.append((ref.at[j * 64 : (j + 1) * 64, :], tokens.at[row : row + 64, half + 128 :]))
    loads = [pltpu.make_async_copy(src, dst, in_sems.at[i]) for i, (src, dst) in enumerate(loads)]
    for load in loads:
        load.start()

    def fetch(matrix, s, slot):
        return pltpu.make_async_copy(matrix.at[expert_of[s]], ring.at[slot], w_sems.at[slot])

    def fetch_inner(s):
        fetch(gate, s, 2 * s).start()
        fetch(up, s, 2 * s + 1).start()

    fetch_inner(0)

    for load in loads[:4]:
        load.wait()
    fetch_inner(1)
    notes = tokens[:, notes_at : notes_at + 128]
    width = notes.shape[1]
    source = lax.broadcasted_iota(jnp.int32, (width, width), 0)
    target = lax.broadcasted_iota(jnp.int32, (width, width), 1)
    expert = jnp.where(target == 0, first, jnp.where(target - 1 < first, target - 1, target))
    wanted = (source < 24) & (target < 4) & (lax.rem(source, 8) == place[0] * 4 + expert)
    share = dot_nn(notes, jnp.where(wanted, 1.0, 0.0).astype(jnp.bfloat16))
    kept = jnp.where(share > 0.0, 1.0, 0.0)
    below = lax.broadcasted_iota(jnp.int32, (count, count), 1) < lax.broadcasted_iota(
        jnp.int32, (count, count), 0
    )
    rank = dot_nn(jnp.where(below, 1.0, 0.0).astype(jnp.bfloat16), kept.astype(jnp.bfloat16))
    spot = jnp.where(kept > 0.0, rank, -1000.0)
    spot_t = spot.T
    lane = lax.broadcasted_iota(jnp.int32, (1, width), 1)
    for s, (row, rows) in enumerate(spans):
        ids = lax.broadcasted_iota(jnp.int32, (rows, count), 0).astype(jnp.float32)
        picked = jnp.where(ids == spot_t[s : s + 1, :], 1.0, 0.0).astype(jnp.bfloat16)
        pick[row : row + rows, :] = picked
        found = dot_nn(picked, notes)
        mine = (lane < 24) & (lax.rem(lane, 8) == place[0] * 4 + expert_of[s])
        part = jnp.sum(jnp.where(mine, found, 0.0), axis=1, keepdims=True)
        scale[row : row + rows, :] = jnp.broadcast_to(part, (rows, width))
    for block in range(spread.shape[1] // 128):
        ids = (lax.broadcasted_iota(jnp.int32, (count, 128), 1) + block * 128).astype(jnp.float32)
        total = jnp.zeros((count, 128), jnp.float32)
        for s, (row, rows) in enumerate(spans):
            if row < (block + 1) * 128 and row + rows > block * 128:
                total = total + jnp.where(ids == spot[:, s : s + 1] + row, 1.0, 0.0)
        spread[:, block * 128 : (block + 1) * 128] = total.astype(jnp.bfloat16)
    made[5 * tile :, :] = jnp.zeros_like(made[5 * tile :, :])

    for load in loads[4:]:
        load.wait()

    for start in range(0, 2 * half, 512):
        at = start if start < half else start + 128
        taken[:, start : start + 512] = dot_nn(pick[...], tokens[:, at : at + 512]).astype(jnp.bfloat16)

    fetch_inner(2)
    for s, (row, rows) in enumerate(spans):
        fetch(gate, s, 2 * s).wait()
        g = dot_nt(taken[row : row + rows, :], ring[2 * s])
        fetch(up, s, 2 * s + 1).wait()
        u = dot_nt(taken[row : row + rows, :], ring[2 * s + 1])
        act[row : row + rows, :] = (g / (1.0 + jnp.exp(-g)) * u).astype(jnp.bfloat16)
        if s == 0:
            fetch_inner(3)
        for later in ((), (0,), (1, 2), (3,))[s]:
            fetch(down, later, 2 * later).start()

    for s, (row, rows) in enumerate(spans):
        fetch(down, s, 2 * s).wait()
        part = scale[row : row + rows, 0:1]
        for start in range(0, 2 * half, 1024):
            o = dot_nn(act[row : row + rows, :], ring[2 * s, :, start : start + 1024])
            made[row : row + rows, start : start + 1024] = (o * part).astype(jnp.bfloat16)

    stores = []
    rows = count // 2
    for i, (out, out_keep, out_send) in enumerate(((out_a, a_keep, a_send), (out_b, b_keep, b_send))):
        for start in range(0, half, 1024):
            for at in range(start, start + 1024, 512):
                y = dot_nn(spread[...], made[:, i * half + at : i * half + at + 512]).astype(jnp.bfloat16)
                if i == 0:
                    out[:, at : at + 512] = y
                else:
                    for j in range(8):
                        to = (j // 4) * 4 + (j % 2) * 2 + (j // 2) % 2
                        out[to * 64 : (to + 1) * 64, at : at + 512] = y[j * 64 : (j + 1) * 64, :]
            for side, target_ref in enumerate((out_keep, out_send)):
                store = pltpu.make_async_copy(
                    out.at[side * rows : (side + 1) * rows, start : start + 1024],
                    target_ref.at[:, start : start + 1024],
                    out_sems.at[len(stores)],
                )
                store.start()
                stores.append(store)
    for store in stores:
        store.wait()


def experts_call(place, favored, pieces_a, pieces_b, gate, up, down):
    _, hidden, width = gate.shape
    count = sum(piece.shape[0] for piece in pieces_a)
    tile = CAP_MOST * 32
    rows, padded = 5 * tile, -(-5 * tile // 128) * 128
    half = width // 2
    smem, hbm = (pl.BlockSpec(memory_space=s) for s in (pltpu.SMEM, pl.ANY))
    out = jax.ShapeDtypeStruct((count // 2, half), jnp.bfloat16)
    return pl.pallas_call(
        experts_kernel,
        out_shape=(out,) * 4,
        in_specs=[smem, smem] + [hbm] * 11,
        out_specs=(hbm,) * 4,
        scratch_shapes=[
            pltpu.VMEM((count, width + 128), jnp.bfloat16),
            pltpu.VMEM((8, hidden, width), jnp.bfloat16),
            pltpu.VMEM((rows, count), jnp.bfloat16),
            pltpu.VMEM((count, padded), jnp.bfloat16),
            pltpu.VMEM((rows, 128), jnp.float32),
            pltpu.VMEM((rows, width), jnp.bfloat16),
            pltpu.VMEM((rows, hidden), jnp.bfloat16),
            pltpu.VMEM((padded, width), jnp.bfloat16),
            pltpu.VMEM((count, half), jnp.bfloat16),
            pltpu.VMEM((count, half), jnp.bfloat16),
            pltpu.SemaphoreType.DMA((12,)),
            pltpu.SemaphoreType.DMA((8,)),
            pltpu.SemaphoreType.DMA((8,)),
        ],
        compiler_params=pltpu.CompilerParams(vmem_limit_bytes=60 * MIB),
        cost_estimate=pl.CostEstimate(
            flops=6 * rows * hidden * width, bytes_accessed=24 * hidden * width, transcendentals=rows * hidden
        ),
        name="experts",
    )(place, favored, *pieces_a, *pieces_b, gate, up, down)


def kept_shares(chosen_specialists, selection_shares, allowed_placements, favored_specialist):
    count, experts = chosen_specialists.shape[0], allowed_placements.shape[0]
    index = jnp.arange(experts, dtype=jnp.int32)
    picked = chosen_specialists[:, :, None] == index[None, None, :]
    named = jnp.any(picked, axis=1)
    earlier = jnp.arange(count)[:, None] > jnp.arange(count)[None, :]
    before = jnp.dot(
        earlier.astype(jnp.bfloat16), named.astype(jnp.bfloat16), preferred_element_type=jnp.float32
    )
    limit = jnp.where(index == favored_specialist[0], PLACEMENT_MOST, allowed_placements)
    share = jnp.sum(jnp.where(picked, selection_shares[:, :, None], 0.0), axis=1)
    return jnp.where(before < limit[None, :].astype(jnp.float32), share, 0.0)


def notes_of(shares):
    parts = []
    for _ in range(3):
        part = lax.reduce_precision(shares, 8, 7)
        parts.append(part.astype(jnp.bfloat16))
        shares = shares - part
    notes = jnp.concatenate(parts, axis=1)
    return jnp.pad(notes, ((0, 0), (0, 128 - notes.shape[1])))


def joined(*parts):
    return jnp.concatenate(parts, axis=0)


def plus(a, b):
    return (a.astype(jnp.float32) + b.astype(jnp.float32)).astype(jnp.bfloat16)


def local_fast(
    skip_stream_entry,
    question_vectors,
    fresh_lookup_vectors,
    fresh_content_vectors,
    stored_lookup_sheets,
    stored_content_sheets,
    sequence_sheet_map,
    stored_position_counts,
    attention_merge_matrix,
    premix_scale_factor,
    chosen_specialists,
    selection_shares,
    allowed_placements,
    favored_specialist,
    gating_matrices,
    expand_matrices,
    contract_matrices,
):
    width = skip_stream_entry.shape[1]
    half = width // 2
    own_experts = gating_matrices.shape[0]
    count = chosen_specialists.shape[0]
    x, t = lax.axis_index("expert"), lax.axis_index("tensor")

    send, keep = attention_call(
        t.astype(jnp.int32)[None],
        sequence_sheet_map.T,
        stored_position_counts,
        question_vectors,
        fresh_lookup_vectors,
        fresh_content_vectors,
        stored_lookup_sheets.reshape(-1, HD),
        stored_content_sheets.reshape(-1, HD),
        attention_merge_matrix,
    )
    got, chosen_specialists, selection_shares, premix_scale_factor = lax.optimization_barrier(
        (over_core(send), chosen_specialists, selection_shares, premix_scale_factor)
    )
    far = plus(got[0:count], keep[0:count])
    near = plus(got[count:], keep[count:])
    own_attn = over_y(far).astype(jnp.float32) + near.astype(jnp.float32)
    stream = (skip_stream_entry.astype(jnp.float32) + own_attn).astype(jnp.bfloat16)
    wide = stream.astype(jnp.float32)
    squares = jnp.mean(wide * wide, axis=1, keepdims=True)
    normed = (wide * lax.rsqrt(squares + 1e-05) * premix_scale_factor.astype(jnp.float32)).astype(
        jnp.bfloat16
    )

    notes = notes_of(
        kept_shares(chosen_specialists, selection_shares, allowed_placements, favored_specialist)
    )
    hot = favored_specialist - x * own_experts
    hot = jnp.where((hot >= 0) & (hot < own_experts), hot, -1).astype(jnp.int32)

    part = jnp.concatenate([normed[:, :half], notes, normed[:, half:]], axis=1)
    column = [part, over_z(part, 1), over_z(part, 2), over_z(part, 3)]
    gathered = []
    for lanes, first, second in (
        (slice(0, half + 128), over_x, over_y),
        (slice(half + 128, None), over_y, over_x),
    ):
        part = joined(*[rows[:, lanes] for rows in column])
        part = joined(part, first(part))
        other = second(part)
        gathered.append((part, other, over_core(part), over_core(other)))
    a_keep, a_send, b_keep, b_send = experts_call(
        x.astype(jnp.int32)[None], hot, *gathered, gating_matrices, expand_matrices, contract_matrices
    )
    results = []
    for sent, kept, first, second in (
        (a_send, a_keep, over_y, over_x),
        (b_send, b_keep, over_x, over_y),
    ):
        got = over_core(sent)
        rows = kept.shape[0] // 2
        far = plus(got[rows:], kept[rows:])
        near = plus(got[:rows], kept[:rows])
        got = first(far)
        rows = rows // 2
        far = plus(got[rows:], near[rows:])
        near = plus(got[:rows], near[:rows])
        got = second(far)
        results.append(near.astype(jnp.float32) + got.astype(jnp.float32))
    total = jnp.concatenate(results, axis=1)
    out = total[0:count]
    for k in (1, 2, 3):
        mine = total[k * count : (k + 1) * count].astype(jnp.bfloat16)
        out = out + over_z(mine, k).astype(jnp.float32)
    return (wide + out).astype(jnp.bfloat16)


def solution(mesh):
    placed = (
        P(("dp", "expert", "tensor"), None),
        P(("dp", "expert"), "tensor"),
        P(("dp", "expert"), "tensor"),
        P(("dp", "expert"), "tensor"),
        P(("dp", "expert"), "tensor", None, None),
        P(("dp", "expert"), "tensor", None, None),
        P(("dp", "expert"), None),
        P(("dp", "expert")),
        P("tensor", None),
        P(),
        P(("dp", "expert", "tensor"), None),
        P(("dp", "expert", "tensor"), None),
        P(),
        P(),
        P("expert", ("dp", "tensor"), None),
        P("expert", ("dp", "tensor"), None),
        P("expert", ("dp", "tensor"), None),
    )
    sizes = tuple(mesh.shape[name] for name in ("dp", "expert", "tensor"))
    return jax.shard_map(
        local_fast if sizes == (4, 2, 4) else local,
        mesh=mesh,
        in_specs=placed,
        out_specs=P(("dp", "expert", "tensor"), None),
        check_vma=False,
    )
```

```python
from functools import reduce
import math

import jax
import jax.numpy as jnp
from jax import lax
from jax.experimental import pallas as pl
from jax.experimental.pallas import tpu as pltpu
from jax.sharding import PartitionSpec as P

HD = 128
PLACEMENT_MOST = 6


def normalize(parts):
    highest = reduce(
        jnp.maximum,
        [
            jnp.max(jnp.where(visible, scores, -jnp.inf), axis=-1, keepdims=True)
            for scores, visible in parts
        ],
    )
    portions = [jnp.where(visible, jnp.exp(scores - highest), 0.0) for scores, visible in parts]
    denominator = reduce(
        jnp.add, [jnp.sum(portion, axis=-1, keepdims=True) for portion in portions]
    )
    return [(portion / denominator).astype(jnp.bfloat16) for portion in portions]


def attend(question_vectors, new_keys, new_values, key_pages, value_pages, table, spans):
    rows_all, head_count, head_width = question_vectors.shape
    kv_heads = new_keys.shape[1]
    group_size = head_count // kv_heads
    single_count = spans.shape[0] - 1
    page_count = table.shape[1]
    page_width = key_pages.shape[2]
    context = page_count * page_width
    inverse_root = 1.0 / math.sqrt(head_width)
    page_keys = key_pages[table]
    page_values = value_pages[table]
    grouped = question_vectors.reshape(rows_all, kv_heads, group_size, head_width)
    positions = jnp.arange(context, dtype=jnp.int32)
    single_q = grouped[:single_count]
    cache_dec = (
        jnp.einsum(
            "rkgh,rmkph->rkgmp",
            single_q,
            page_keys[:single_count],
            preferred_element_type=jnp.float32,
        ).reshape(single_count, kv_heads, group_size, context)
        * inverse_root
    )
    seen_dec = (positions[None, :] < spans[:single_count, None])[:, None, None, :]
    own_dec = (
        jnp.einsum(
            "rkgh,rkh->rkg", single_q, new_keys[:single_count], preferred_element_type=jnp.float32
        )[..., None]
        * inverse_root
    )
    weight_cache, weight_own = normalize(
        [(cache_dec, seen_dec), (own_dec, jnp.full(own_dec.shape, True))]
    )
    out_dec = jnp.einsum(
        "rkgmp,rmkph->rkgh",
        weight_cache.reshape(single_count, kv_heads, group_size, page_count, page_width),
        page_values[:single_count],
        preferred_element_type=jnp.float32,
    )
    out_dec = (
        out_dec
        + weight_own.astype(jnp.float32)
        * new_values[:single_count].astype(jnp.float32)[:, :, None, :]
    )
    prompt_q = grouped[single_count:]
    prompt_rows = rows_all - single_count
    cache_pro = (
        jnp.einsum(
            "rkgh,mkph->rkgmp",
            prompt_q,
            page_keys[single_count],
            preferred_element_type=jnp.float32,
        ).reshape(prompt_rows, kv_heads, group_size, context)
        * inverse_root
    )
    seen_pro = (positions < spans[single_count])[None, None, None, :]
    new_pro = (
        jnp.einsum(
            "rkgh,mkh->rkgm", prompt_q, new_keys[single_count:], preferred_element_type=jnp.float32
        )
        * inverse_root
    )
    prompt_index = jnp.arange(prompt_rows, dtype=jnp.int32)
    causal = (prompt_index[:, None] >= prompt_index[None, :])[:, None, None, :]
    weight_cpro, weight_npro = normalize([(cache_pro, seen_pro), (new_pro, causal)])
    out_pro = jnp.einsum(
        "rkgmp,mkph->rkgh",
        weight_cpro.reshape(prompt_rows, kv_heads, group_size, page_count, page_width),
        page_values[single_count],
        preferred_element_type=jnp.float32,
    )
    out_pro = out_pro + jnp.einsum(
        "rkgm,mkh->rkgh", weight_npro, new_values[single_count:], preferred_element_type=jnp.float32
    )
    joined = jnp.concatenate([out_dec, out_pro], axis=0).astype(jnp.bfloat16)
    return joined.reshape(rows_all, head_count * head_width)


def slot_table(member, ranking, keeping, slot_count):
    slot_hit = (
        ranking[:, :, None, None] == jnp.arange(slot_count, dtype=jnp.int32)[None, None, None, :]
    )
    return ((member[..., None] > 0) & keeping[:, :, None, None] & slot_hit).astype(jnp.bfloat16)


def expert_pass(send, gating_matrices, expand_matrices, contract_matrices):
    specialist_index, slot_count, model_width = send.shape
    holders = lax.axis_size("expert")
    local_count = gating_matrices.shape[0]
    arrived = lax.all_to_all(
        send.reshape(holders, local_count, slot_count, model_width),
        "expert",
        split_axis=0,
        concat_axis=0,
        tiled=True,
    )
    row_piece = lax.all_gather(arrived, ("dp", "tensor"), axis=0, tiled=True)
    gate_part = jnp.einsum(
        "qesd,efd->qesf", row_piece, gating_matrices, preferred_element_type=jnp.float32
    )
    up_part = jnp.einsum(
        "qesd,efd->qesf", row_piece, expand_matrices, preferred_element_type=jnp.float32
    )
    hidden = (jax.nn.silu(gate_part) * up_part).astype(jnp.bfloat16)
    summed = lax.psum_scatter(
        jnp.einsum(
            "qesf,efd->qesd", hidden, contract_matrices, preferred_element_type=jnp.float32
        ).astype(jnp.bfloat16),
        ("dp", "tensor"),
        scatter_dimension=0,
        tiled=True,
    )
    arrived_back = lax.all_to_all(summed, "expert", split_axis=0, concat_axis=0, tiled=True)
    return arrived_back.reshape(specialist_index, slot_count, model_width)


def local(
    skip_stream_entry,
    question_vectors,
    fresh_lookup_vectors,
    fresh_content_vectors,
    stored_lookup_sheets,
    stored_content_sheets,
    sequence_sheet_map,
    stored_position_counts,
    attention_merge_matrix,
    premix_scale_factor,
    chosen_specialists,
    selection_shares,
    allowed_placements,
    favored_specialist,
    gating_matrices,
    expand_matrices,
    contract_matrices,
):
    token_count = chosen_specialists.shape[0]
    specialist_index = allowed_placements.shape[0]
    picked = (
        chosen_specialists[:, :, None]
        == jnp.arange(specialist_index, dtype=jnp.int32)[None, None, :]
    ).astype(jnp.int32)
    flat_routes = picked.reshape(token_count * 2, specialist_index)
    busiest_specialist = favored_specialist[0]
    before = (jnp.cumsum(flat_routes, axis=0) - flat_routes).reshape(
        token_count, 2, specialist_index
    )
    ranking = jnp.sum(before * picked, axis=2)
    placement_ceiling = jnp.where(
        jnp.arange(specialist_index, dtype=jnp.int32) == busiest_specialist,
        PLACEMENT_MOST,
        allowed_placements,
    )
    keeping = ranking < jnp.sum(picked * placement_ceiling[None, None, :], axis=2)
    row_total = question_vectors.shape[0]
    heads_out = attend(
        question_vectors.reshape(row_total, -1, HD),
        fresh_lookup_vectors.reshape(row_total, -1, HD),
        fresh_content_vectors.reshape(row_total, -1, HD),
        stored_lookup_sheets,
        stored_content_sheets,
        sequence_sheet_map,
        stored_position_counts,
    )
    total_attn = lax.psum(
        jnp.dot(heads_out, attention_merge_matrix, preferred_element_type=jnp.float32).astype(
            jnp.bfloat16
        ),
        "tensor",
    ).astype(jnp.float32)
    own_attn = lax.dynamic_slice_in_dim(
        total_attn, lax.axis_index("tensor") * token_count, token_count, 0
    )
    stream = (skip_stream_entry.astype(jnp.float32) + own_attn).astype(jnp.bfloat16)
    wide = stream.astype(jnp.float32)
    squares = jnp.mean(wide * wide, axis=1, keepdims=True)
    normed = (wide * lax.rsqrt(squares + 1e-05) * premix_scale_factor.astype(jnp.float32)).astype(
        jnp.bfloat16
    )
    main_slots = PLACEMENT_MOST
    table_main = slot_table(picked, ranking, keeping, main_slots)
    send = jnp.einsum(
        "nkes,nd->esd", table_main, normed, preferred_element_type=jnp.float32
    ).astype(jnp.bfloat16)
    expert_out = expert_pass(send, gating_matrices, expand_matrices, contract_matrices)
    chosen = jnp.einsum("nkes,esd->nkd", table_main, expert_out, preferred_element_type=jnp.float32)
    mixed = jnp.sum(selection_shares[:, :, None] * chosen, axis=1)
    return (wide + mixed).astype(jnp.bfloat16)


PAIRS_CORE = [(0, 1), (1, 0), (2, 3), (3, 2)]
PAIRS_Y = [(0, 2), (2, 0), (1, 3), (3, 1)]
PAIRS_X = [(0, 1), (1, 0)]
SINGLES = 16
PROMPT = 48
CAP_MOST = 3
NEG = -1e30
MIB = 1 << 20
EXPERTS_MIB = 43


def over_core(a):
    return lax.ppermute(a, "tensor", PAIRS_CORE)


def over_y(a):
    return lax.ppermute(a, "tensor", PAIRS_Y)


def over_x(a):
    return lax.ppermute(a, "expert", PAIRS_X)


def over_z(a, k):
    return lax.ppermute(a, "dp", [(i, i ^ k) for i in range(4)])


def dot_nt(a, b):
    return lax.dot_general(a, b, (((1,), (1,)), ((), ())), preferred_element_type=jnp.float32)


def dot_nn(a, b):
    return lax.dot_general(a, b, (((1,), (0,)), ((), ())), preferred_element_type=jnp.float32)


def note_routes(allowed, favored, chosen, shares, notes):
    experts, count = allowed.shape[0], chosen.shape[1]
    expert = lax.broadcasted_iota(jnp.int32, (experts, count), 0)
    picked = [jnp.where(chosen[k : k + 1, :] == expert, 1.0, 0.0) for k in range(2)]
    earlier = lax.broadcasted_iota(jnp.int32, (count, count), 0) < lax.broadcasted_iota(
        jnp.int32, (count, count), 1
    )
    before = dot_nn(
        (picked[0] + picked[1]).astype(jnp.bfloat16), jnp.where(earlier, 1.0, 0.0).astype(jnp.bfloat16)
    )
    limit = jnp.zeros((experts, count), jnp.int32)
    for e in range(experts):
        limit = jnp.where(expert == e, allowed[e], limit)
    limit = jnp.where(expert == favored[0], PLACEMENT_MOST, limit).astype(jnp.float32)
    rest = picked[0] * shares[0:1, :] + picked[1] * shares[1:2, :]
    rest = jnp.where(before < limit, rest, 0.0)
    parts = []
    for _ in range(3):
        part = rest.astype(jnp.bfloat16).astype(jnp.float32)
        parts.append(part)
        rest = rest - part
    parts.append(jnp.zeros((128 - 3 * experts, count), jnp.float32))
    parts = jnp.concatenate(parts, axis=0)
    parts = jnp.concatenate([parts, jnp.zeros((128, 128 - count), jnp.float32)], axis=1)
    notes[...] = parts.T[0:count, :].astype(jnp.bfloat16)


def attend_kernel(
    place, table, counts, allowed, favored, chosen, shares, q_hbm, k_new_hbm, v_new_hbm, k_hbm, v_hbm, w_hbm,
    send, keep, notes,
    q, k_new, v_new, k_pool, v_pool, w_out, scores, times, weights, k_prompt, v_prompt, heads, ordered, sems,
):
    pool_rows = k_pool.shape[0]
    pages = pool_rows // 128
    slots = table.shape[0]
    group = q.shape[1] // HD
    pairs = [(q_hbm, q), (k_new_hbm, k_new)]
    for source, target, parts in ((k_hbm, k_pool, 2), (v_hbm, v_pool, 2), (w_hbm, w_out, 4)):
        rows = source.shape[0] // parts
        for i in range(parts):
            pairs.append((source.at[i * rows : (i + 1) * rows, :], target.at[i * rows : (i + 1) * rows, :]))
    pairs.insert(4, (v_new_hbm, v_new))
    copies = [pltpu.make_async_copy(src, dst, sems.at[i]) for i, (src, dst) in enumerate(pairs)]
    for copy in copies:
        copy.start()
    note_routes(allowed, favored, chosen, shares, notes)
    root = 1.0 / math.sqrt(HD)

    lane = lax.broadcasted_iota(jnp.int32, (SINGLES, 128), 1)
    request = lax.broadcasted_iota(jnp.int32, (SINGLES, 128), 0)
    spans = jnp.zeros((SINGLES, 128), jnp.int32)
    named = [spans] * slots
    for r in range(SINGLES):
        here = request == r
        spans = jnp.where(here, counts[r], spans)
        named = [jnp.where(here, table[m, r], named[m]) for m in range(slots)]
    seen = [jnp.where(lane + m * 128 < spans, 1.0, 0.0) for m in range(slots)]
    for page in range(pages):
        total = jnp.zeros((SINGLES, 128), jnp.float32)
        for m in range(slots):
            total = total + jnp.where(named[m] == page, seen[m], 0.0)
        times[:, page * 128 : (page + 1) * 128] = total

    for copy in copies[:4]:
        copy.wait()
    q_single = jnp.concatenate([q[0:SINGLES, h * HD : (h + 1) * HD] for h in range(group)], axis=0)
    q_prompt = jnp.concatenate([q[SINGLES:, h * HD : (h + 1) * HD] for h in range(group)], axis=0)
    step = 1024
    for start in range(0, pool_rows, step):
        scores[:, start : start + step] = dot_nt(q_single, k_pool[start : start + step, :])
    for m in range(slots):
        page = table[m, SINGLES]
        k_prompt[m * 128 : (m + 1) * 128, :] = k_pool[pl.ds(pl.multiple_of(page * 128, 128), 128), :]
    s_cache = dot_nt(q_prompt, k_prompt[...]) * root
    s_new = dot_nt(q_prompt, k_new[SINGLES:, :]) * root
    own = k_new[0:SINGLES, :].astype(jnp.float32)

    denominators, own_parts = [], []
    for h in range(group):
        rows = slice(h * SINGLES, (h + 1) * SINGLES)
        often = times[...]
        s = jnp.where(often > 0.0, scores[rows, :] * root, NEG)
        s_own = (
            jnp.sum(q_single[rows, :].astype(jnp.float32) * own, axis=1, keepdims=True) * root
        )
        highest = jnp.maximum(jnp.max(s, axis=1, keepdims=True), s_own)
        p = jnp.exp(s - highest) * often
        p_own = jnp.exp(s_own - highest)
        denominators.append(jnp.sum(p, axis=1, keepdims=True) + p_own)
        own_parts.append(p_own)
        weights[rows, :] = p.astype(jnp.bfloat16)

    position = lax.broadcasted_iota(jnp.int32, s_cache.shape, 1)
    s_cache = jnp.where(position < counts[SINGLES], s_cache, NEG)
    row = lax.broadcasted_iota(jnp.int32, (PROMPT, PROMPT), 0)
    col = lax.broadcasted_iota(jnp.int32, (PROMPT, PROMPT), 1)
    causal = jnp.concatenate([jnp.where(row >= col, 0.0, NEG)] * group, axis=0)
    s_new = s_new + causal
    highest = jnp.maximum(
        jnp.max(s_cache, axis=1, keepdims=True), jnp.max(s_new, axis=1, keepdims=True)
    )
    p_cache = jnp.exp(s_cache - highest)
    p_new = jnp.exp(s_new - highest)
    denominator = jnp.sum(p_cache, axis=1, keepdims=True) + jnp.sum(p_new, axis=1, keepdims=True)

    for copy in copies[4:7]:
        copy.wait()
    for m in range(slots):
        page = table[m, SINGLES]
        v_prompt[m * 128 : (m + 1) * 128, :] = v_pool[pl.ds(pl.multiple_of(page * 128, 128), 128), :]
    out_prompt = dot_nn(p_cache.astype(jnp.bfloat16), v_prompt[...])
    out_prompt = out_prompt + dot_nn(p_new.astype(jnp.bfloat16), v_new[SINGLES:, :])
    out_prompt = (out_prompt / denominator).astype(jnp.bfloat16)
    out_single = dot_nn(weights[...], v_pool[...])
    fresh = v_new[0:SINGLES, :].astype(jnp.float32)
    for h in range(group):
        lanes = slice(h * HD, (h + 1) * HD)
        one = out_single[h * SINGLES : (h + 1) * SINGLES, :] + own_parts[h] * fresh
        heads[0:SINGLES, lanes] = (one / denominators[h]).astype(jnp.bfloat16)
        heads[SINGLES:, lanes] = out_prompt[h * PROMPT : (h + 1) * PROMPT, :]

    t = place[0]
    core, y = lax.rem(t, 2), lax.div(t, 2)
    order = [(1 - y) * 2 + 1 - core, y * 2 + 1 - core, (1 - y) * 2 + core, y * 2 + core]
    for i, block in enumerate(order):
        ordered[i * 16 : (i + 1) * 16, :] = heads[pl.ds(pl.multiple_of(block * 16, 16), 16), :]
    for copy in copies[7:]:
        copy.wait()
    for start in range(0, w_out.shape[1], 512):
        part = dot_nn(ordered[...], w_out[:, start : start + 512]).astype(jnp.bfloat16)
        send[:, start : start + 512] = part[0:32, :]
        keep[:, start : start + 512] = part[32:64, :]


def attention_call(place, table, counts, allowed, favored, chosen, shares, q, k_new, v_new, k_pool, v_pool, w_out):
    pool_rows, rows, width = k_pool.shape[0], q.shape[0], w_out.shape[1]
    vmem, smem, hbm = (pl.BlockSpec(memory_space=s) for s in (pltpu.VMEM, pltpu.SMEM, pl.ANY))
    half = jax.ShapeDtypeStruct((rows // 2, width), jnp.bfloat16)
    singles = SINGLES * (q.shape[1] // HD)
    return pl.pallas_call(
        attend_kernel,
        out_shape=(half, half, jax.ShapeDtypeStruct((chosen.shape[1], 128), jnp.bfloat16)),
        in_specs=[smem] * 5 + [vmem] * 2 + [hbm] * 6,
        out_specs=(vmem,) * 3,
        scratch_shapes=[
            pltpu.VMEM(q.shape, jnp.bfloat16),
            pltpu.VMEM(k_new.shape, jnp.bfloat16),
            pltpu.VMEM(v_new.shape, jnp.bfloat16),
            pltpu.VMEM((pool_rows, HD), jnp.bfloat16),
            pltpu.VMEM((pool_rows, HD), jnp.bfloat16),
            pltpu.VMEM(w_out.shape, jnp.bfloat16),
            pltpu.VMEM((singles, pool_rows), jnp.float32),
            pltpu.VMEM((SINGLES, pool_rows), jnp.float32),
            pltpu.VMEM((singles, pool_rows), jnp.bfloat16),
            pltpu.VMEM((table.shape[0] * 128, HD), jnp.bfloat16),
            pltpu.VMEM((table.shape[0] * 128, HD), jnp.bfloat16),
            pltpu.VMEM((rows, q.shape[1]), jnp.bfloat16),
            pltpu.VMEM((rows, q.shape[1]), jnp.bfloat16),
            pltpu.SemaphoreType.DMA((11,)),
        ],
        compiler_params=pltpu.CompilerParams(vmem_limit_bytes=60 * MIB),
        cost_estimate=pl.CostEstimate(flops=10**9, bytes_accessed=8 * 10**6, transcendentals=6 * 10**5),
        name="attention",
    )(place, table, counts, allowed, favored, chosen, shares, q, k_new, v_new, k_pool, v_pool, w_out)


def slot_spans(tile):
    return [(0, 2 * tile), (2 * tile, tile), (3 * tile, tile), (4 * tile, tile)]


def experts_kernel(
    place, favored, a0, a1, a2, a3, b0, b1, b2, b3, gate, up, down,
    a_keep, a_send, b_keep, b_send,
    tokens, ring, pick, spread, scale, taken, act, in_sems, w_sems,
):
    count, hidden = tokens.shape[0], act.shape[1]
    half = a_keep.shape[1]
    notes_at = half
    tile = taken.shape[0] // 5
    spans = slot_spans(tile)
    first = jnp.maximum(favored[0], 0)
    expert_of = [first] + [jnp.where(s - 1 < first, s - 1, s) for s in (1, 2, 3)]

    loads = []
    for i, ref in enumerate((a0, a1, a2, a3)):
        loads.append((ref, tokens.at[i * 128 : (i + 1) * 128, 0 : half + 128]))
    for i, ref in enumerate((b0, b1, b2, b3)):
        for j in range(2):
            row = (i // 2) * 256 + j * 128 + (i % 2) * 64
            loads.append((ref.at[j * 64 : (j + 1) * 64, :], tokens.at[row : row + 64, half + 128 :]))
    loads = [pltpu.make_async_copy(src, dst, in_sems.at[i]) for i, (src, dst) in enumerate(loads)]
    for load in loads:
        load.start()

    def fetch(matrix, s, slot):
        rows = ring.at[slot * hidden : (slot + 1) * hidden, :]
        return pltpu.make_async_copy(matrix.at[expert_of[s]], rows, w_sems.at[slot])

    def fetch_inner(s):
        fetch(gate, s, 2 * s).start()
        fetch(up, s, 2 * s + 1).start()

    for load in loads[:4]:
        load.wait()
    fetch_inner(0)
    notes = tokens[:, notes_at : notes_at + 128]
    width = notes.shape[1]
    source = lax.broadcasted_iota(jnp.int32, (width, width), 0)
    target = lax.broadcasted_iota(jnp.int32, (width, width), 1)
    expert = jnp.where(target == 0, first, jnp.where(target - 1 < first, target - 1, target))
    wanted = (source < 24) & (target < 4) & (lax.rem(source, 8) == place[0] * 4 + expert)
    share = dot_nn(notes, jnp.where(wanted, 1.0, 0.0).astype(jnp.bfloat16))
    kept = jnp.where(share > 0.0, 1.0, 0.0)
    below = lax.broadcasted_iota(jnp.int32, (count, count), 1) < lax.broadcasted_iota(
        jnp.int32, (count, count), 0
    )
    rank = dot_nn(jnp.where(below, 1.0, 0.0).astype(jnp.bfloat16), kept.astype(jnp.bfloat16))
    spot = jnp.where(kept > 0.0, rank, -1000.0)
    spot_t = spot.T
    lane = lax.broadcasted_iota(jnp.int32, (1, width), 1)
    for s, (row, rows) in enumerate(spans):
        ids = lax.broadcasted_iota(jnp.int32, (rows, count), 0).astype(jnp.float32)
        picked = jnp.where(ids == spot_t[s : s + 1, :], 1.0, 0.0).astype(jnp.bfloat16)
        pick[row : row + rows, :] = picked
        found = dot_nn(picked, notes)
        mine = (lane < 24) & (lax.rem(lane, 8) == place[0] * 4 + expert_of[s])
        part = jnp.sum(jnp.where(mine, found, 0.0), axis=1, keepdims=True)
        scale[row : row + rows, :] = jnp.broadcast_to(part, (rows, width))
    for block in range(spread.shape[1] // 128):
        ids = (lax.broadcasted_iota(jnp.int32, (count, 128), 1) + block * 128).astype(jnp.float32)
        total = jnp.zeros((count, 128), jnp.float32)
        for s, (row, rows) in enumerate(spans):
            if row < (block + 1) * 128 and row + rows > block * 128:
                total = total + jnp.where(ids == spot[:, s : s + 1] + row, 1.0, 0.0)
        spread[:, block * 128 : (block + 1) * 128] = total.astype(jnp.bfloat16)
    fetch_inner(1)
    for load in loads[4:]:
        load.wait()

    for start in range(0, 2 * half, 512):
        at = start if start < half else start + 128
        taken[:, start : start + 512] = dot_nn(pick[...], tokens[:, at : at + 512]).astype(jnp.bfloat16)

    fetch_inner(2)
    made = tokens
    made[5 * tile :, :] = jnp.zeros_like(made[5 * tile :, :])
    for s, (row, rows) in enumerate(spans):
        x = taken[row : row + rows, :]
        fetch(gate, s, 2 * s).wait()
        g = dot_nt(x, ring[2 * s * hidden : (2 * s + 1) * hidden, :])
        fetch(up, s, 2 * s + 1).wait()
        u = dot_nt(x, ring[(2 * s + 1) * hidden : (2 * s + 2) * hidden, :])
        act[row : row + rows, :] = (g / (1.0 + jnp.exp(-g)) * u).astype(jnp.bfloat16)
        if s == 0:
            fetch_inner(3)
        for later in ((), (0,), (1, 2), (3,))[s]:
            fetch(down, later, 2 * later).start()

    for s, (row, rows) in enumerate(spans):
        fetch(down, s, 2 * s).wait()
        part = scale[row : row + rows, 0:1]
        for start in range(0, 2 * half, 1024):
            o = dot_nn(act[row : row + rows, :], ring[2 * s * hidden : (2 * s + 1) * hidden, start : start + 1024])
            made[row : row + rows, start : start + 1024] = (o * part).astype(jnp.bfloat16)

    rows = count // 2
    for i, outs in enumerate(((a_keep, a_send), (b_keep, b_send))):
        for at in range(0, half, 512):
            y = dot_nn(spread[...], made[:, i * half + at : i * half + at + 512]).astype(jnp.bfloat16)
            for side, out in enumerate(outs):
                if i == 0:
                    out[:, at : at + 512] = y[side * rows : (side + 1) * rows, :]
                else:
                    for j in range(4):
                        to, row = (j % 2) * 2 + j // 2, side * rows + j * 64
                        out[to * 64 : (to + 1) * 64, at : at + 512] = y[row : row + 64, :]


def experts_call(place, favored, pieces_a, pieces_b, gate, up, down):
    _, hidden, width = gate.shape
    count = sum(piece.shape[0] for piece in pieces_a)
    tile = CAP_MOST * 32
    rows, padded = 5 * tile, -(-5 * tile // 128) * 128
    half = width // 2
    smem, vmem, hbm = (pl.BlockSpec(memory_space=s) for s in (pltpu.SMEM, pltpu.VMEM, pl.ANY))
    out = jax.ShapeDtypeStruct((count // 2, half), jnp.bfloat16)
    return pl.pallas_call(
        experts_kernel,
        out_shape=(out,) * 4,
        in_specs=[smem, smem] + [hbm] * 11,
        out_specs=(vmem,) * 4,
        scratch_shapes=[
            pltpu.VMEM((count, width + 128), jnp.bfloat16),
            pltpu.VMEM((8 * hidden, width), jnp.bfloat16),
            pltpu.VMEM((rows, count), jnp.bfloat16),
            pltpu.VMEM((count, padded), jnp.bfloat16),
            pltpu.VMEM((rows, 128), jnp.float32),
            pltpu.VMEM((rows, width), jnp.bfloat16),
            pltpu.VMEM((rows, hidden), jnp.bfloat16),
            pltpu.SemaphoreType.DMA((12,)),
            pltpu.SemaphoreType.DMA((8,)),
        ],
        compiler_params=pltpu.CompilerParams(vmem_limit_bytes=EXPERTS_MIB * MIB),
        cost_estimate=pl.CostEstimate(
            flops=6 * rows * hidden * width, bytes_accessed=24 * hidden * width, transcendentals=rows * hidden
        ),
        name="experts",
    )(place, favored, *pieces_a, *pieces_b, gate, up, down)


def joined(*parts):
    return jnp.concatenate(parts, axis=0)


def plus(a, b):
    return (a.astype(jnp.float32) + b.astype(jnp.float32)).astype(jnp.bfloat16)


def local_fast(
    skip_stream_entry,
    question_vectors,
    fresh_lookup_vectors,
    fresh_content_vectors,
    stored_lookup_sheets,
    stored_content_sheets,
    sequence_sheet_map,
    stored_position_counts,
    attention_merge_matrix,
    premix_scale_factor,
    chosen_specialists,
    selection_shares,
    allowed_placements,
    favored_specialist,
    gating_matrices,
    expand_matrices,
    contract_matrices,
):
    width = skip_stream_entry.shape[1]
    half = width // 2
    own_experts = gating_matrices.shape[0]
    count = chosen_specialists.shape[0]
    x, t = lax.axis_index("expert"), lax.axis_index("tensor")

    send, keep, notes = attention_call(
        t.astype(jnp.int32)[None],
        sequence_sheet_map.T,
        stored_position_counts,
        allowed_placements,
        favored_specialist,
        chosen_specialists.T,
        selection_shares.T,
        question_vectors,
        fresh_lookup_vectors,
        fresh_content_vectors,
        stored_lookup_sheets.reshape(-1, HD),
        stored_content_sheets.reshape(-1, HD),
        attention_merge_matrix,
    )
    got = over_core(send)
    far = plus(got[0:count], keep[0:count])
    near = plus(got[count:], keep[count:])
    own_attn = over_y(far).astype(jnp.float32) + near.astype(jnp.float32)
    stream = (skip_stream_entry.astype(jnp.float32) + own_attn).astype(jnp.bfloat16)
    wide = stream.astype(jnp.float32)
    squares = jnp.mean(wide * wide, axis=1, keepdims=True)
    normed = (wide * lax.rsqrt(squares + 1e-05) * premix_scale_factor.astype(jnp.float32)).astype(
        jnp.bfloat16
    )

    hot = favored_specialist - x * own_experts
    hot = jnp.where((hot >= 0) & (hot < own_experts), hot, -1).astype(jnp.int32)

    part = jnp.concatenate([normed[:, :half], notes, normed[:, half:]], axis=1)
    column = [part, over_z(part, 1), over_z(part, 2), over_z(part, 3)]
    gathered = []
    for lanes, first, second in (
        (slice(0, half + 128), over_x, over_y),
        (slice(half + 128, None), over_y, over_x),
    ):
        part = joined(*[rows[:, lanes] for rows in column])
        part = joined(part, first(part))
        other = second(part)
        gathered.append((part, other, over_core(part), over_core(other)))
    a_keep, a_send, b_keep, b_send = experts_call(
        x.astype(jnp.int32)[None], hot, *gathered, gating_matrices, expand_matrices, contract_matrices
    )
    results = []
    for sent, kept, first, second in (
        (a_send, a_keep, over_y, over_x),
        (b_send, b_keep, over_x, over_y),
    ):
        got = over_core(sent)
        rows = kept.shape[0] // 2
        from_first, got, kept = lax.optimization_barrier((first(plus(got[rows:], kept[rows:])), got, kept))
        rows = rows // 2
        near = plus(got[: 2 * rows], kept[: 2 * rows])
        got = second(plus(from_first[rows:], near[rows:]))
        near = plus(from_first[:rows], near[:rows])
        results.append(near.astype(jnp.float32) + got.astype(jnp.float32))
    total_a, total_b = results
    sent = jnp.concatenate([total_b[count : 2 * count], total_b[3 * count :]], axis=0).astype(jnp.bfloat16)
    got = over_z(sent, 1).astype(jnp.float32)
    out_a = total_a[0:count]
    for k in (1, 2, 3):
        mine = total_a[k * count : (k + 1) * count].astype(jnp.bfloat16)
        out_a = out_a + over_z(mine, k).astype(jnp.float32)
    far = (total_b[2 * count : 3 * count] + got[count:]).astype(jnp.bfloat16)
    out_b = total_b[0:count] + got[0:count] + over_z(far, 2).astype(jnp.float32)
    return (wide + jnp.concatenate([out_a, out_b], axis=1)).astype(jnp.bfloat16)


def solution(mesh):
    placed = (
        P(("dp", "expert", "tensor"), None),
        P(("dp", "expert"), "tensor"),
        P(("dp", "expert"), "tensor"),
        P(("dp", "expert"), "tensor"),
        P(("dp", "expert"), "tensor", None, None),
        P(("dp", "expert"), "tensor", None, None),
        P(("dp", "expert"), None),
        P(("dp", "expert")),
        P("tensor", None),
        P(),
        P(("dp", "expert", "tensor"), None),
        P(("dp", "expert", "tensor"), None),
        P(),
        P(),
        P("expert", ("dp", "tensor"), None),
        P("expert", ("dp", "tensor"), None),
        P("expert", ("dp", "tensor"), None),
    )
    sizes = tuple(mesh.shape[name] for name in ("dp", "expert", "tensor"))
    return jax.shard_map(
        local_fast if sizes == (4, 2, 4) else local,
        mesh=mesh,
        in_specs=placed,
        out_specs=P(("dp", "expert", "tensor"), None),
        check_vma=False,
    )
```

```python
from functools import reduce
import math

import jax
import jax.numpy as jnp
from jax import lax
from jax.experimental import pallas as pl
from jax.experimental.pallas import tpu as pltpu
from jax.sharding import PartitionSpec as P

HD = 128
PLACEMENT_MOST = 6


def normalize(parts):
    highest = reduce(
        jnp.maximum,
        [
            jnp.max(jnp.where(visible, scores, -jnp.inf), axis=-1, keepdims=True)
            for scores, visible in parts
        ],
    )
    portions = [jnp.where(visible, jnp.exp(scores - highest), 0.0) for scores, visible in parts]
    denominator = reduce(
        jnp.add, [jnp.sum(portion, axis=-1, keepdims=True) for portion in portions]
    )
    return [(portion / denominator).astype(jnp.bfloat16) for portion in portions]


def attend(question_vectors, new_keys, new_values, key_pages, value_pages, table, spans):
    rows_all, head_count, head_width = question_vectors.shape
    kv_heads = new_keys.shape[1]
    group_size = head_count // kv_heads
    single_count = spans.shape[0] - 1
    page_count = table.shape[1]
    page_width = key_pages.shape[2]
    context = page_count * page_width
    inverse_root = 1.0 / math.sqrt(head_width)
    page_keys = key_pages[table]
    page_values = value_pages[table]
    grouped = question_vectors.reshape(rows_all, kv_heads, group_size, head_width)
    positions = jnp.arange(context, dtype=jnp.int32)
    single_q = grouped[:single_count]
    cache_dec = (
        jnp.einsum(
            "rkgh,rmkph->rkgmp",
            single_q,
            page_keys[:single_count],
            preferred_element_type=jnp.float32,
        ).reshape(single_count, kv_heads, group_size, context)
        * inverse_root
    )
    seen_dec = (positions[None, :] < spans[:single_count, None])[:, None, None, :]
    own_dec = (
        jnp.einsum(
            "rkgh,rkh->rkg", single_q, new_keys[:single_count], preferred_element_type=jnp.float32
        )[..., None]
        * inverse_root
    )
    weight_cache, weight_own = normalize(
        [(cache_dec, seen_dec), (own_dec, jnp.full(own_dec.shape, True))]
    )
    out_dec = jnp.einsum(
        "rkgmp,rmkph->rkgh",
        weight_cache.reshape(single_count, kv_heads, group_size, page_count, page_width),
        page_values[:single_count],
        preferred_element_type=jnp.float32,
    )
    out_dec = (
        out_dec
        + weight_own.astype(jnp.float32)
        * new_values[:single_count].astype(jnp.float32)[:, :, None, :]
    )
    prompt_q = grouped[single_count:]
    prompt_rows = rows_all - single_count
    cache_pro = (
        jnp.einsum(
            "rkgh,mkph->rkgmp",
            prompt_q,
            page_keys[single_count],
            preferred_element_type=jnp.float32,
        ).reshape(prompt_rows, kv_heads, group_size, context)
        * inverse_root
    )
    seen_pro = (positions < spans[single_count])[None, None, None, :]
    new_pro = (
        jnp.einsum(
            "rkgh,mkh->rkgm", prompt_q, new_keys[single_count:], preferred_element_type=jnp.float32
        )
        * inverse_root
    )
    prompt_index = jnp.arange(prompt_rows, dtype=jnp.int32)
    causal = (prompt_index[:, None] >= prompt_index[None, :])[:, None, None, :]
    weight_cpro, weight_npro = normalize([(cache_pro, seen_pro), (new_pro, causal)])
    out_pro = jnp.einsum(
        "rkgmp,mkph->rkgh",
        weight_cpro.reshape(prompt_rows, kv_heads, group_size, page_count, page_width),
        page_values[single_count],
        preferred_element_type=jnp.float32,
    )
    out_pro = out_pro + jnp.einsum(
        "rkgm,mkh->rkgh", weight_npro, new_values[single_count:], preferred_element_type=jnp.float32
    )
    joined = jnp.concatenate([out_dec, out_pro], axis=0).astype(jnp.bfloat16)
    return joined.reshape(rows_all, head_count * head_width)


def slot_table(member, ranking, keeping, slot_count):
    slot_hit = (
        ranking[:, :, None, None] == jnp.arange(slot_count, dtype=jnp.int32)[None, None, None, :]
    )
    return ((member[..., None] > 0) & keeping[:, :, None, None] & slot_hit).astype(jnp.bfloat16)


def expert_pass(send, gating_matrices, expand_matrices, contract_matrices):
    specialist_index, slot_count, model_width = send.shape
    holders = lax.axis_size("expert")
    local_count = gating_matrices.shape[0]
    arrived = lax.all_to_all(
        send.reshape(holders, local_count, slot_count, model_width),
        "expert",
        split_axis=0,
        concat_axis=0,
        tiled=True,
    )
    row_piece = lax.all_gather(arrived, ("dp", "tensor"), axis=0, tiled=True)
    gate_part = jnp.einsum(
        "qesd,efd->qesf", row_piece, gating_matrices, preferred_element_type=jnp.float32
    )
    up_part = jnp.einsum(
        "qesd,efd->qesf", row_piece, expand_matrices, preferred_element_type=jnp.float32
    )
    hidden = (jax.nn.silu(gate_part) * up_part).astype(jnp.bfloat16)
    summed = lax.psum_scatter(
        jnp.einsum(
            "qesf,efd->qesd", hidden, contract_matrices, preferred_element_type=jnp.float32
        ).astype(jnp.bfloat16),
        ("dp", "tensor"),
        scatter_dimension=0,
        tiled=True,
    )
    arrived_back = lax.all_to_all(summed, "expert", split_axis=0, concat_axis=0, tiled=True)
    return arrived_back.reshape(specialist_index, slot_count, model_width)


def local(
    skip_stream_entry,
    question_vectors,
    fresh_lookup_vectors,
    fresh_content_vectors,
    stored_lookup_sheets,
    stored_content_sheets,
    sequence_sheet_map,
    stored_position_counts,
    attention_merge_matrix,
    premix_scale_factor,
    chosen_specialists,
    selection_shares,
    allowed_placements,
    favored_specialist,
    gating_matrices,
    expand_matrices,
    contract_matrices,
):
    token_count = chosen_specialists.shape[0]
    specialist_index = allowed_placements.shape[0]
    picked = (
        chosen_specialists[:, :, None]
        == jnp.arange(specialist_index, dtype=jnp.int32)[None, None, :]
    ).astype(jnp.int32)
    flat_routes = picked.reshape(token_count * 2, specialist_index)
    busiest_specialist = favored_specialist[0]
    before = (jnp.cumsum(flat_routes, axis=0) - flat_routes).reshape(
        token_count, 2, specialist_index
    )
    ranking = jnp.sum(before * picked, axis=2)
    placement_ceiling = jnp.where(
        jnp.arange(specialist_index, dtype=jnp.int32) == busiest_specialist,
        PLACEMENT_MOST,
        allowed_placements,
    )
    keeping = ranking < jnp.sum(picked * placement_ceiling[None, None, :], axis=2)
    row_total = question_vectors.shape[0]
    heads_out = attend(
        question_vectors.reshape(row_total, -1, HD),
        fresh_lookup_vectors.reshape(row_total, -1, HD),
        fresh_content_vectors.reshape(row_total, -1, HD),
        stored_lookup_sheets,
        stored_content_sheets,
        sequence_sheet_map,
        stored_position_counts,
    )
    total_attn = lax.psum(
        jnp.dot(heads_out, attention_merge_matrix, preferred_element_type=jnp.float32).astype(
            jnp.bfloat16
        ),
        "tensor",
    ).astype(jnp.float32)
    own_attn = lax.dynamic_slice_in_dim(
        total_attn, lax.axis_index("tensor") * token_count, token_count, 0
    )
    stream = (skip_stream_entry.astype(jnp.float32) + own_attn).astype(jnp.bfloat16)
    wide = stream.astype(jnp.float32)
    squares = jnp.mean(wide * wide, axis=1, keepdims=True)
    normed = (wide * lax.rsqrt(squares + 1e-05) * premix_scale_factor.astype(jnp.float32)).astype(
        jnp.bfloat16
    )
    main_slots = PLACEMENT_MOST
    table_main = slot_table(picked, ranking, keeping, main_slots)
    send = jnp.einsum(
        "nkes,nd->esd", table_main, normed, preferred_element_type=jnp.float32
    ).astype(jnp.bfloat16)
    expert_out = expert_pass(send, gating_matrices, expand_matrices, contract_matrices)
    chosen = jnp.einsum("nkes,esd->nkd", table_main, expert_out, preferred_element_type=jnp.float32)
    mixed = jnp.sum(selection_shares[:, :, None] * chosen, axis=1)
    return (wide + mixed).astype(jnp.bfloat16)


PAIRS_CORE = [(0, 1), (1, 0), (2, 3), (3, 2)]
PAIRS_Y = [(0, 2), (2, 0), (1, 3), (3, 1)]
PAIRS_X = [(0, 1), (1, 0)]
SINGLES = 16
PROMPT = 48
CAP_MOST = 3
NEG = -1e30
MIB = 1 << 20
EXPERTS_MIB = 43


def over_core(a):
    return lax.ppermute(a, "tensor", PAIRS_CORE)


def over_y(a):
    return lax.ppermute(a, "tensor", PAIRS_Y)


def over_x(a):
    return lax.ppermute(a, "expert", PAIRS_X)


def over_z(a, k):
    return lax.ppermute(a, "dp", [(i, i ^ k) for i in range(4)])


def dot_nt(a, b):
    return lax.dot_general(a, b, (((1,), (1,)), ((), ())), preferred_element_type=jnp.float32)


def dot_nn(a, b):
    return lax.dot_general(a, b, (((1,), (0,)), ((), ())), preferred_element_type=jnp.float32)


def note_routes(allowed, favored, chosen, shares, notes):
    experts, count = allowed.shape[0], chosen.shape[1]
    expert = lax.broadcasted_iota(jnp.int32, (experts, count), 0)
    picked = [jnp.where(chosen[k : k + 1, :] == expert, 1.0, 0.0) for k in range(2)]
    earlier = lax.broadcasted_iota(jnp.int32, (count, count), 0) < lax.broadcasted_iota(
        jnp.int32, (count, count), 1
    )
    before = dot_nn(
        (picked[0] + picked[1]).astype(jnp.bfloat16), jnp.where(earlier, 1.0, 0.0).astype(jnp.bfloat16)
    )
    limit = jnp.zeros((experts, count), jnp.int32)
    for e in range(experts):
        limit = jnp.where(expert == e, allowed[e], limit)
    limit = jnp.where(expert == favored[0], PLACEMENT_MOST, limit).astype(jnp.float32)
    rest = picked[0] * shares[0:1, :] + picked[1] * shares[1:2, :]
    rest = jnp.where(before < limit, rest, 0.0)
    parts = []
    for _ in range(3):
        part = rest.astype(jnp.bfloat16).astype(jnp.float32)
        parts.append(part)
        rest = rest - part
    parts.append(jnp.zeros((128 - 3 * experts, count), jnp.float32))
    parts = jnp.concatenate(parts, axis=0)
    parts = jnp.concatenate([parts, jnp.zeros((128, 128 - count), jnp.float32)], axis=1)
    notes[...] = parts.T[0:count, :]


def attend_kernel(
    place, table, counts, allowed, favored, chosen, shares, q_hbm, k_new_hbm, v_new_hbm, k_hbm, v_hbm, w_hbm,
    send, keep, notes,
    q, k_new, v_new, k_pool, v_pool, w_out, scores, times, weights, k_prompt, v_prompt, heads, ordered, sems,
):
    pool_rows = k_pool.shape[0]
    pages = pool_rows // 128
    slots = table.shape[0]
    group = q.shape[1] // HD
    pairs = [(q_hbm, q), (k_new_hbm, k_new)]
    for source, target, parts in ((k_hbm, k_pool, 2), (v_hbm, v_pool, 2), (w_hbm, w_out, 4)):
        rows = source.shape[0] // parts
        for i in range(parts):
            pairs.append((source.at[i * rows : (i + 1) * rows, :], target.at[i * rows : (i + 1) * rows, :]))
    pairs.insert(4, (v_new_hbm, v_new))
    copies = [pltpu.make_async_copy(src, dst, sems.at[i]) for i, (src, dst) in enumerate(pairs)]
    for copy in copies:
        copy.start()
    note_routes(allowed, favored, chosen, shares, notes)
    root = 1.0 / math.sqrt(HD)

    lane = lax.broadcasted_iota(jnp.int32, (SINGLES, 128), 1)
    request = lax.broadcasted_iota(jnp.int32, (SINGLES, 128), 0)
    spans = jnp.zeros((SINGLES, 128), jnp.int32)
    named = [spans] * slots
    for r in range(SINGLES):
        here = request == r
        spans = jnp.where(here, counts[r], spans)
        named = [jnp.where(here, table[m, r], named[m]) for m in range(slots)]
    seen = [jnp.where(lane + m * 128 < spans, 1.0, 0.0) for m in range(slots)]
    for page in range(pages):
        total = jnp.zeros((SINGLES, 128), jnp.float32)
        for m in range(slots):
            total = total + jnp.where(named[m] == page, seen[m], 0.0)
        times[:, page * 128 : (page + 1) * 128] = total

    for copy in copies[:4]:
        copy.wait()
    q_single = jnp.concatenate([q[0:SINGLES, h * HD : (h + 1) * HD] for h in range(group)], axis=0)
    q_prompt = jnp.concatenate([q[SINGLES:, h * HD : (h + 1) * HD] for h in range(group)], axis=0)
    step = 1024
    for start in range(0, pool_rows, step):
        scores[:, start : start + step] = dot_nt(q_single, k_pool[start : start + step, :])
    for m in range(slots):
        page = table[m, SINGLES]
        k_prompt[m * 128 : (m + 1) * 128, :] = k_pool[pl.ds(pl.multiple_of(page * 128, 128), 128), :]
    s_cache = dot_nt(q_prompt, k_prompt[...]) * root
    s_new = dot_nt(q_prompt, k_new[SINGLES:, :]) * root
    own = k_new[0:SINGLES, :].astype(jnp.float32)

    denominators, own_parts = [], []
    for h in range(group):
        rows = slice(h * SINGLES, (h + 1) * SINGLES)
        often = times[...]
        s = jnp.where(often > 0.0, scores[rows, :] * root, NEG)
        s_own = (
            jnp.sum(q_single[rows, :].astype(jnp.float32) * own, axis=1, keepdims=True) * root
        )
        highest = jnp.maximum(jnp.max(s, axis=1, keepdims=True), s_own)
        p = jnp.exp(s - highest) * often
        p_own = jnp.exp(s_own - highest)
        denominators.append(jnp.sum(p, axis=1, keepdims=True) + p_own)
        own_parts.append(p_own)
        weights[rows, :] = p.astype(jnp.bfloat16)

    position = lax.broadcasted_iota(jnp.int32, s_cache.shape, 1)
    s_cache = jnp.where(position < counts[SINGLES], s_cache, NEG)
    row = lax.broadcasted_iota(jnp.int32, (PROMPT, PROMPT), 0)
    col = lax.broadcasted_iota(jnp.int32, (PROMPT, PROMPT), 1)
    causal = jnp.concatenate([jnp.where(row >= col, 0.0, NEG)] * group, axis=0)
    s_new = s_new + causal
    highest = jnp.maximum(
        jnp.max(s_cache, axis=1, keepdims=True), jnp.max(s_new, axis=1, keepdims=True)
    )
    p_cache = jnp.exp(s_cache - highest)
    p_new = jnp.exp(s_new - highest)
    denominator = jnp.sum(p_cache, axis=1, keepdims=True) + jnp.sum(p_new, axis=1, keepdims=True)

    for copy in copies[4:7]:
        copy.wait()
    for m in range(slots):
        page = table[m, SINGLES]
        v_prompt[m * 128 : (m + 1) * 128, :] = v_pool[pl.ds(pl.multiple_of(page * 128, 128), 128), :]
    out_prompt = dot_nn(p_cache.astype(jnp.bfloat16), v_prompt[...])
    out_prompt = out_prompt + dot_nn(p_new.astype(jnp.bfloat16), v_new[SINGLES:, :])
    out_prompt = (out_prompt / denominator).astype(jnp.bfloat16)
    out_single = dot_nn(weights[...], v_pool[...])
    fresh = v_new[0:SINGLES, :].astype(jnp.float32)
    for h in range(group):
        lanes = slice(h * HD, (h + 1) * HD)
        one = out_single[h * SINGLES : (h + 1) * SINGLES, :] + own_parts[h] * fresh
        heads[0:SINGLES, lanes] = (one / denominators[h]).astype(jnp.bfloat16)
        heads[SINGLES:, lanes] = out_prompt[h * PROMPT : (h + 1) * PROMPT, :]

    t = place[0]
    core, y = lax.rem(t, 2), lax.div(t, 2)
    order = [(1 - y) * 2 + 1 - core, y * 2 + 1 - core, (1 - y) * 2 + core, y * 2 + core]
    for i, block in enumerate(order):
        ordered[i * 16 : (i + 1) * 16, :] = heads[pl.ds(pl.multiple_of(block * 16, 16), 16), :]
    for copy in copies[7:]:
        copy.wait()
    for start in range(0, w_out.shape[1], 512):
        part = dot_nn(ordered[...], w_out[:, start : start + 512]).astype(jnp.bfloat16)
        send[:, start : start + 512] = part[0:32, :]
        keep[:, start : start + 512] = part[32:64, :]


def attention_call(place, table, counts, allowed, favored, chosen, shares, q, k_new, v_new, k_pool, v_pool, w_out):
    pool_rows, rows, width = k_pool.shape[0], q.shape[0], w_out.shape[1]
    vmem, smem, hbm = (pl.BlockSpec(memory_space=s) for s in (pltpu.VMEM, pltpu.SMEM, pl.ANY))
    half = jax.ShapeDtypeStruct((rows // 2, width), jnp.bfloat16)
    singles = SINGLES * (q.shape[1] // HD)
    return pl.pallas_call(
        attend_kernel,
        out_shape=(half, half, jax.ShapeDtypeStruct((chosen.shape[1], 128), jnp.float32)),
        in_specs=[smem] * 5 + [vmem] * 2 + [hbm] * 6,
        out_specs=(vmem,) * 3,
        scratch_shapes=[
            pltpu.VMEM(q.shape, jnp.bfloat16),
            pltpu.VMEM(k_new.shape, jnp.bfloat16),
            pltpu.VMEM(v_new.shape, jnp.bfloat16),
            pltpu.VMEM((pool_rows, HD), jnp.bfloat16),
            pltpu.VMEM((pool_rows, HD), jnp.bfloat16),
            pltpu.VMEM(w_out.shape, jnp.bfloat16),
            pltpu.VMEM((singles, pool_rows), jnp.float32),
            pltpu.VMEM((SINGLES, pool_rows), jnp.float32),
            pltpu.VMEM((singles, pool_rows), jnp.bfloat16),
            pltpu.VMEM((table.shape[0] * 128, HD), jnp.bfloat16),
            pltpu.VMEM((table.shape[0] * 128, HD), jnp.bfloat16),
            pltpu.VMEM((rows, q.shape[1]), jnp.bfloat16),
            pltpu.VMEM((rows, q.shape[1]), jnp.bfloat16),
            pltpu.SemaphoreType.DMA((11,)),
        ],
        compiler_params=pltpu.CompilerParams(vmem_limit_bytes=60 * MIB),
        cost_estimate=pl.CostEstimate(flops=10**9, bytes_accessed=8 * 10**6, transcendentals=6 * 10**5),
        name="attention",
    )(place, table, counts, allowed, favored, chosen, shares, q, k_new, v_new, k_pool, v_pool, w_out)


def slot_spans(tile):
    return [(0, 2 * tile), (2 * tile, tile), (3 * tile, tile), (4 * tile, tile)]


def experts_kernel(
    place, favored, a0, a1, a2, a3, b0, b1, b2, b3, gate, up, down,
    a_keep_near, a_keep_far, a_send_near, a_send_far, b_keep_near, b_keep_far, b_send_near, b_send_far,
    tokens, ring, pick, spread, scale, taken, act, in_sems, w_sems,
):
    count, hidden = tokens.shape[0], act.shape[1]
    half = a_keep_near.shape[1]
    notes_at = half
    tile = taken.shape[0] // 5
    spans = slot_spans(tile)
    first = jnp.maximum(favored[0], 0)
    expert_of = [first] + [jnp.where(s - 1 < first, s - 1, s) for s in (1, 2, 3)]

    loads = []
    for i, ref in enumerate((a0, a1, a2, a3)):
        loads.append((ref, tokens.at[i * 128 : (i + 1) * 128, 0 : half + 128]))
    for i, ref in enumerate((b0, b1, b2, b3)):
        for j in range(2):
            row = (i // 2) * 256 + j * 128 + (i % 2) * 64
            loads.append((ref.at[j * 64 : (j + 1) * 64, :], tokens.at[row : row + 64, half + 128 :]))
    loads = [pltpu.make_async_copy(src, dst, in_sems.at[i]) for i, (src, dst) in enumerate(loads)]
    for load in loads:
        load.start()

    def fetch(matrix, s, slot):
        rows = ring.at[slot * hidden : (slot + 1) * hidden, :]
        return pltpu.make_async_copy(matrix.at[expert_of[s]], rows, w_sems.at[slot])

    def fetch_inner(s):
        fetch(gate, s, 2 * s).start()
        fetch(up, s, 2 * s + 1).start()

    for load in loads[:4]:
        load.wait()
    fetch_inner(0)
    notes = tokens[:, notes_at : notes_at + 128]
    width = notes.shape[1]
    source = lax.broadcasted_iota(jnp.int32, (width, width), 0)
    target = lax.broadcasted_iota(jnp.int32, (width, width), 1)
    expert = jnp.where(target == 0, first, jnp.where(target - 1 < first, target - 1, target))
    wanted = (source < 24) & (target < 4) & (lax.rem(source, 8) == place[0] * 4 + expert)
    share = dot_nn(notes, jnp.where(wanted, 1.0, 0.0).astype(jnp.bfloat16))
    kept = jnp.where(share > 0.0, 1.0, 0.0)
    below = lax.broadcasted_iota(jnp.int32, (count, count), 1) < lax.broadcasted_iota(
        jnp.int32, (count, count), 0
    )
    rank = dot_nn(jnp.where(below, 1.0, 0.0).astype(jnp.bfloat16), kept.astype(jnp.bfloat16))
    spot = jnp.where(kept > 0.0, rank, -1000.0)
    spot_t = spot.T
    lane = lax.broadcasted_iota(jnp.int32, (1, width), 1)
    for s, (row, rows) in enumerate(spans):
        ids = lax.broadcasted_iota(jnp.int32, (rows, count), 0).astype(jnp.float32)
        picked = jnp.where(ids == spot_t[s : s + 1, :], 1.0, 0.0).astype(jnp.bfloat16)
        pick[row : row + rows, :] = picked
        found = dot_nn(picked, notes)
        mine = (lane < 24) & (lax.rem(lane, 8) == place[0] * 4 + expert_of[s])
        part = jnp.sum(jnp.where(mine, found, 0.0), axis=1, keepdims=True)
        scale[row : row + rows, :] = jnp.broadcast_to(part, (rows, width))
    for block in range(spread.shape[1] // 128):
        ids = (lax.broadcasted_iota(jnp.int32, (count, 128), 1) + block * 128).astype(jnp.float32)
        total = jnp.zeros((count, 128), jnp.float32)
        for s, (row, rows) in enumerate(spans):
            if row < (block + 1) * 128 and row + rows > block * 128:
                total = total + jnp.where(ids == spot[:, s : s + 1] + row, 1.0, 0.0)
        spread[:, block * 128 : (block + 1) * 128] = total.astype(jnp.bfloat16)
    fetch_inner(1)
    for load in loads[4:]:
        load.wait()

    for start in range(0, 2 * half, 512):
        at = start if start < half else start + 128
        taken[:, start : start + 512] = dot_nn(pick[...], tokens[:, at : at + 512]).astype(jnp.bfloat16)

    fetch_inner(2)
    made = tokens
    made[5 * tile :, :] = jnp.zeros_like(made[5 * tile :, :])
    for s, (row, rows) in enumerate(spans):
        x = taken[row : row + rows, :]
        fetch(gate, s, 2 * s).wait()
        g = dot_nt(x, ring[2 * s * hidden : (2 * s + 1) * hidden, :])
        fetch(up, s, 2 * s + 1).wait()
        u = dot_nt(x, ring[(2 * s + 1) * hidden : (2 * s + 2) * hidden, :])
        act[row : row + rows, :] = (g / (1.0 + jnp.exp(-g)) * u).astype(jnp.bfloat16)
        if s == 0:
            fetch_inner(3)
        for later in ((), (0,), (1, 2), (3,))[s]:
            fetch(down, later, 2 * later).start()

    for s, (row, rows) in enumerate(spans):
        fetch(down, s, 2 * s).wait()
        part = scale[row : row + rows, 0:1]
        for start in range(0, 2 * half, 1024):
            o = dot_nn(act[row : row + rows, :], ring[2 * s * hidden : (2 * s + 1) * hidden, start : start + 1024])
            made[row : row + rows, start : start + 1024] = (o * part).astype(jnp.bfloat16)

    outs_a = (a_keep_near, a_keep_far, a_send_near, a_send_far)
    outs_b = (b_keep_near, b_keep_far, b_send_near, b_send_far)
    for i, outs in enumerate((outs_a, outs_b)):
        for at in range(0, half, 512):
            y = dot_nn(spread[...], made[:, i * half + at : i * half + at + 512]).astype(jnp.bfloat16)
            for j in range(8):
                to = j if i == 0 else j // 4 * 4 + j % 2 * 2 + j // 2 % 2
                rows = slice(to % 2 * 64, to % 2 * 64 + 64)
                outs[to // 2][rows, at : at + 512] = y[j * 64 : (j + 1) * 64, :]


def experts_call(place, favored, pieces_a, pieces_b, gate, up, down):
    _, hidden, width = gate.shape
    count = sum(piece.shape[0] for piece in pieces_a)
    tile = CAP_MOST * 32
    rows, padded = 5 * tile, -(-5 * tile // 128) * 128
    half = width // 2
    smem, vmem, hbm = (pl.BlockSpec(memory_space=s) for s in (pltpu.SMEM, pltpu.VMEM, pl.ANY))
    out = jax.ShapeDtypeStruct((count // 4, half), jnp.bfloat16)
    return pl.pallas_call(
        experts_kernel,
        out_shape=(out,) * 8,
        in_specs=[smem, smem] + [hbm] * 11,
        out_specs=(vmem,) * 8,
        scratch_shapes=[
            pltpu.VMEM((count, width + 128), jnp.bfloat16),
            pltpu.VMEM((8 * hidden, width), jnp.bfloat16),
            pltpu.VMEM((rows, count), jnp.bfloat16),
            pltpu.VMEM((count, padded), jnp.bfloat16),
            pltpu.VMEM((rows, 128), jnp.float32),
            pltpu.VMEM((rows, width), jnp.bfloat16),
            pltpu.VMEM((rows, hidden), jnp.bfloat16),
            pltpu.SemaphoreType.DMA((12,)),
            pltpu.SemaphoreType.DMA((8,)),
        ],
        compiler_params=pltpu.CompilerParams(vmem_limit_bytes=EXPERTS_MIB * MIB),
        cost_estimate=pl.CostEstimate(
            flops=6 * rows * hidden * width, bytes_accessed=24 * hidden * width, transcendentals=rows * hidden
        ),
        name="experts",
    )(place, favored, *pieces_a, *pieces_b, gate, up, down)


def joined(*parts):
    return jnp.concatenate(parts, axis=0)


def plus(a, b):
    return (a.astype(jnp.float32) + b.astype(jnp.float32)).astype(jnp.bfloat16)


def local_fast(
    skip_stream_entry,
    question_vectors,
    fresh_lookup_vectors,
    fresh_content_vectors,
    stored_lookup_sheets,
    stored_content_sheets,
    sequence_sheet_map,
    stored_position_counts,
    attention_merge_matrix,
    premix_scale_factor,
    chosen_specialists,
    selection_shares,
    allowed_placements,
    favored_specialist,
    gating_matrices,
    expand_matrices,
    contract_matrices,
):
    width = skip_stream_entry.shape[1]
    half = width // 2
    own_experts = gating_matrices.shape[0]
    count = chosen_specialists.shape[0]
    x, t = lax.axis_index("expert"), lax.axis_index("tensor")

    send, keep, notes = attention_call(
        t.astype(jnp.int32)[None],
        sequence_sheet_map.T,
        stored_position_counts,
        allowed_placements,
        favored_specialist,
        chosen_specialists.T,
        selection_shares.T,
        question_vectors,
        fresh_lookup_vectors,
        fresh_content_vectors,
        stored_lookup_sheets.reshape(-1, HD),
        stored_content_sheets.reshape(-1, HD),
        attention_merge_matrix,
    )
    got = over_core(send)
    keep, notes = lax.optimization_barrier((keep.astype(jnp.float32), notes.astype(jnp.bfloat16)))
    skip = lax.optimization_barrier(skip_stream_entry.astype(jnp.float32))
    far = plus(got[0:count], keep[0:count])
    near = plus(got[count:], keep[count:])
    own_attn = over_y(far).astype(jnp.float32) + near.astype(jnp.float32)
    stream = (skip + own_attn).astype(jnp.bfloat16)
    wide = stream.astype(jnp.float32)
    squares = jnp.mean(wide * wide, axis=1, keepdims=True)
    normed = (wide * lax.rsqrt(squares + 1e-05) * premix_scale_factor.astype(jnp.float32)).astype(
        jnp.bfloat16
    )

    hot = favored_specialist - x * own_experts
    hot = jnp.where((hot >= 0) & (hot < own_experts), hot, -1).astype(jnp.int32)

    part = jnp.concatenate([normed[:, :half], notes, normed[:, half:]], axis=1)
    third, second, first = over_z(part, 3), over_z(part, 2), over_z(part, 1)
    column = [part, first, second, third]
    gathered = []
    for lanes, first, second in (
        (slice(0, half + 128), over_x, over_y),
        (slice(half + 128, None), over_y, over_x),
    ):
        part = joined(*[rows[:, lanes] for rows in column])
        part = joined(part, first(part))
        other = second(part)
        gathered.append((part, other, over_core(part), over_core(other)))
    outs = experts_call(
        x.astype(jnp.int32)[None], hot, *gathered, gating_matrices, expand_matrices, contract_matrices
    )
    results = []
    for (keep_near, keep_far, send_near, send_far), first, second in (
        (outs[:4], over_y, over_x),
        (outs[4:], over_x, over_y),
    ):
        far = first(plus(over_core(send_far), keep_far))
        near = plus(over_core(send_near), keep_near)
        rows = near.shape[0] // 2
        got = second(plus(far[rows:], near[rows:]))
        results.append(plus(far[:rows], near[:rows]).astype(jnp.float32) + got.astype(jnp.float32))
    total_a, total_b = results
    sent = jnp.concatenate([total_b[count : 2 * count], total_b[3 * count :]], axis=0).astype(jnp.bfloat16)
    got = over_z(sent, 1).astype(jnp.float32)
    out_a = total_a[0:count]
    for k in (1, 2, 3):
        mine = total_a[k * count : (k + 1) * count].astype(jnp.bfloat16)
        out_a = out_a + over_z(mine, k).astype(jnp.float32)
    far = (total_b[2 * count : 3 * count] + got[count:]).astype(jnp.bfloat16)
    out_b = total_b[0:count] + got[0:count] + over_z(far, 2).astype(jnp.float32)
    return (wide + jnp.concatenate([out_a, out_b], axis=1)).astype(jnp.bfloat16)


def solution(mesh):
    placed = (
        P(("dp", "expert", "tensor"), None),
        P(("dp", "expert"), "tensor"),
        P(("dp", "expert"), "tensor"),
        P(("dp", "expert"), "tensor"),
        P(("dp", "expert"), "tensor", None, None),
        P(("dp", "expert"), "tensor", None, None),
        P(("dp", "expert"), None),
        P(("dp", "expert")),
        P("tensor", None),
        P(),
        P(("dp", "expert", "tensor"), None),
        P(("dp", "expert", "tensor"), None),
        P(),
        P(),
        P("expert", ("dp", "tensor"), None),
        P("expert", ("dp", "tensor"), None),
        P("expert", ("dp", "tensor"), None),
    )
    sizes = tuple(mesh.shape[name] for name in ("dp", "expert", "tensor"))
    return jax.shard_map(
        local_fast if sizes == (4, 2, 4) else local,
        mesh=mesh,
        in_specs=placed,
        out_specs=P(("dp", "expert", "tensor"), None),
        check_vma=False,
    )
```

```python
from functools import reduce
import math

import jax
import jax.numpy as jnp
from jax import lax
from jax.experimental import pallas as pl
from jax.experimental.pallas import tpu as pltpu
from jax.sharding import PartitionSpec as P

HD = 128
PLACEMENT_MOST = 6


def normalize(parts):
    highest = reduce(
        jnp.maximum,
        [
            jnp.max(jnp.where(visible, scores, -jnp.inf), axis=-1, keepdims=True)
            for scores, visible in parts
        ],
    )
    portions = [jnp.where(visible, jnp.exp(scores - highest), 0.0) for scores, visible in parts]
    denominator = reduce(
        jnp.add, [jnp.sum(portion, axis=-1, keepdims=True) for portion in portions]
    )
    return [(portion / denominator).astype(jnp.bfloat16) for portion in portions]


def attend(question_vectors, new_keys, new_values, key_pages, value_pages, table, spans):
    rows_all, head_count, head_width = question_vectors.shape
    kv_heads = new_keys.shape[1]
    group_size = head_count // kv_heads
    single_count = spans.shape[0] - 1
    page_count = table.shape[1]
    page_width = key_pages.shape[2]
    context = page_count * page_width
    inverse_root = 1.0 / math.sqrt(head_width)
    page_keys = key_pages[table]
    page_values = value_pages[table]
    grouped = question_vectors.reshape(rows_all, kv_heads, group_size, head_width)
    positions = jnp.arange(context, dtype=jnp.int32)
    single_q = grouped[:single_count]
    cache_dec = (
        jnp.einsum(
            "rkgh,rmkph->rkgmp",
            single_q,
            page_keys[:single_count],
            preferred_element_type=jnp.float32,
        ).reshape(single_count, kv_heads, group_size, context)
        * inverse_root
    )
    seen_dec = (positions[None, :] < spans[:single_count, None])[:, None, None, :]
    own_dec = (
        jnp.einsum(
            "rkgh,rkh->rkg", single_q, new_keys[:single_count], preferred_element_type=jnp.float32
        )[..., None]
        * inverse_root
    )
    weight_cache, weight_own = normalize(
        [(cache_dec, seen_dec), (own_dec, jnp.full(own_dec.shape, True))]
    )
    out_dec = jnp.einsum(
        "rkgmp,rmkph->rkgh",
        weight_cache.reshape(single_count, kv_heads, group_size, page_count, page_width),
        page_values[:single_count],
        preferred_element_type=jnp.float32,
    )
    out_dec = (
        out_dec
        + weight_own.astype(jnp.float32)
        * new_values[:single_count].astype(jnp.float32)[:, :, None, :]
    )
    prompt_q = grouped[single_count:]
    prompt_rows = rows_all - single_count
    cache_pro = (
        jnp.einsum(
            "rkgh,mkph->rkgmp",
            prompt_q,
            page_keys[single_count],
            preferred_element_type=jnp.float32,
        ).reshape(prompt_rows, kv_heads, group_size, context)
        * inverse_root
    )
    seen_pro = (positions < spans[single_count])[None, None, None, :]
    new_pro = (
        jnp.einsum(
            "rkgh,mkh->rkgm", prompt_q, new_keys[single_count:], preferred_element_type=jnp.float32
        )
        * inverse_root
    )
    prompt_index = jnp.arange(prompt_rows, dtype=jnp.int32)
    causal = (prompt_index[:, None] >= prompt_index[None, :])[:, None, None, :]
    weight_cpro, weight_npro = normalize([(cache_pro, seen_pro), (new_pro, causal)])
    out_pro = jnp.einsum(
        "rkgmp,mkph->rkgh",
        weight_cpro.reshape(prompt_rows, kv_heads, group_size, page_count, page_width),
        page_values[single_count],
        preferred_element_type=jnp.float32,
    )
    out_pro = out_pro + jnp.einsum(
        "rkgm,mkh->rkgh", weight_npro, new_values[single_count:], preferred_element_type=jnp.float32
    )
    joined = jnp.concatenate([out_dec, out_pro], axis=0).astype(jnp.bfloat16)
    return joined.reshape(rows_all, head_count * head_width)


def slot_table(member, ranking, keeping, slot_count):
    slot_hit = (
        ranking[:, :, None, None] == jnp.arange(slot_count, dtype=jnp.int32)[None, None, None, :]
    )
    return ((member[..., None] > 0) & keeping[:, :, None, None] & slot_hit).astype(jnp.bfloat16)


def expert_pass(send, gating_matrices, expand_matrices, contract_matrices):
    specialist_index, slot_count, model_width = send.shape
    holders = lax.axis_size("expert")
    local_count = gating_matrices.shape[0]
    arrived = lax.all_to_all(
        send.reshape(holders, local_count, slot_count, model_width),
        "expert",
        split_axis=0,
        concat_axis=0,
        tiled=True,
    )
    row_piece = lax.all_gather(arrived, ("dp", "tensor"), axis=0, tiled=True)
    gate_part = jnp.einsum(
        "qesd,efd->qesf", row_piece, gating_matrices, preferred_element_type=jnp.float32
    )
    up_part = jnp.einsum(
        "qesd,efd->qesf", row_piece, expand_matrices, preferred_element_type=jnp.float32
    )
    hidden = (jax.nn.silu(gate_part) * up_part).astype(jnp.bfloat16)
    summed = lax.psum_scatter(
        jnp.einsum(
            "qesf,efd->qesd", hidden, contract_matrices, preferred_element_type=jnp.float32
        ).astype(jnp.bfloat16),
        ("dp", "tensor"),
        scatter_dimension=0,
        tiled=True,
    )
    arrived_back = lax.all_to_all(summed, "expert", split_axis=0, concat_axis=0, tiled=True)
    return arrived_back.reshape(specialist_index, slot_count, model_width)


def local(
    skip_stream_entry,
    question_vectors,
    fresh_lookup_vectors,
    fresh_content_vectors,
    stored_lookup_sheets,
    stored_content_sheets,
    sequence_sheet_map,
    stored_position_counts,
    attention_merge_matrix,
    premix_scale_factor,
    chosen_specialists,
    selection_shares,
    allowed_placements,
    favored_specialist,
    gating_matrices,
    expand_matrices,
    contract_matrices,
):
    token_count = chosen_specialists.shape[0]
    specialist_index = allowed_placements.shape[0]
    picked = (
        chosen_specialists[:, :, None]
        == jnp.arange(specialist_index, dtype=jnp.int32)[None, None, :]
    ).astype(jnp.int32)
    flat_routes = picked.reshape(token_count * 2, specialist_index)
    busiest_specialist = favored_specialist[0]
    before = (jnp.cumsum(flat_routes, axis=0) - flat_routes).reshape(
        token_count, 2, specialist_index
    )
    ranking = jnp.sum(before * picked, axis=2)
    placement_ceiling = jnp.where(
        jnp.arange(specialist_index, dtype=jnp.int32) == busiest_specialist,
        PLACEMENT_MOST,
        allowed_placements,
    )
    keeping = ranking < jnp.sum(picked * placement_ceiling[None, None, :], axis=2)
    row_total = question_vectors.shape[0]
    heads_out = attend(
        question_vectors.reshape(row_total, -1, HD),
        fresh_lookup_vectors.reshape(row_total, -1, HD),
        fresh_content_vectors.reshape(row_total, -1, HD),
        stored_lookup_sheets,
        stored_content_sheets,
        sequence_sheet_map,
        stored_position_counts,
    )
    total_attn = lax.psum(
        jnp.dot(heads_out, attention_merge_matrix, preferred_element_type=jnp.float32).astype(
            jnp.bfloat16
        ),
        "tensor",
    ).astype(jnp.float32)
    own_attn = lax.dynamic_slice_in_dim(
        total_attn, lax.axis_index("tensor") * token_count, token_count, 0
    )
    stream = (skip_stream_entry.astype(jnp.float32) + own_attn).astype(jnp.bfloat16)
    wide = stream.astype(jnp.float32)
    squares = jnp.mean(wide * wide, axis=1, keepdims=True)
    normed = (wide * lax.rsqrt(squares + 1e-05) * premix_scale_factor.astype(jnp.float32)).astype(
        jnp.bfloat16
    )
    main_slots = PLACEMENT_MOST
    table_main = slot_table(picked, ranking, keeping, main_slots)
    send = jnp.einsum(
        "nkes,nd->esd", table_main, normed, preferred_element_type=jnp.float32
    ).astype(jnp.bfloat16)
    expert_out = expert_pass(send, gating_matrices, expand_matrices, contract_matrices)
    chosen = jnp.einsum("nkes,esd->nkd", table_main, expert_out, preferred_element_type=jnp.float32)
    mixed = jnp.sum(selection_shares[:, :, None] * chosen, axis=1)
    return (wide + mixed).astype(jnp.bfloat16)


PAIRS_CORE = [(0, 1), (1, 0), (2, 3), (3, 2)]
PAIRS_Y = [(0, 2), (2, 0), (1, 3), (3, 1)]
PAIRS_X = [(0, 1), (1, 0)]
SINGLES = 16
PROMPT = 48
CAP_MOST = 3
NEG = -1e30
MIB = 1 << 20
EXPERTS_MIB = 43


def over_core(a):
    return lax.ppermute(a, "tensor", PAIRS_CORE)


def over_y(a):
    return lax.ppermute(a, "tensor", PAIRS_Y)


def over_x(a):
    return lax.ppermute(a, "expert", PAIRS_X)


def over_z(a, k):
    return lax.ppermute(a, "dp", [(i, i ^ k) for i in range(4)])


def dot_nt(a, b):
    return lax.dot_general(a, b, (((1,), (1,)), ((), ())), preferred_element_type=jnp.float32)


def dot_nn(a, b):
    return lax.dot_general(a, b, (((1,), (0,)), ((), ())), preferred_element_type=jnp.float32)


def note_routes(allowed, favored, chosen, shares, notes):
    experts, count = allowed.shape[0], chosen.shape[1]
    expert = lax.broadcasted_iota(jnp.int32, (experts, count), 0)
    picked = [jnp.where(chosen[k : k + 1, :] == expert, 1.0, 0.0) for k in range(2)]
    earlier = lax.broadcasted_iota(jnp.int32, (count, count), 0) < lax.broadcasted_iota(
        jnp.int32, (count, count), 1
    )
    before = dot_nn(
        (picked[0] + picked[1]).astype(jnp.bfloat16), jnp.where(earlier, 1.0, 0.0).astype(jnp.bfloat16)
    )
    limit = jnp.zeros((experts, count), jnp.int32)
    for e in range(experts):
        limit = jnp.where(expert == e, allowed[e], limit)
    limit = jnp.where(expert == favored[0], PLACEMENT_MOST, limit).astype(jnp.float32)
    rest = picked[0] * shares[0:1, :] + picked[1] * shares[1:2, :]
    rest = jnp.where(before < limit, rest, 0.0)
    parts = []
    for _ in range(3):
        part = rest.astype(jnp.bfloat16).astype(jnp.float32)
        parts.append(part)
        rest = rest - part
    parts.append(jnp.zeros((128 - 3 * experts, count), jnp.float32))
    parts = jnp.concatenate(parts, axis=0)
    parts = jnp.concatenate([parts, jnp.zeros((128, 128 - count), jnp.float32)], axis=1)
    notes[...] = parts.T[0:count, :]


def attend_kernel(
    place, table, counts, allowed, favored, chosen, shares, q_hbm, k_new_hbm, v_new_hbm, k_hbm, v_hbm, w_hbm,
    send, keep, notes,
    q, k_new, v_new, k_pool, v_pool, w_out, scores, times, weights, k_prompt, v_prompt, heads, ordered, sems,
):
    pool_rows = k_pool.shape[0]
    pages = pool_rows // 128
    slots = table.shape[0]
    group = q.shape[1] // HD
    pairs = [(q_hbm, q), (k_new_hbm, k_new)]
    for source, target, parts in ((k_hbm, k_pool, 2), (v_hbm, v_pool, 2), (w_hbm, w_out, 4)):
        rows = source.shape[0] // parts
        for i in range(parts):
            pairs.append((source.at[i * rows : (i + 1) * rows, :], target.at[i * rows : (i + 1) * rows, :]))
    pairs.insert(4, (v_new_hbm, v_new))
    copies = [pltpu.make_async_copy(src, dst, sems.at[i]) for i, (src, dst) in enumerate(pairs)]
    for copy in copies:
        copy.start()
    note_routes(allowed, favored, chosen, shares, notes)
    root = 1.0 / math.sqrt(HD)

    lane = lax.broadcasted_iota(jnp.int32, (SINGLES, 128), 1)
    request = lax.broadcasted_iota(jnp.int32, (SINGLES, 128), 0)
    spans = jnp.zeros((SINGLES, 128), jnp.int32)
    named = [spans] * slots
    for r in range(SINGLES):
        here = request == r
        spans = jnp.where(here, counts[r], spans)
        named = [jnp.where(here, table[m, r], named[m]) for m in range(slots)]
    seen = [jnp.where(lane + m * 128 < spans, 1.0, 0.0) for m in range(slots)]
    for page in range(pages):
        total = jnp.zeros((SINGLES, 128), jnp.float32)
        for m in range(slots):
            total = total + jnp.where(named[m] == page, seen[m], 0.0)
        times[:, page * 128 : (page + 1) * 128] = total

    for copy in copies[:4]:
        copy.wait()
    q_single = jnp.concatenate([q[0:SINGLES, h * HD : (h + 1) * HD] for h in range(group)], axis=0)
    q_prompt = jnp.concatenate([q[SINGLES:, h * HD : (h + 1) * HD] for h in range(group)], axis=0)
    step = 1024
    for start in range(0, pool_rows, step):
        scores[:, start : start + step] = dot_nt(q_single, k_pool[start : start + step, :])
    for m in range(slots):
        page = table[m, SINGLES]
        k_prompt[m * 128 : (m + 1) * 128, :] = k_pool[pl.ds(pl.multiple_of(page * 128, 128), 128), :]
    s_cache = dot_nt(q_prompt, k_prompt[...]) * root
    s_new = dot_nt(q_prompt, k_new[SINGLES:, :]) * root
    own = k_new[0:SINGLES, :].astype(jnp.float32)

    denominators, own_parts = [], []
    for h in range(group):
        rows = slice(h * SINGLES, (h + 1) * SINGLES)
        often = times[...]
        s = jnp.where(often > 0.0, scores[rows, :] * root, NEG)
        s_own = (
            jnp.sum(q_single[rows, :].astype(jnp.float32) * own, axis=1, keepdims=True) * root
        )
        highest = jnp.maximum(jnp.max(s, axis=1, keepdims=True), s_own)
        p = jnp.exp(s - highest) * often
        p_own = jnp.exp(s_own - highest)
        denominators.append(jnp.sum(p, axis=1, keepdims=True) + p_own)
        own_parts.append(p_own)
        weights[rows, :] = p.astype(jnp.bfloat16)

    position = lax.broadcasted_iota(jnp.int32, s_cache.shape, 1)
    s_cache = jnp.where(position < counts[SINGLES], s_cache, NEG)
    row = lax.broadcasted_iota(jnp.int32, (PROMPT, PROMPT), 0)
    col = lax.broadcasted_iota(jnp.int32, (PROMPT, PROMPT), 1)
    causal = jnp.concatenate([jnp.where(row >= col, 0.0, NEG)] * group, axis=0)
    s_new = s_new + causal
    highest = jnp.maximum(
        jnp.max(s_cache, axis=1, keepdims=True), jnp.max(s_new, axis=1, keepdims=True)
    )
    p_cache = jnp.exp(s_cache - highest)
    p_new = jnp.exp(s_new - highest)
    denominator = jnp.sum(p_cache, axis=1, keepdims=True) + jnp.sum(p_new, axis=1, keepdims=True)

    for copy in copies[4:7]:
        copy.wait()
    for m in range(slots):
        page = table[m, SINGLES]
        v_prompt[m * 128 : (m + 1) * 128, :] = v_pool[pl.ds(pl.multiple_of(page * 128, 128), 128), :]
    out_prompt = dot_nn(p_cache.astype(jnp.bfloat16), v_prompt[...])
    out_prompt = out_prompt + dot_nn(p_new.astype(jnp.bfloat16), v_new[SINGLES:, :])
    out_prompt = (out_prompt / denominator).astype(jnp.bfloat16)
    out_single = dot_nn(weights[...], v_pool[...])
    fresh = v_new[0:SINGLES, :].astype(jnp.float32)
    for h in range(group):
        lanes = slice(h * HD, (h + 1) * HD)
        one = out_single[h * SINGLES : (h + 1) * SINGLES, :] + own_parts[h] * fresh
        heads[0:SINGLES, lanes] = (one / denominators[h]).astype(jnp.bfloat16)
        heads[SINGLES:, lanes] = out_prompt[h * PROMPT : (h + 1) * PROMPT, :]

    t = place[0]
    core, y = lax.rem(t, 2), lax.div(t, 2)
    order = [(1 - y) * 2 + 1 - core, y * 2 + 1 - core, (1 - y) * 2 + core, y * 2 + core]
    for i, block in enumerate(order):
        ordered[i * 16 : (i + 1) * 16, :] = heads[pl.ds(pl.multiple_of(block * 16, 16), 16), :]
    for copy in copies[7:]:
        copy.wait()
    for start in range(0, w_out.shape[1], 512):
        part = dot_nn(ordered[...], w_out[:, start : start + 512]).astype(jnp.bfloat16)
        send[:, start : start + 512] = part[0:32, :]
        keep[:, start : start + 512] = part[32:64, :]


def in_hbm(array):
    return pltpu.with_memory_space_constraint(array, pltpu.HBM)


def attention_call(place, table, counts, allowed, favored, chosen, shares, q, k_new, v_new, k_pool, v_pool, w_out):
    pool_rows, rows, width = k_pool.shape[0], q.shape[0], w_out.shape[1]
    vmem, smem, hbm = (pl.BlockSpec(memory_space=s) for s in (pltpu.VMEM, pltpu.SMEM, pl.ANY))
    half = jax.ShapeDtypeStruct((rows // 2, width), jnp.bfloat16)
    singles = SINGLES * (q.shape[1] // HD)
    return pl.pallas_call(
        attend_kernel,
        out_shape=(half, half, jax.ShapeDtypeStruct((chosen.shape[1], 128), jnp.float32)),
        in_specs=[smem] * 5 + [vmem] * 2 + [hbm] * 6,
        out_specs=(vmem,) * 3,
        scratch_shapes=[
            pltpu.VMEM(q.shape, jnp.bfloat16),
            pltpu.VMEM(k_new.shape, jnp.bfloat16),
            pltpu.VMEM(v_new.shape, jnp.bfloat16),
            pltpu.VMEM((pool_rows, HD), jnp.bfloat16),
            pltpu.VMEM((pool_rows, HD), jnp.bfloat16),
            pltpu.VMEM(w_out.shape, jnp.bfloat16),
            pltpu.VMEM((singles, pool_rows), jnp.float32),
            pltpu.VMEM((SINGLES, pool_rows), jnp.float32),
            pltpu.VMEM((singles, pool_rows), jnp.bfloat16),
            pltpu.VMEM((table.shape[0] * 128, HD), jnp.bfloat16),
            pltpu.VMEM((table.shape[0] * 128, HD), jnp.bfloat16),
            pltpu.VMEM((rows, q.shape[1]), jnp.bfloat16),
            pltpu.VMEM((rows, q.shape[1]), jnp.bfloat16),
            pltpu.SemaphoreType.DMA((11,)),
        ],
        compiler_params=pltpu.CompilerParams(vmem_limit_bytes=60 * MIB),
        cost_estimate=pl.CostEstimate(flops=10**9, bytes_accessed=8 * 10**6, transcendentals=6 * 10**5),
        name="attention",
    )(place, table, counts, allowed, favored, chosen, shares, q, k_new, v_new, k_pool, v_pool, w_out)


def slot_spans(tile):
    return [(0, 2 * tile), (2 * tile, tile), (3 * tile, tile), (4 * tile, tile)]


def experts_kernel(
    place, favored, a0, a1, a2, a3, b0, b1, b2, b3, gate, up, down,
    a_keep_near, a_keep_far, a_send_near, a_send_far, b_keep_near, b_keep_far, b_send_near, b_send_far,
    tokens, ring, pick, spread, scale, taken, act, in_sems, w_sems,
):
    count, hidden = tokens.shape[0], act.shape[1]
    half = a_keep_near.shape[1]
    notes_at = half
    tile = taken.shape[0] // 5
    spans = slot_spans(tile)
    first = jnp.maximum(favored[0], 0)
    expert_of = [first] + [jnp.where(s - 1 < first, s - 1, s) for s in (1, 2, 3)]

    def fetch(matrix, s, slot):
        rows = ring.at[slot * hidden : (slot + 1) * hidden, :]
        return pltpu.make_async_copy(matrix.at[expert_of[s]], rows, w_sems.at[slot])

    def fetch_inner(s):
        fetch(gate, s, 2 * s).start()
        fetch(up, s, 2 * s + 1).start()

    loads = []
    for i, ref in enumerate((b0, b1, b2, b3)):
        for j in range(2):
            row = (i // 2) * 256 + j * 128 + (i % 2) * 64
            rows = tokens.at[row : row + 64, half + 128 :]
            loads.append(
                pltpu.make_async_copy(ref.at[j * 64 : (j + 1) * 64, :], rows, in_sems.at[len(loads)])
            )
            loads[-1].start()
    fetch_inner(0)
    fetch_inner(1)
    for i, ref in enumerate((a0, a1, a2, a3)):
        tokens[i * 128 : (i + 1) * 128, 0 : half + 128] = ref[...]

    notes = tokens[:, notes_at : notes_at + 128]
    width = notes.shape[1]
    source = lax.broadcasted_iota(jnp.int32, (width, width), 0)
    target = lax.broadcasted_iota(jnp.int32, (width, width), 1)
    expert = jnp.where(target == 0, first, jnp.where(target - 1 < first, target - 1, target))
    wanted = (source < 24) & (target < 4) & (lax.rem(source, 8) == place[0] * 4 + expert)
    share = dot_nn(notes, jnp.where(wanted, 1.0, 0.0).astype(jnp.bfloat16))
    kept = jnp.where(share > 0.0, 1.0, 0.0)
    side = count // 2
    side_rows = 5 * tile // 2
    below = lax.broadcasted_iota(jnp.int32, (side, side), 1) < lax.broadcasted_iota(
        jnp.int32, (side, side), 0
    )
    below = jnp.where(below, 1.0, 0.0).astype(jnp.bfloat16)
    lane = lax.broadcasted_iota(jnp.int32, (1, width), 1)
    for h in range(2):
        here = slice(h * side, (h + 1) * side)
        rank = dot_nn(below, kept[here].astype(jnp.bfloat16))
        spot = jnp.where(kept[here] > 0.0, rank, -1000.0)
        spot_t = spot.T
        for s, (row, rows) in enumerate(spans):
            size, at = rows // 2, h * side_rows + row // 2
            ids = lax.broadcasted_iota(jnp.int32, (size, side), 0).astype(jnp.float32)
            picked = jnp.where(ids == spot_t[s : s + 1, :], 1.0, 0.0).astype(jnp.bfloat16)
            pick[at : at + size, :] = picked
            found = dot_nn(picked, notes[here])
            mine = (lane < 24) & (lax.rem(lane, 8) == place[0] * 4 + expert_of[s])
            part = jnp.sum(jnp.where(mine, found, 0.0), axis=1, keepdims=True)
            scale[row + h * size : row + (h + 1) * size, :] = jnp.broadcast_to(part, (size, width))
        for block in range(spread.shape[1] // 128):
            ids = (lax.broadcasted_iota(jnp.int32, (side, 128), 1) + block * 128).astype(jnp.float32)
            total = jnp.zeros((side, 128), jnp.float32)
            for s, (row, rows) in enumerate(spans):
                if row // 2 < (block + 1) * 128 and (row + rows) // 2 > block * 128:
                    total = total + jnp.where(ids == spot[:, s : s + 1] + row // 2, 1.0, 0.0)
            spread[here, block * 128 : (block + 1) * 128] = total.astype(jnp.bfloat16)

    fetch_inner(2)
    for load in loads:
        load.wait()

    for start in range(0, 2 * half, 512):
        at = start if start < half else start + 128
        for h in range(2):
            found = dot_nn(
                pick[h * side_rows : (h + 1) * side_rows, :], tokens[h * side : (h + 1) * side, at : at + 512]
            ).astype(jnp.bfloat16)
            for row, rows in spans:
                size = rows // 2
                taken[row + h * size : row + (h + 1) * size, start : start + 512] = found[
                    row // 2 : row // 2 + size, :
                ]

    fetch_inner(3)
    made = tokens
    for h in range(2):
        rest = slice(h * side + side_rows, (h + 1) * side)
        made[rest, :] = jnp.zeros_like(made[rest, :])
    for s, (row, rows) in enumerate(spans):
        x = taken[row : row + rows, :]
        fetch(gate, s, 2 * s).wait()
        g = dot_nt(x, ring[2 * s * hidden : (2 * s + 1) * hidden, :])
        fetch(up, s, 2 * s + 1).wait()
        u = dot_nt(x, ring[(2 * s + 1) * hidden : (2 * s + 2) * hidden, :])
        act[row : row + rows, :] = (g / (1.0 + jnp.exp(-g)) * u).astype(jnp.bfloat16)
        for later in (2 * s, 2 * s + 1):
            if later < 4:
                fetch(down, later, later).start()

    for s, (row, rows) in enumerate(spans):
        fetch(down, s, s).wait()
        part = scale[row : row + rows, 0:1]
        for start in range(0, 2 * half, 1024):
            o = dot_nn(act[row : row + rows, :], ring[s * hidden : (s + 1) * hidden, start : start + 1024])
            o = (o * part).astype(jnp.bfloat16)
            size = rows // 2
            for h in range(2):
                at = h * side + row // 2
                made[at : at + size, start : start + 1024] = o[h * size : (h + 1) * size, :]

    outs_a = (a_keep_near, a_keep_far, a_send_near, a_send_far)
    outs_b = (b_keep_near, b_keep_far, b_send_near, b_send_far)
    for i, outs in enumerate((outs_a, outs_b)):
        for at in range(0, half, 512):
            for h in range(2):
                here = slice(h * side, (h + 1) * side)
                y = dot_nn(spread[here, :], made[here, i * half + at : i * half + at + 512]).astype(jnp.bfloat16)
                for j in range(4):
                    to = j if i == 0 else j % 2 * 2 + j // 2
                    rows = slice(to % 2 * 64, to % 2 * 64 + 64)
                    outs[h * 2 + to // 2][rows, at : at + 512] = y[j * 64 : (j + 1) * 64, :]


def experts_call(place, favored, pieces_a, pieces_b, gate, up, down):
    _, hidden, width = gate.shape
    count = sum(piece.shape[0] for piece in pieces_a)
    tile = CAP_MOST * 32
    rows, padded = 5 * tile, -(-5 * tile // 256) * 128
    half = width // 2
    smem, vmem, hbm = (pl.BlockSpec(memory_space=s) for s in (pltpu.SMEM, pltpu.VMEM, pl.ANY))
    out = jax.ShapeDtypeStruct((count // 4, half), jnp.bfloat16)
    return pl.pallas_call(
        experts_kernel,
        out_shape=(out,) * 8,
        in_specs=[smem, smem] + [vmem] * 4 + [hbm] * 7,
        out_specs=(vmem,) * 8,
        scratch_shapes=[
            pltpu.VMEM((count, width + 128), jnp.bfloat16),
            pltpu.VMEM((8 * hidden, width), jnp.bfloat16),
            pltpu.VMEM((rows, count // 2), jnp.bfloat16),
            pltpu.VMEM((count, padded), jnp.bfloat16),
            pltpu.VMEM((rows, 128), jnp.float32),
            pltpu.VMEM((rows, width), jnp.bfloat16),
            pltpu.VMEM((rows, hidden), jnp.bfloat16),
            pltpu.SemaphoreType.DMA((8,)),
            pltpu.SemaphoreType.DMA((8,)),
        ],
        compiler_params=pltpu.CompilerParams(vmem_limit_bytes=EXPERTS_MIB * MIB),
        cost_estimate=pl.CostEstimate(
            flops=6 * rows * hidden * width, bytes_accessed=24 * hidden * width, transcendentals=rows * hidden
        ),
        name="experts",
    )(place, favored, *pieces_a, *pieces_b, *map(in_hbm, (gate, up, down)))


def joined(*parts):
    return jnp.concatenate(parts, axis=0)


def plus(a, b):
    return (a.astype(jnp.float32) + b.astype(jnp.float32)).astype(jnp.bfloat16)


def local_fast(
    skip_stream_entry,
    question_vectors,
    fresh_lookup_vectors,
    fresh_content_vectors,
    stored_lookup_sheets,
    stored_content_sheets,
    sequence_sheet_map,
    stored_position_counts,
    attention_merge_matrix,
    premix_scale_factor,
    chosen_specialists,
    selection_shares,
    allowed_placements,
    favored_specialist,
    gating_matrices,
    expand_matrices,
    contract_matrices,
):
    width = skip_stream_entry.shape[1]
    half = width // 2
    own_experts = gating_matrices.shape[0]
    count = chosen_specialists.shape[0]
    x, t = lax.axis_index("expert"), lax.axis_index("tensor")

    send, keep, notes = attention_call(
        t.astype(jnp.int32)[None],
        sequence_sheet_map.T,
        stored_position_counts,
        allowed_placements,
        favored_specialist,
        chosen_specialists.T,
        selection_shares.T,
        question_vectors,
        fresh_lookup_vectors,
        fresh_content_vectors,
        stored_lookup_sheets.reshape(-1, HD),
        stored_content_sheets.reshape(-1, HD),
        attention_merge_matrix,
    )
    got = over_core(send)
    keep, notes = lax.optimization_barrier((keep.astype(jnp.float32), notes.astype(jnp.bfloat16)))
    skip = lax.optimization_barrier(skip_stream_entry.astype(jnp.float32))
    far = plus(got[0:count], keep[0:count])
    near = plus(got[count:], keep[count:])
    own_attn = over_y(far).astype(jnp.float32) + near.astype(jnp.float32)
    stream = (skip + own_attn).astype(jnp.bfloat16)
    wide = stream.astype(jnp.float32)
    squares = jnp.mean(wide * wide, axis=1, keepdims=True)
    normed = (wide * lax.rsqrt(squares + 1e-05) * premix_scale_factor.astype(jnp.float32)).astype(
        jnp.bfloat16
    )

    hot = favored_specialist - x * own_experts
    hot = jnp.where((hot >= 0) & (hot < own_experts), hot, -1).astype(jnp.int32)

    part_a, part_b = jnp.concatenate([normed[:, :half], notes], axis=1), normed[:, half:]
    second = over_z(part_b, 2)
    third, middle, first = over_z(part_a, 3), over_z(part_a, 2), over_z(part_a, 1)
    pairs = over_z(joined(part_b, second), 1)
    part_a = joined(part_a, first, middle, third)
    part_b = joined(part_b, pairs[:count], second, pairs[count:])
    gathered = []
    for part, first, second in ((part_a, over_x, over_y), (part_b, over_y, over_x)):
        part = joined(part, first(part))
        other = second(part)
        gathered.append((part, other, over_core(part), over_core(other)))
    outs = experts_call(
        x.astype(jnp.int32)[None], hot, *gathered, gating_matrices, expand_matrices, contract_matrices
    )
    results = []
    for (keep_near, keep_far, send_near, send_far), first, second in (
        (outs[:4], over_y, over_x),
        (outs[4:], over_x, over_y),
    ):
        far = first(plus(over_core(send_far), keep_far))
        near = plus(over_core(send_near), keep_near)
        rows = near.shape[0] // 2
        got = second(plus(far[rows:], near[rows:]))
        results.append(plus(far[:rows], near[:rows]).astype(jnp.float32) + got.astype(jnp.float32))
    total_a, total_b = results
    sent = jnp.concatenate([total_b[count : 2 * count], total_b[3 * count :]], axis=0).astype(jnp.bfloat16)
    got = over_z(sent, 1).astype(jnp.float32)
    out_a = total_a[0:count]
    for k in (1, 2, 3):
        mine = total_a[k * count : (k + 1) * count].astype(jnp.bfloat16)
        out_a = out_a + over_z(mine, k).astype(jnp.float32)
    far = (total_b[2 * count : 3 * count] + got[count:]).astype(jnp.bfloat16)
    out_b = total_b[0:count] + got[0:count] + over_z(far, 2).astype(jnp.float32)
    return (wide + jnp.concatenate([out_a, out_b], axis=1)).astype(jnp.bfloat16)


def solution(mesh):
    placed = (
        P(("dp", "expert", "tensor"), None),
        P(("dp", "expert"), "tensor"),
        P(("dp", "expert"), "tensor"),
        P(("dp", "expert"), "tensor"),
        P(("dp", "expert"), "tensor", None, None),
        P(("dp", "expert"), "tensor", None, None),
        P(("dp", "expert"), None),
        P(("dp", "expert")),
        P("tensor", None),
        P(),
        P(("dp", "expert", "tensor"), None),
        P(("dp", "expert", "tensor"), None),
        P(),
        P(),
        P("expert", ("dp", "tensor"), None),
        P("expert", ("dp", "tensor"), None),
        P("expert", ("dp", "tensor"), None),
    )
    sizes = tuple(mesh.shape[name] for name in ("dp", "expert", "tensor"))
    return jax.shard_map(
        local_fast if sizes == (4, 2, 4) else local,
        mesh=mesh,
        in_specs=placed,
        out_specs=P(("dp", "expert", "tensor"), None),
        check_vma=False,
    )
```

```python
from functools import reduce
import math

import jax
import jax.numpy as jnp
from jax import lax
from jax.experimental import pallas as pl
from jax.experimental.pallas import tpu as pltpu
from jax.sharding import PartitionSpec as P

HD = 128
PLACEMENT_MOST = 6


def normalize(parts):
    highest = reduce(
        jnp.maximum,
        [
            jnp.max(jnp.where(visible, scores, -jnp.inf), axis=-1, keepdims=True)
            for scores, visible in parts
        ],
    )
    portions = [jnp.where(visible, jnp.exp(scores - highest), 0.0) for scores, visible in parts]
    denominator = reduce(
        jnp.add, [jnp.sum(portion, axis=-1, keepdims=True) for portion in portions]
    )
    return [(portion / denominator).astype(jnp.bfloat16) for portion in portions]


def attend(question_vectors, new_keys, new_values, key_pages, value_pages, table, spans):
    rows_all, head_count, head_width = question_vectors.shape
    kv_heads = new_keys.shape[1]
    group_size = head_count // kv_heads
    single_count = spans.shape[0] - 1
    page_count = table.shape[1]
    page_width = key_pages.shape[2]
    context = page_count * page_width
    inverse_root = 1.0 / math.sqrt(head_width)
    page_keys = key_pages[table]
    page_values = value_pages[table]
    grouped = question_vectors.reshape(rows_all, kv_heads, group_size, head_width)
    positions = jnp.arange(context, dtype=jnp.int32)
    single_q = grouped[:single_count]
    cache_dec = (
        jnp.einsum(
            "rkgh,rmkph->rkgmp",
            single_q,
            page_keys[:single_count],
            preferred_element_type=jnp.float32,
        ).reshape(single_count, kv_heads, group_size, context)
        * inverse_root
    )
    seen_dec = (positions[None, :] < spans[:single_count, None])[:, None, None, :]
    own_dec = (
        jnp.einsum(
            "rkgh,rkh->rkg", single_q, new_keys[:single_count], preferred_element_type=jnp.float32
        )[..., None]
        * inverse_root
    )
    weight_cache, weight_own = normalize(
        [(cache_dec, seen_dec), (own_dec, jnp.full(own_dec.shape, True))]
    )
    out_dec = jnp.einsum(
        "rkgmp,rmkph->rkgh",
        weight_cache.reshape(single_count, kv_heads, group_size, page_count, page_width),
        page_values[:single_count],
        preferred_element_type=jnp.float32,
    )
    out_dec = (
        out_dec
        + weight_own.astype(jnp.float32)
        * new_values[:single_count].astype(jnp.float32)[:, :, None, :]
    )
    prompt_q = grouped[single_count:]
    prompt_rows = rows_all - single_count
    cache_pro = (
        jnp.einsum(
            "rkgh,mkph->rkgmp",
            prompt_q,
            page_keys[single_count],
            preferred_element_type=jnp.float32,
        ).reshape(prompt_rows, kv_heads, group_size, context)
        * inverse_root
    )
    seen_pro = (positions < spans[single_count])[None, None, None, :]
    new_pro = (
        jnp.einsum(
            "rkgh,mkh->rkgm", prompt_q, new_keys[single_count:], preferred_element_type=jnp.float32
        )
        * inverse_root
    )
    prompt_index = jnp.arange(prompt_rows, dtype=jnp.int32)
    causal = (prompt_index[:, None] >= prompt_index[None, :])[:, None, None, :]
    weight_cpro, weight_npro = normalize([(cache_pro, seen_pro), (new_pro, causal)])
    out_pro = jnp.einsum(
        "rkgmp,mkph->rkgh",
        weight_cpro.reshape(prompt_rows, kv_heads, group_size, page_count, page_width),
        page_values[single_count],
        preferred_element_type=jnp.float32,
    )
    out_pro = out_pro + jnp.einsum(
        "rkgm,mkh->rkgh", weight_npro, new_values[single_count:], preferred_element_type=jnp.float32
    )
    joined = jnp.concatenate([out_dec, out_pro], axis=0).astype(jnp.bfloat16)
    return joined.reshape(rows_all, head_count * head_width)


def slot_table(member, ranking, keeping, slot_count):
    slot_hit = (
        ranking[:, :, None, None] == jnp.arange(slot_count, dtype=jnp.int32)[None, None, None, :]
    )
    return ((member[..., None] > 0) & keeping[:, :, None, None] & slot_hit).astype(jnp.bfloat16)


def expert_pass(send, gating_matrices, expand_matrices, contract_matrices):
    specialist_index, slot_count, model_width = send.shape
    holders = lax.axis_size("expert")
    local_count = gating_matrices.shape[0]
    arrived = lax.all_to_all(
        send.reshape(holders, local_count, slot_count, model_width),
        "expert",
        split_axis=0,
        concat_axis=0,
        tiled=True,
    )
    row_piece = lax.all_gather(arrived, ("dp", "tensor"), axis=0, tiled=True)
    gate_part = jnp.einsum(
        "qesd,efd->qesf", row_piece, gating_matrices, preferred_element_type=jnp.float32
    )
    up_part = jnp.einsum(
        "qesd,efd->qesf", row_piece, expand_matrices, preferred_element_type=jnp.float32
    )
    hidden = (jax.nn.silu(gate_part) * up_part).astype(jnp.bfloat16)
    summed = lax.psum_scatter(
        jnp.einsum(
            "qesf,efd->qesd", hidden, contract_matrices, preferred_element_type=jnp.float32
        ).astype(jnp.bfloat16),
        ("dp", "tensor"),
        scatter_dimension=0,
        tiled=True,
    )
    arrived_back = lax.all_to_all(summed, "expert", split_axis=0, concat_axis=0, tiled=True)
    return arrived_back.reshape(specialist_index, slot_count, model_width)


def local(
    skip_stream_entry,
    question_vectors,
    fresh_lookup_vectors,
    fresh_content_vectors,
    stored_lookup_sheets,
    stored_content_sheets,
    sequence_sheet_map,
    stored_position_counts,
    attention_merge_matrix,
    premix_scale_factor,
    chosen_specialists,
    selection_shares,
    allowed_placements,
    favored_specialist,
    gating_matrices,
    expand_matrices,
    contract_matrices,
):
    token_count = chosen_specialists.shape[0]
    specialist_index = allowed_placements.shape[0]
    picked = (
        chosen_specialists[:, :, None]
        == jnp.arange(specialist_index, dtype=jnp.int32)[None, None, :]
    ).astype(jnp.int32)
    flat_routes = picked.reshape(token_count * 2, specialist_index)
    busiest_specialist = favored_specialist[0]
    before = (jnp.cumsum(flat_routes, axis=0) - flat_routes).reshape(
        token_count, 2, specialist_index
    )
    ranking = jnp.sum(before * picked, axis=2)
    placement_ceiling = jnp.where(
        jnp.arange(specialist_index, dtype=jnp.int32) == busiest_specialist,
        PLACEMENT_MOST,
        allowed_placements,
    )
    keeping = ranking < jnp.sum(picked * placement_ceiling[None, None, :], axis=2)
    row_total = question_vectors.shape[0]
    heads_out = attend(
        question_vectors.reshape(row_total, -1, HD),
        fresh_lookup_vectors.reshape(row_total, -1, HD),
        fresh_content_vectors.reshape(row_total, -1, HD),
        stored_lookup_sheets,
        stored_content_sheets,
        sequence_sheet_map,
        stored_position_counts,
    )
    total_attn = lax.psum(
        jnp.dot(heads_out, attention_merge_matrix, preferred_element_type=jnp.float32).astype(
            jnp.bfloat16
        ),
        "tensor",
    ).astype(jnp.float32)
    own_attn = lax.dynamic_slice_in_dim(
        total_attn, lax.axis_index("tensor") * token_count, token_count, 0
    )
    stream = (skip_stream_entry.astype(jnp.float32) + own_attn).astype(jnp.bfloat16)
    wide = stream.astype(jnp.float32)
    squares = jnp.mean(wide * wide, axis=1, keepdims=True)
    normed = (wide * lax.rsqrt(squares + 1e-05) * premix_scale_factor.astype(jnp.float32)).astype(
        jnp.bfloat16
    )
    main_slots = PLACEMENT_MOST
    table_main = slot_table(picked, ranking, keeping, main_slots)
    send = jnp.einsum(
        "nkes,nd->esd", table_main, normed, preferred_element_type=jnp.float32
    ).astype(jnp.bfloat16)
    expert_out = expert_pass(send, gating_matrices, expand_matrices, contract_matrices)
    chosen = jnp.einsum("nkes,esd->nkd", table_main, expert_out, preferred_element_type=jnp.float32)
    mixed = jnp.sum(selection_shares[:, :, None] * chosen, axis=1)
    return (wide + mixed).astype(jnp.bfloat16)


PAIRS_CORE = [(0, 1), (1, 0), (2, 3), (3, 2)]
PAIRS_Y = [(0, 2), (2, 0), (1, 3), (3, 1)]
PAIRS_X = [(0, 1), (1, 0)]
SINGLES = 16
PROMPT = 48
CAP_MOST = 3
NEG = -1e30
MIB = 1 << 20
EXPERTS_MIB = 43


def over_core(a):
    return lax.ppermute(a, "tensor", PAIRS_CORE)


def over_y(a):
    return lax.ppermute(a, "tensor", PAIRS_Y)


def over_x(a):
    return lax.ppermute(a, "expert", PAIRS_X)


def over_z(a, k):
    return lax.ppermute(a, "dp", [(i, i ^ k) for i in range(4)])


def dot_nt(a, b):
    return lax.dot_general(a, b, (((1,), (1,)), ((), ())), preferred_element_type=jnp.float32)


def dot_nn(a, b):
    return lax.dot_general(a, b, (((1,), (0,)), ((), ())), preferred_element_type=jnp.float32)


def note_routes(allowed, favored, chosen, shares, notes):
    experts, count = allowed.shape[0], chosen.shape[1]
    expert = lax.broadcasted_iota(jnp.int32, (experts, count), 0)
    picked = [jnp.where(chosen[k : k + 1, :] == expert, 1.0, 0.0) for k in range(2)]
    earlier = lax.broadcasted_iota(jnp.int32, (count, count), 0) < lax.broadcasted_iota(
        jnp.int32, (count, count), 1
    )
    before = dot_nn(
        (picked[0] + picked[1]).astype(jnp.bfloat16), jnp.where(earlier, 1.0, 0.0).astype(jnp.bfloat16)
    )
    limit = jnp.zeros((experts, count), jnp.int32)
    for e in range(experts):
        limit = jnp.where(expert == e, allowed[e], limit)
    limit = jnp.where(expert == favored[0], PLACEMENT_MOST, limit).astype(jnp.float32)
    rest = picked[0] * shares[0:1, :] + picked[1] * shares[1:2, :]
    rest = jnp.where(before < limit, rest, 0.0)
    parts = []
    for _ in range(3):
        part = rest.astype(jnp.bfloat16).astype(jnp.float32)
        parts.append(part)
        rest = rest - part
    parts.append(jnp.zeros((128 - 3 * experts, count), jnp.float32))
    parts = jnp.concatenate(parts, axis=0)
    parts = jnp.concatenate([parts, jnp.zeros((128, 128 - count), jnp.float32)], axis=1)
    notes[...] = parts.T[0:count, :]


def attend_kernel(
    place, table, counts, allowed, favored, chosen, shares, q_hbm, k_new_hbm, v_new_hbm, k_hbm, v_hbm, w_hbm,
    send, keep, notes,
    q, k_new, v_new, k_pool, v_pool, w_out, scores, times, weights, k_prompt, v_prompt, heads, ordered, sems,
):
    pool_rows = k_pool.shape[0]
    pages = pool_rows // 128
    slots = table.shape[0]
    group = q.shape[1] // HD
    pairs = [(q_hbm, q), (k_new_hbm, k_new)]
    for source, target, parts in ((k_hbm, k_pool, 2), (v_hbm, v_pool, 2), (w_hbm, w_out, 4)):
        rows = source.shape[0] // parts
        for i in range(parts):
            pairs.append((source.at[i * rows : (i + 1) * rows, :], target.at[i * rows : (i + 1) * rows, :]))
    pairs.insert(4, (v_new_hbm, v_new))
    copies = [pltpu.make_async_copy(src, dst, sems.at[i]) for i, (src, dst) in enumerate(pairs)]
    for copy in copies:
        copy.start()
    note_routes(allowed, favored, chosen, shares, notes)
    root = 1.0 / math.sqrt(HD)

    lane = lax.broadcasted_iota(jnp.int32, (SINGLES, 128), 1)
    request = lax.broadcasted_iota(jnp.int32, (SINGLES, 128), 0)
    spans = jnp.zeros((SINGLES, 128), jnp.int32)
    named = [spans] * slots
    for r in range(SINGLES):
        here = request == r
        spans = jnp.where(here, counts[r], spans)
        named = [jnp.where(here, table[m, r], named[m]) for m in range(slots)]
    seen = [jnp.where(lane + m * 128 < spans, 1.0, 0.0) for m in range(slots)]
    for page in range(pages):
        total = jnp.zeros((SINGLES, 128), jnp.float32)
        for m in range(slots):
            total = total + jnp.where(named[m] == page, seen[m], 0.0)
        times[:, page * 128 : (page + 1) * 128] = total

    for copy in copies[:4]:
        copy.wait()
    q_single = jnp.concatenate([q[0:SINGLES, h * HD : (h + 1) * HD] for h in range(group)], axis=0)
    q_prompt = jnp.concatenate([q[SINGLES:, h * HD : (h + 1) * HD] for h in range(group)], axis=0)
    step = 1024
    for start in range(0, pool_rows, step):
        scores[:, start : start + step] = dot_nt(q_single, k_pool[start : start + step, :])
    for m in range(slots):
        page = table[m, SINGLES]
        k_prompt[m * 128 : (m + 1) * 128, :] = k_pool[pl.ds(pl.multiple_of(page * 128, 128), 128), :]
    s_cache = dot_nt(q_prompt, k_prompt[...]) * root
    s_new = dot_nt(q_prompt, k_new[SINGLES:, :]) * root
    own = k_new[0:SINGLES, :].astype(jnp.float32)

    denominators, own_parts = [], []
    for h in range(group):
        rows = slice(h * SINGLES, (h + 1) * SINGLES)
        often = times[...]
        s = jnp.where(often > 0.0, scores[rows, :] * root, NEG)
        s_own = (
            jnp.sum(q_single[rows, :].astype(jnp.float32) * own, axis=1, keepdims=True) * root
        )
        highest = jnp.maximum(jnp.max(s, axis=1, keepdims=True), s_own)
        p = jnp.exp(s - highest) * often
        p_own = jnp.exp(s_own - highest)
        denominators.append(jnp.sum(p, axis=1, keepdims=True) + p_own)
        own_parts.append(p_own)
        weights[rows, :] = p.astype(jnp.bfloat16)

    position = lax.broadcasted_iota(jnp.int32, s_cache.shape, 1)
    s_cache = jnp.where(position < counts[SINGLES], s_cache, NEG)
    row = lax.broadcasted_iota(jnp.int32, (PROMPT, PROMPT), 0)
    col = lax.broadcasted_iota(jnp.int32, (PROMPT, PROMPT), 1)
    causal = jnp.concatenate([jnp.where(row >= col, 0.0, NEG)] * group, axis=0)
    s_new = s_new + causal
    highest = jnp.maximum(
        jnp.max(s_cache, axis=1, keepdims=True), jnp.max(s_new, axis=1, keepdims=True)
    )
    p_cache = jnp.exp(s_cache - highest)
    p_new = jnp.exp(s_new - highest)
    denominator = jnp.sum(p_cache, axis=1, keepdims=True) + jnp.sum(p_new, axis=1, keepdims=True)

    for copy in copies[4:7]:
        copy.wait()
    for m in range(slots):
        page = table[m, SINGLES]
        v_prompt[m * 128 : (m + 1) * 128, :] = v_pool[pl.ds(pl.multiple_of(page * 128, 128), 128), :]
    out_prompt = dot_nn(p_cache.astype(jnp.bfloat16), v_prompt[...])
    out_prompt = out_prompt + dot_nn(p_new.astype(jnp.bfloat16), v_new[SINGLES:, :])
    out_prompt = (out_prompt / denominator).astype(jnp.bfloat16)
    out_single = dot_nn(weights[...], v_pool[...])
    fresh = v_new[0:SINGLES, :].astype(jnp.float32)
    for h in range(group):
        lanes = slice(h * HD, (h + 1) * HD)
        one = out_single[h * SINGLES : (h + 1) * SINGLES, :] + own_parts[h] * fresh
        heads[0:SINGLES, lanes] = (one / denominators[h]).astype(jnp.bfloat16)
        heads[SINGLES:, lanes] = out_prompt[h * PROMPT : (h + 1) * PROMPT, :]

    t = place[0]
    core, y = lax.rem(t, 2), lax.div(t, 2)
    order = [(1 - y) * 2 + 1 - core, y * 2 + 1 - core, (1 - y) * 2 + core, y * 2 + core]
    for i, block in enumerate(order):
        ordered[i * 16 : (i + 1) * 16, :] = heads[pl.ds(pl.multiple_of(block * 16, 16), 16), :]
    for copy in copies[7:]:
        copy.wait()
    for start in range(0, w_out.shape[1], 512):
        part = dot_nn(ordered[...], w_out[:, start : start + 512]).astype(jnp.bfloat16)
        send[:, start : start + 512] = part[0:32, :]
        keep[:, start : start + 512] = part[32:64, :]


def in_hbm(array):
    return pltpu.with_memory_space_constraint(array, pltpu.HBM)


def attention_call(place, table, counts, allowed, favored, chosen, shares, q, k_new, v_new, k_pool, v_pool, w_out):
    pool_rows, rows, width = k_pool.shape[0], q.shape[0], w_out.shape[1]
    vmem, smem, hbm = (pl.BlockSpec(memory_space=s) for s in (pltpu.VMEM, pltpu.SMEM, pl.ANY))
    half = jax.ShapeDtypeStruct((rows // 2, width), jnp.bfloat16)
    singles = SINGLES * (q.shape[1] // HD)
    return pl.pallas_call(
        attend_kernel,
        out_shape=(half, half, jax.ShapeDtypeStruct((chosen.shape[1], 128), jnp.float32)),
        in_specs=[smem] * 5 + [vmem] * 2 + [hbm] * 6,
        out_specs=(vmem,) * 3,
        scratch_shapes=[
            pltpu.VMEM(q.shape, jnp.bfloat16),
            pltpu.VMEM(k_new.shape, jnp.bfloat16),
            pltpu.VMEM(v_new.shape, jnp.bfloat16),
            pltpu.VMEM((pool_rows, HD), jnp.bfloat16),
            pltpu.VMEM((pool_rows, HD), jnp.bfloat16),
            pltpu.VMEM(w_out.shape, jnp.bfloat16),
            pltpu.VMEM((singles, pool_rows), jnp.float32),
            pltpu.VMEM((SINGLES, pool_rows), jnp.float32),
            pltpu.VMEM((singles, pool_rows), jnp.bfloat16),
            pltpu.VMEM((table.shape[0] * 128, HD), jnp.bfloat16),
            pltpu.VMEM((table.shape[0] * 128, HD), jnp.bfloat16),
            pltpu.VMEM((rows, q.shape[1]), jnp.bfloat16),
            pltpu.VMEM((rows, q.shape[1]), jnp.bfloat16),
            pltpu.SemaphoreType.DMA((11,)),
        ],
        compiler_params=pltpu.CompilerParams(vmem_limit_bytes=60 * MIB),
        cost_estimate=pl.CostEstimate(flops=10**9, bytes_accessed=8 * 10**6, transcendentals=6 * 10**5),
        name="attention",
    )(place, table, counts, allowed, favored, chosen, shares, q, k_new, v_new, k_pool, v_pool, w_out)


def slot_spans(tile):
    return [(0, 2 * tile), (2 * tile, tile), (3 * tile, tile), (4 * tile, tile)]


def experts_kernel(
    place, favored, a0, a1, a2, a3, b0, b1, b2, b3, gate, up, down,
    a_keep_near, a_keep_far, a_send_near, a_send_far, b_keep_near, b_keep_far, b_send_near, b_send_far,
    tokens, ring, pick, spread, scale, taken, act, in_sems, w_sems,
):
    count, hidden = tokens.shape[0], act.shape[1]
    half = a_keep_near.shape[1]
    notes_at = half
    tile = taken.shape[0] // 5
    spans = slot_spans(tile)
    first = jnp.maximum(favored[0], 0)
    expert_of = [first] + [jnp.where(s - 1 < first, s - 1, s) for s in (1, 2, 3)]

    def fetch(matrix, s, slot):
        rows = ring.at[slot * hidden : (slot + 1) * hidden, :]
        return pltpu.make_async_copy(matrix.at[expert_of[s]], rows, w_sems.at[slot])

    def fetch_inner(s):
        fetch(gate, s, 2 * s).start()
        fetch(up, s, 2 * s + 1).start()

    loads = []
    for i, ref in enumerate((b0, b1, b2, b3)):
        for j in range(2):
            row = (i // 2) * 256 + j * 128 + (i % 2) * 64
            rows = tokens.at[row : row + 64, half + 128 :]
            loads.append(
                pltpu.make_async_copy(ref.at[j * 64 : (j + 1) * 64, :], rows, in_sems.at[len(loads)])
            )
            loads[-1].start()
    fetch_inner(0)
    fetch_inner(1)
    for i, ref in enumerate((a0, a1, a2, a3)):
        tokens[i * 128 : (i + 1) * 128, 0 : half + 128] = ref[...]

    notes = tokens[:, notes_at : notes_at + 128]
    width = notes.shape[1]
    source = lax.broadcasted_iota(jnp.int32, (width, width), 0)
    target = lax.broadcasted_iota(jnp.int32, (width, width), 1)
    expert = jnp.where(target == 0, first, jnp.where(target - 1 < first, target - 1, target))
    wanted = (source < 24) & (target < 4) & (lax.rem(source, 8) == place[0] * 4 + expert)
    share = dot_nn(notes, jnp.where(wanted, 1.0, 0.0).astype(jnp.bfloat16))
    kept = jnp.where(share > 0.0, 1.0, 0.0)
    side = count // 2
    side_rows = 5 * tile // 2
    below = lax.broadcasted_iota(jnp.int32, (side, side), 1) < lax.broadcasted_iota(
        jnp.int32, (side, side), 0
    )
    below = jnp.where(below, 1.0, 0.0).astype(jnp.bfloat16)
    lane = lax.broadcasted_iota(jnp.int32, (1, width), 1)
    for h in range(2):
        here = slice(h * side, (h + 1) * side)
        rank = dot_nn(below, kept[here].astype(jnp.bfloat16))
        spot = jnp.where(kept[here] > 0.0, rank, -1000.0)
        spot_t = spot.T
        for s, (row, rows) in enumerate(spans):
            size, at = rows // 2, h * side_rows + row // 2
            ids = lax.broadcasted_iota(jnp.int32, (size, side), 0).astype(jnp.float32)
            picked = jnp.where(ids == spot_t[s : s + 1, :], 1.0, 0.0).astype(jnp.bfloat16)
            pick[at : at + size, :] = picked
            found = dot_nn(picked, notes[here])
            mine = (lane < 24) & (lax.rem(lane, 8) == place[0] * 4 + expert_of[s])
            part = jnp.sum(jnp.where(mine, found, 0.0), axis=1, keepdims=True)
            scale[row + h * size : row + (h + 1) * size, :] = jnp.broadcast_to(part, (size, width))
        for block in range(spread.shape[1] // 128):
            ids = (lax.broadcasted_iota(jnp.int32, (side, 128), 1) + block * 128).astype(jnp.float32)
            total = jnp.zeros((side, 128), jnp.float32)
            for s, (row, rows) in enumerate(spans):
                if row // 2 < (block + 1) * 128 and (row + rows) // 2 > block * 128:
                    total = total + jnp.where(ids == spot[:, s : s + 1] + row // 2, 1.0, 0.0)
            spread[here, block * 128 : (block + 1) * 128] = total.astype(jnp.bfloat16)

    fetch_inner(2)
    for load in loads:
        load.wait()

    for start in range(0, 2 * half, 512):
        at = start if start < half else start + 128
        for h in range(2):
            found = dot_nn(
                pick[h * side_rows : (h + 1) * side_rows, :], tokens[h * side : (h + 1) * side, at : at + 512]
            ).astype(jnp.bfloat16)
            for row, rows in spans:
                size = rows // 2
                taken[row + h * size : row + (h + 1) * size, start : start + 512] = found[
                    row // 2 : row // 2 + size, :
                ]

    fetch_inner(3)
    made = tokens
    for h in range(2):
        rest = slice(h * side + side_rows, (h + 1) * side)
        made[rest, :] = jnp.zeros_like(made[rest, :])
    for s, (row, rows) in enumerate(spans):
        x = taken[row : row + rows, :]
        fetch(gate, s, 2 * s).wait()
        g = dot_nt(x, ring[2 * s * hidden : (2 * s + 1) * hidden, :])
        fetch(up, s, 2 * s + 1).wait()
        u = dot_nt(x, ring[(2 * s + 1) * hidden : (2 * s + 2) * hidden, :])
        act[row : row + rows, :] = (g / (1.0 + jnp.exp(-g)) * u).astype(jnp.bfloat16)
        for later in (2 * s, 2 * s + 1):
            if later < 4:
                fetch(down, later, later).start()

    for s, (row, rows) in enumerate(spans):
        fetch(down, s, s).wait()
        part = scale[row : row + rows, 0:1]
        for start in range(0, 2 * half, 1024):
            o = dot_nn(act[row : row + rows, :], ring[s * hidden : (s + 1) * hidden, start : start + 1024])
            o = (o * part).astype(jnp.bfloat16)
            size = rows // 2
            for h in range(2):
                at = h * side + row // 2
                made[at : at + size, start : start + 1024] = o[h * size : (h + 1) * size, :]

    outs_a = (a_keep_near, a_keep_far, a_send_near, a_send_far)
    outs_b = (b_keep_near, b_keep_far, b_send_near, b_send_far)
    for i, outs in enumerate((outs_a, outs_b)):
        for at in range(0, half, 512):
            for h in range(2):
                here = slice(h * side, (h + 1) * side)
                y = dot_nn(spread[here, :], made[here, i * half + at : i * half + at + 512]).astype(jnp.bfloat16)
                for j in range(4):
                    to = j if i == 0 else j % 2 * 2 + j // 2
                    rows = slice(to % 2 * 64, to % 2 * 64 + 64)
                    outs[h * 2 + to // 2][rows, at : at + 512] = y[j * 64 : (j + 1) * 64, :]


def experts_call(place, favored, pieces_a, pieces_b, gate, up, down):
    _, hidden, width = gate.shape
    count = sum(piece.shape[0] for piece in pieces_a)
    tile = CAP_MOST * 32
    rows, padded = 5 * tile, -(-5 * tile // 256) * 128
    half = width // 2
    smem, vmem, hbm = (pl.BlockSpec(memory_space=s) for s in (pltpu.SMEM, pltpu.VMEM, pl.ANY))
    out = jax.ShapeDtypeStruct((count // 4, half), jnp.bfloat16)
    return pl.pallas_call(
        experts_kernel,
        out_shape=(out,) * 8,
        in_specs=[smem, smem] + [vmem] * 4 + [hbm] * 7,
        out_specs=(vmem,) * 8,
        scratch_shapes=[
            pltpu.VMEM((count, width + 128), jnp.bfloat16),
            pltpu.VMEM((8 * hidden, width), jnp.bfloat16),
            pltpu.VMEM((rows, count // 2), jnp.bfloat16),
            pltpu.VMEM((count, padded), jnp.bfloat16),
            pltpu.VMEM((rows, 128), jnp.float32),
            pltpu.VMEM((rows, width), jnp.bfloat16),
            pltpu.VMEM((rows, hidden), jnp.bfloat16),
            pltpu.SemaphoreType.DMA((8,)),
            pltpu.SemaphoreType.DMA((8,)),
        ],
        compiler_params=pltpu.CompilerParams(vmem_limit_bytes=EXPERTS_MIB * MIB),
        cost_estimate=pl.CostEstimate(
            flops=6 * rows * hidden * width, bytes_accessed=24 * hidden * width, transcendentals=rows * hidden
        ),
        name="experts",
    )(place, favored, *pieces_a, *pieces_b, *map(in_hbm, (gate, up, down)))


def joined(*parts):
    return jnp.concatenate(parts, axis=0)


def plus(a, b):
    return (a.astype(jnp.float32) + b.astype(jnp.float32)).astype(jnp.bfloat16)


def local_fast(
    skip_stream_entry,
    question_vectors,
    fresh_lookup_vectors,
    fresh_content_vectors,
    stored_lookup_sheets,
    stored_content_sheets,
    sequence_sheet_map,
    stored_position_counts,
    attention_merge_matrix,
    premix_scale_factor,
    chosen_specialists,
    selection_shares,
    allowed_placements,
    favored_specialist,
    gating_matrices,
    expand_matrices,
    contract_matrices,
):
    width = skip_stream_entry.shape[1]
    half = width // 2
    own_experts = gating_matrices.shape[0]
    count = chosen_specialists.shape[0]
    x, t = lax.axis_index("expert"), lax.axis_index("tensor")

    send, keep, notes = attention_call(
        t.astype(jnp.int32)[None],
        sequence_sheet_map.T,
        stored_position_counts,
        allowed_placements,
        favored_specialist,
        chosen_specialists.T,
        selection_shares.T,
        question_vectors,
        fresh_lookup_vectors,
        fresh_content_vectors,
        stored_lookup_sheets.reshape(-1, HD),
        stored_content_sheets.reshape(-1, HD),
        attention_merge_matrix,
    )
    got = over_core(send)
    keep, notes = lax.optimization_barrier((keep.astype(jnp.float32), notes.astype(jnp.bfloat16)))
    skip = lax.optimization_barrier(skip_stream_entry.astype(jnp.float32))
    far = plus(got[0:count], keep[0:count])
    near = plus(got[count:], keep[count:])
    own_attn = over_y(far).astype(jnp.float32) + near.astype(jnp.float32)
    stream = (skip + own_attn).astype(jnp.bfloat16)
    wide = stream.astype(jnp.float32)
    squares = jnp.mean(wide * wide, axis=1, keepdims=True)
    normed = (wide * lax.rsqrt(squares + 1e-05) * premix_scale_factor.astype(jnp.float32)).astype(
        jnp.bfloat16
    )

    hot = favored_specialist - x * own_experts
    hot = jnp.where((hot >= 0) & (hot < own_experts), hot, -1).astype(jnp.int32)

    part_a, part_b = jnp.concatenate([normed[:, :half], notes], axis=1), normed[:, half:]
    second = over_z(part_b, 2)
    third, middle, first = over_z(part_a, 3), over_z(part_a, 2), over_z(part_a, 1)
    pairs = over_z(joined(part_b, second), 1)
    part_a = joined(part_a, first, middle, third)
    part_b = joined(part_b, pairs[:count], second, pairs[count:])
    gathered = []
    for part, first, second in ((part_a, over_x, over_y), (part_b, over_y, over_x)):
        part = joined(part, first(part))
        other = second(part)
        gathered.append((part, other, over_core(part), over_core(other)))
    outs = experts_call(
        x.astype(jnp.int32)[None], hot, *gathered, gating_matrices, expand_matrices, contract_matrices
    )
    results = []
    for (keep_near, keep_far, send_near, send_far), first, second in (
        (outs[:4], over_y, over_x),
        (outs[4:], over_x, over_y),
    ):
        far = first(plus(over_core(send_far), keep_far))
        near = plus(over_core(send_near), keep_near)
        rows = near.shape[0] // 2
        got = second(plus(far[rows:], near[rows:]))
        results.append(plus(far[:rows], near[:rows]).astype(jnp.float32) + got.astype(jnp.float32))
    total_b, total_a = results
    sent = jnp.concatenate([total_b[count : 2 * count], total_b[3 * count :]], axis=0).astype(jnp.bfloat16)
    got = over_z(sent, 1).astype(jnp.float32)
    out_a = total_a[0:count]
    for k in (1, 2, 3):
        mine = total_a[k * count : (k + 1) * count].astype(jnp.bfloat16)
        out_a = out_a + over_z(mine, k).astype(jnp.float32)
    far = (total_b[2 * count : 3 * count] + got[count:]).astype(jnp.bfloat16)
    out_b = total_b[0:count] + got[0:count] + over_z(far, 2).astype(jnp.float32)
    return (wide + jnp.concatenate([out_b, out_a], axis=1)).astype(jnp.bfloat16)


def solution(mesh):
    placed = (
        P(("dp", "expert", "tensor"), None),
        P(("dp", "expert"), "tensor"),
        P(("dp", "expert"), "tensor"),
        P(("dp", "expert"), "tensor"),
        P(("dp", "expert"), "tensor", None, None),
        P(("dp", "expert"), "tensor", None, None),
        P(("dp", "expert"), None),
        P(("dp", "expert")),
        P("tensor", None),
        P(),
        P(("dp", "expert", "tensor"), None),
        P(("dp", "expert", "tensor"), None),
        P(),
        P(),
        P("expert", ("dp", "tensor"), None),
        P("expert", ("dp", "tensor"), None),
        P("expert", ("dp", "tensor"), None),
    )
    sizes = tuple(mesh.shape[name] for name in ("dp", "expert", "tensor"))
    return jax.shard_map(
        local_fast if sizes == (4, 2, 4) else local,
        mesh=mesh,
        in_specs=placed,
        out_specs=P(("dp", "expert", "tensor"), None),
        check_vma=False,
    )
```
